32 devices in a mesh: head: 2 (over x), blk: 16 (over z, y, core).
Axes of the slice: x: 2, y: 2, z: 4, core: 2. Of those that a mesh axis runs over, the one named last changes fastest.
Arguments:
- inputs: bfloat16 [4096, 2048], P(('head', 'blk')), may hold values from -6 to 6
- attn_norm_gain: bfloat16 [2048], P(('head', 'blk')), may hold values from 0.5 to 1.5
- attn_norm_bias: bfloat16 [2048], P(('head', 'blk')), may hold values from -1.25 to 1.25
- mlp_norm_gain: bfloat16 [2048], P(('head', 'blk')), may hold values from 0.5 to 1.5
- mlp_norm_bias: bfloat16 [2048], P(('head', 'blk')), may hold values from -1.25 to 1.25
- qkv_weight: bfloat16 [2048, 6144], P(('head', 'blk')), may hold values from -0.125 to 0.125
- qkv_bias: bfloat16 [6144], P(('head', 'blk')), may hold values from -1.25 to 1.25
- dense_weight: bfloat16 [2048, 2048], P(('head', 'blk')), may hold values from -2 to 2
- dense_bias: bfloat16 [2048], P(('head', 'blk')), may hold values from -1.25 to 1.25
- expand_weight: bfloat16 [2048, 8192], P(('head', 'blk')), may hold values from -0.125 to 0.125
- expand_bias: bfloat16 [8192], P(('head', 'blk')), may hold values from -1.25 to 1.25
- shrink_weight: bfloat16 [2048, 8192], P(('head', 'blk')), may hold values from -0.0625 to 0.0625
- shrink_bias: bfloat16 [2048], P(('head', 'blk')), may hold values from -1.25 to 1.25
- token_of_row: int32 [4096], replicated, may hold values from 0 to 4095, as said below
- cont_parent: int32 [8], replicated, may hold values from 0 to 0, as said below
- position_ids: int32 [4096], P(('head', 'blk')), may hold values from 0 to 2815, as said below
- cotangent: bfloat16 [4096, 2048], P(('head', 'blk')), may hold values from -12 to 12
Outputs:
- output: bfloat16 [4096, 2048], P(('head', 'blk'))
- input_grad: bfloat16 [4096, 2048], P(('head', 'blk'))
- attn_norm_gain_grad: float32 [2048], P(('head', 'blk'))
- attn_norm_bias_grad: float32 [2048], P(('head', 'blk'))
- mlp_norm_gain_grad: float32 [2048], P(('head', 'blk'))
- mlp_norm_bias_grad: float32 [2048], P(('head', 'blk'))
- qkv_weight_grad: float32 [2048, 6144], P(('head', 'blk'))
- qkv_bias_grad: float32 [4096], P(('head', 'blk'))
- value_bias_grad: float32 [2048], P(('head', 'blk'))
- dense_weight_grad: float32 [2048, 2048], P(('head', 'blk'))
- dense_bias_grad: float32 [2048], P(('head', 'blk'))
- expand_weight_grad: float32 [2048, 8192], P(('head', 'blk'))
- expand_bias_grad: float32 [8192], P(('head', 'blk'))
- shrink_weight_grad: float32 [2048, 8192], P(('head', 'blk'))
- shrink_bias_grad: float32 [2048], P(('head', 'blk'))
The draws below stay inside these ranges and needn't reach their ends.
Inputs may be any that keep to these rules, and one draw needn't show every extreme that they name: `token_of_row`: a permutation of the logical tokens; each aligned stripe of 16 logical tokens lies whole on one device, and each aligned run of 32 stripes puts one stripe on every device. `cont_parent`: each prompt is named by exactly 8 continuations. `position_ids`: a prompt token's position is its place in the prompt; the tokens of a continuation take 2048 + its gap + their place, with one gap of 0 to 512 for each continuation.
All inputs are finite; a program needn't handle non-finite values.
Results may differ from the reference program's by a relative error of at most 0.013.
Values may be sent and summed in bfloat16 or wider, within the bound.
A program may use at most 704 MiB of HBM per device.

```python
import math
import jax
import jax.numpy as jnp
from jax import lax

D = 2048
HEADS = 8
HEAD_DIM = 256
ROT = 64
FF = 8192
TOK_DEV = 128
PROMPT = 2048
CONT = 256
STRIPE = 16
GAP = 512
CPP = 8
SEQ = 4096
TOKENS = 4096
GROUPS = 1
CONTS = 8


def stripe_layout(key):
    key_rows = jax.random.fold_in(key, 5)
    key_first, key_second = jax.random.split(key_rows)
    device_total = TOKENS // TOK_DEV
    residue = jax.random.permutation(key_first, device_total)
    within = jax.vmap(lambda each_key: jax.random.permutation(each_key, TOK_DEV))(jax.random.split(key_second, device_total))
    stripe_id = within // STRIPE * device_total + residue[:, None]
    return (stripe_id * STRIPE + within % STRIPE).reshape(-1).astype(jnp.int32)


def draw_token_of_row(key, part):
    return stripe_layout(key)


def draw_cont_parent(key, part):
    key = jax.random.fold_in(key, 9)
    return (jax.random.permutation(key, CONTS) % GROUPS).astype(jnp.int32)


def draw_position_ids(key, part):
    token_ids = stripe_layout(key)
    key = jax.random.fold_in(key, 7)
    gap_sizes = jax.random.randint(key, (CONTS,), 0, GAP + 1).astype(jnp.int32).at[0].set(GAP)
    prompt_total = GROUPS * PROMPT
    is_prompt = token_ids < prompt_total
    offset = token_ids - prompt_total
    cont_id = jnp.clip(offset // CONT, 0, CONTS - 1)
    position = jnp.where(is_prompt, token_ids % PROMPT, PROMPT + gap_sizes[cont_id] + offset % CONT)
    return position.astype(jnp.int32)


def with_spikes(drawn, own_key, source, target, shards_of, factor):
    owner, partner = [(jnp.arange(drawn.shape[axis_at]) // (drawn.shape[axis_at] // shards_of)).reshape([-1 if axis == axis_at else 1 for axis in range(drawn.ndim)]) for axis_at in (source, target)]
    chosen = jax.random.permutation(own_key, shards_of)[partner]
    strong = (owner == chosen) | (owner == (partner + shards_of // 2) % shards_of)
    return jnp.where(strong, factor * drawn, drawn)


def shard_levels(rng, shape, pieces, low, high):
    def one(axis_at, parts):
        steps = jax.random.uniform(jax.random.fold_in(jax.random.fold_in(rng, 6), axis_at), (parts,), jnp.float32, low / len(pieces), high / len(pieces))
        return jnp.repeat(jnp.exp(steps), shape[axis_at] // parts).reshape((-1,) + (1,) * (len(shape) - axis_at - 1))

    factor_of = one(*pieces[0])
    for cut in pieces[1:]:
        factor_of = factor_of * one(*cut)
    return factor_of


def noise(rng, dims, scale, limit, cuts=(), kind=jnp.bfloat16):
    factor_of = shard_levels(rng, dims, cuts, -0.22, 0.18) if cuts else 1.0
    entries = jax.random.normal(rng, dims, jnp.float32) * scale * factor_of
    return jnp.minimum(jnp.maximum(entries, -limit), limit).astype(kind)


def gaussian_with(own_key, dims, deviation, bound, cuts, heavy, kind=jnp.bfloat16):
    values = deviation * jax.random.normal(own_key, dims, jnp.float32)
    if cuts:
        values = values * shard_levels(own_key, dims, cuts, -0.22, 0.18)
    return jnp.clip(with_spikes(values, jax.random.fold_in(own_key, 3), *heavy), -bound, bound).astype(kind)


def setup_inputs(seed: int = 0) -> dict:
    seeds = jax.random.split(jax.random.key(seed), 18)
    return {
        "inputs": noise(seeds[0], (TOKENS, D), 1.0, 6.0, ((0, 32),)),
        "attn_norm_gain": jnp.clip(1.0 + 0.1 * jax.random.normal(seeds[1], (D,), jnp.float32), 0.5, 1.5).astype(jnp.bfloat16),
        "attn_norm_bias": noise(seeds[2], (D,), 0.2, 1.25, ((0, 32),)),
        "mlp_norm_gain": jnp.clip(1.0 + 0.1 * jax.random.normal(seeds[3], (D,), jnp.float32), 0.5, 1.5).astype(jnp.bfloat16),
        "mlp_norm_bias": noise(seeds[4], (D,), 0.2, 1.25, ((0, 32),)),
        "qkv_weight": noise(seeds[5], (D, 3 * D), D ** -0.5, 0.125, ((0, 32),)),
        "qkv_bias": noise(seeds[6], (3 * D,), 0.2, 1.25, ((0, 32),)),
        "dense_weight": noise(seeds[7], (D, D), (max(D // 256, 1)) ** -0.5, 2.0, ((0, 32),)),
        "dense_bias": noise(seeds[8], (D,), 0.2, 1.25, ((0, 32),)),
        "expand_weight": noise(seeds[9], (D, FF), D ** -0.5, 0.125, ((0, 32),)),
        "expand_bias": noise(seeds[10], (FF,), 0.2, 1.25, ((0, 32),)),
        "shrink_weight": noise(seeds[11], (D, FF), FF ** -0.5, 0.0625, ((0, 32),)),
        "shrink_bias": noise(seeds[12], (D,), 0.2, 1.25, ((0, 32),)),
        "token_of_row": draw_token_of_row(jax.random.fold_in(seeds[17], 71), 0),
        "cont_parent": draw_cont_parent(jax.random.fold_in(seeds[17], 71), 0),
        "position_ids": draw_position_ids(jax.random.fold_in(seeds[17], 71), 0),
        "cotangent": gaussian_with(seeds[16], (TOKENS, D), 1.0, 12.0, ((0, 32),), (0, 1, 32, 2.75)),
    }


@jax.custom_vjp
def low(v):
    return lax.optimization_barrier(v.astype(jnp.bfloat16)).astype(jnp.float32)

@jax.custom_vjp
def low_back(v):
    return v

def low_keep(v):
    return (low(v), None)

def low_pass(kept, grad):
    return (grad,)

def back_keep(v):
    return (v, None)

def back_low(kept, grad):
    return (low(grad),)
low.defvjp(low_keep, low_pass)
low_back.defvjp(back_keep, back_low)

def layer_norm(values, gain, shift):
    average = lax.optimization_barrier(jnp.mean(values, -1, keepdims=True))
    centered = values - average
    spread = lax.optimization_barrier(jnp.mean(centered * centered, -1, keepdims=True))
    return centered * lax.rsqrt(spread + 1e-05) * gain + shift

def angles_of(positions):
    frequency = 10000.0 ** (-jnp.arange(0, ROT, 2, dtype=jnp.float32) / ROT)
    return positions.astype(jnp.float32)[:, None] * frequency[None, :]

def rotate(values, angles):
    half_rot = ROT // 2
    cosine = jnp.cos(angles)[:, None, :]
    sine_part = jnp.sin(angles)[:, None, :]
    leading = values[..., :half_rot]
    behind = values[..., half_rot:ROT]
    return jnp.concatenate([leading * cosine - behind * sine_part, behind * cosine + leading * sine_part, values[..., ROT:]], -1)

def attend(queries, keys, values):
    places = jnp.arange(SEQ, dtype=jnp.int32)
    is_prompt = places < PROMPT
    cont_id = jnp.where(is_prompt, -1, (places - PROMPT) // CONT)
    position = jnp.where(is_prompt, places, (places - PROMPT) % CONT)
    row_width = min(512, SEQ)
    score_scale = 1.0 / math.sqrt(HEAD_DIM)

    def one_block(first_row):
        query_block = lax.dynamic_slice_in_dim(queries, first_row, row_width, 0)
        rows_cont = lax.dynamic_slice_in_dim(cont_id, first_row, row_width, 0)
        rows_place = lax.dynamic_slice_in_dim(position, first_row, row_width, 0)
        rows_prompt = lax.dynamic_slice_in_dim(is_prompt, first_row, row_width, 0)
        earlier = position[None, :] <= rows_place[:, None]
        allowed = is_prompt[None, :] & (jnp.logical_not(rows_prompt)[:, None] | earlier) | (rows_cont[:, None] == cont_id[None, :]) & earlier
        scores = low_back(jnp.einsum('qhd,khd->hqk', query_block, keys, precision=lax.Precision.HIGHEST) * score_scale)
        scores = jnp.where(allowed[None], scores, -1e+30)
        row_peak = lax.optimization_barrier(jnp.max(scores, -1, keepdims=True))
        weights = jnp.where(allowed[None], jnp.exp(scores - row_peak), 0.0)
        probability = low(weights / lax.optimization_barrier(jnp.sum(weights, -1, keepdims=True)))
        return jnp.einsum('hqk,khd->qhd', probability, values, precision=lax.Precision.HIGHEST)
    starts = jnp.arange(SEQ // row_width, dtype=jnp.int32) * row_width
    blocks = lax.map(jax.checkpoint(one_block), starts)
    return blocks.reshape(SEQ, HEADS, HEAD_DIM)

def group_layer(states, params, positions):
    gain_one, shift_one, gain_two, shift_two, weight_qkv, bias_qkv, weight_dense, bias_dense, weight_expand, bias_expand, weight_shrink, bias_shrink = params
    norm_one = low(layer_norm(states, gain_one, shift_one))
    norm_two = low(layer_norm(states, gain_two, shift_two))
    mixed = low_back(jnp.dot(norm_one, weight_qkv, precision=lax.Precision.HIGHEST) + bias_qkv)
    mixed = mixed.reshape(SEQ, 3, HEADS, HEAD_DIM)
    angles = angles_of(positions)
    queries = low_back(low(rotate(mixed[:, 0], angles)))
    keys = low_back(low(rotate(mixed[:, 1], angles)))
    values = low_back(low(mixed[:, 2]))
    attended = low_back(low(attend(queries, keys, values))).reshape(SEQ, D)
    expanded = low_back(jnp.dot(norm_two, weight_expand, precision=lax.Precision.HIGHEST) + bias_expand)
    activated = low(jax.nn.gelu(expanded, approximate=False))
    branch_one = jnp.dot(attended, weight_dense.T, precision=lax.Precision.HIGHEST) + bias_dense
    branch_two = jnp.dot(activated, weight_shrink.T, precision=lax.Precision.HIGHEST) + bias_shrink
    return states + branch_one + branch_two

def reference(inputs, attn_norm_gain, attn_norm_bias, mlp_norm_gain, mlp_norm_bias, qkv_weight, qkv_bias, dense_weight, dense_bias, expand_weight, expand_bias, shrink_weight, shrink_bias, token_of_row, cont_parent, position_ids, cotangent):
    params = tuple((weight_item.astype(jnp.float32) for weight_item in (attn_norm_gain, attn_norm_bias, mlp_norm_gain, mlp_norm_bias, qkv_weight, qkv_bias, dense_weight, dense_bias, expand_weight, expand_bias, shrink_weight, shrink_bias)))
    states = inputs.astype(jnp.float32)
    row_of_token = jnp.zeros((TOKENS,), jnp.int32).at[token_of_row].set(jnp.arange(TOKENS, dtype=jnp.int32))
    cont_order = jnp.argsort(cont_parent, stable=True).astype(jnp.int32)
    prompt_tokens = jnp.arange(GROUPS * PROMPT, dtype=jnp.int32).reshape(GROUPS, PROMPT)
    cont_tokens = GROUPS * PROMPT + cont_order.reshape(GROUPS, CPP)[:, :, None] * CONT + jnp.arange(CONT, dtype=jnp.int32)[None, None, :]
    group_tokens = jnp.concatenate([prompt_tokens, cont_tokens.reshape(GROUPS, CPP * CONT)], 1)
    group_rows = row_of_token[group_tokens]

    def forward(states_in, params_in):

        def one_group(running, row_ids):
            result = jax.checkpoint(group_layer)(states_in[row_ids], params_in, position_ids[row_ids])
            return (running, result)
        running, stacked = lax.scan(one_group, jnp.zeros((), jnp.float32), group_rows)
        return jnp.zeros((TOKENS, D), jnp.float32).at[group_rows.reshape(-1)].set(stacked.reshape(TOKENS, D))
    output, pullback = jax.vjp(forward, states, params)
    gradients = pullback(cotangent.astype(jnp.float32))
    param_grads = gradients[1]
    return (output.astype(jnp.bfloat16), gradients[0].astype(jnp.bfloat16), param_grads[0], param_grads[1], param_grads[2], param_grads[3], param_grads[4], param_grads[5][:2 * D], param_grads[5][2 * D:], param_grads[6], param_grads[7], param_grads[8], param_grads[9], param_grads[10], param_grads[11])
```

```python
import functools
import math

import jax
import jax.numpy as jnp
from jax import lax
from jax.experimental import pallas as pl
from jax.experimental.pallas import tpu as pltpu
from jax.sharding import PartitionSpec as P

HEADS = 8
HEAD_DIM = 256
ROT = 64
PROMPT = 2048
CONT = 256
STRIPE = 16
MESH = pl.DeviceIdType.MESH
BF = jnp.bfloat16
F32 = jnp.float32
ANY = pl.BlockSpec(memory_space=pl.ANY)
VMEM = pl.BlockSpec(memory_space=pltpu.VMEM)
DMA = pltpu.SemaphoreType.DMA


class Place:
    def __init__(self, ways):
        self.ways = ways
        self.x = lax.axis_index("head")
        b = lax.axis_index("blk")
        self.c = b % 2
        self.h = (b // 2) % HEADS
        self.w = b // (2 * HEADS)
        self.hy = self.h % 2
        self.hz = self.h // 2

    def device(self, x=None, w=None, h=None, c=None):
        x = self.x if x is None else x
        w = self.w if w is None else w
        h = self.h if h is None else h
        c = self.c if c is None else c
        return (x, w * (2 * HEADS) + h * 2 + c)

    def peers_h(self):
        return [self.device(h=(self.h + k) % HEADS) for k in range(1, HEADS)]

    def peers_w(self):
        return [self.device(w=(self.w + k) % self.ways) for k in range(1, self.ways)]

    def peer_x(self):
        return self.device(x=1 - self.x)

    def peer_c(self):
        return self.device(c=1 - self.c)

    def peer_y(self):
        return self.device(h=self.h + 1 - 2 * self.hy)


def greet(devices):
    barrier = pltpu.get_barrier_semaphore()
    for one in devices:
        pl.semaphore_signal(barrier, inc=1, device_id=one, device_id_type=MESH)
    pl.semaphore_wait(barrier, len(devices))


def remote(src, dst, send, recv, device):
    return pltpu.make_async_remote_copy(
        src_ref=src, dst_ref=dst, send_sem=send, recv_sem=recv, device_id=device, device_id_type=MESH
    )


def call(body, out_shape, ins, scratch, ident, out_spec=ANY, in_spec=ANY):
    return pl.pallas_call(
        body,
        out_shape=out_shape,
        in_specs=[in_spec] * len(ins),
        out_specs=jax.tree.map(lambda _: out_spec, out_shape),
        scratch_shapes=scratch,
        compiler_params=pltpu.CompilerParams(
            collective_id=ident, has_side_effects=True, vmem_limit_bytes=60 * 2**20
        ),
    )(*ins)


LINE = HEADS // 2


def spread_rows(place, own, full, up, down, side, recv):
    hz, hy = place.hz, place.hy

    def piece(src, z, target, send):
        idx = z * 2 + hy
        return remote(src, full.at[:, idx], send, recv.at[idx], target)

    def up_to():
        return place.device(h=place.h + 2)

    def down_to():
        return place.device(h=place.h - 2)

    def first():
        @pl.when(hz < LINE - 1)
        def _():
            piece(own, hz, up_to(), up.at[0]).start()

        @pl.when(hz > 0)
        def _():
            piece(own, hz, down_to(), down.at[0]).start()

        piece(own, hz, place.peer_y(), side.at[0]).start()

    def arrived(idx):
        remote(full.at[:, idx], full.at[:, idx], side.at[0], recv.at[idx], place.peer_y()).wait_recv()

    def step(s):
        low, high = hz - s - 1, hz + s + 1

        @pl.when(low >= 0)
        def _():
            arrived(low * 2 + hy)
            src = full.at[:, low * 2 + hy]

            @pl.when(hz < LINE - 1)
            def _():
                piece(src, low, up_to(), up.at[s + 1]).start()

            piece(src, low, place.peer_y(), side.at[low + 1]).start()

        @pl.when(high < LINE)
        def _():
            arrived(high * 2 + hy)
            src = full.at[:, high * 2 + hy]

            @pl.when(hz > 0)
            def _():
                piece(src, high, down_to(), down.at[s + 1]).start()

            piece(src, high, place.peer_y(), side.at[high + 1]).start()

    def finish():
        for z in range(LINE):
            arrived(z * 2 + 1 - hy)

    def sent():
        piece(own, hz, place.peer_y(), side.at[0]).wait_send()
        for z in range(LINE):
            @pl.when(z != hz)
            def _():
                piece(own, z, place.peer_y(), side.at[z + 1]).wait_send()
        for s in range(LINE - 1):
            @pl.when((hz < LINE - 1) & (hz - s >= 0))
            def _():
                piece(own, hz, up_to(), up.at[s]).wait_send()

            @pl.when((hz > 0) & (hz + s < LINE))
            def _():
                piece(own, hz, down_to(), down.at[s]).wait_send()

    return first, step, finish, sent


def gather_kernel(ways, n_in, g_in, w_in, m_in, n_all, g_all, w_all, m_all,
                  local, nu, nd, ns, nr, gu, gd, gs, gr, wa, wx, wc, wr, ma, mx, mc, mr):
    place = Place(ways)
    x, w, h, c = place.x, place.w, place.h, place.c
    stage_a = [(dw, dh) for dw in range(ways) for dh in range(HEADS) if (dw, dh) != (0, 0)]
    greet(
        [place.device(w=(w + dw) % ways, h=(h + dh) % HEADS) for dw, dh in stage_a]
        + [place.peer_x(), place.peer_c()]
    )
    n_first, n_step, n_finish, n_sent = spread_rows(place, n_in, n_all, nu, nd, ns, nr)
    g_first, g_step, g_finish, g_sent = spread_rows(place, g_in, g_all, gu, gd, gs, gr)
    copies = [
        pltpu.make_async_copy(n_in, n_all.at[:, h], local.at[0]),
        pltpu.make_async_copy(g_in, g_all.at[:, h], local.at[1]),
        pltpu.make_async_copy(w_in.at[h], w_all.at[x, w, h, c], local.at[2]),
        pltpu.make_async_copy(m_in.at[h], m_all.at[x, w, h, c], local.at[3]),
    ]
    n_first()
    sends = []

    def send(src, dst, s, r, device):
        copy = remote(src, dst, s, r, device)
        copy.start()
        sends.append(copy)

    pairs = ((w_all, wa, wx, wc, wr), (m_all, ma, mx, mc, mr))
    for k, (dw, dh) in enumerate(stage_a):
        h2 = (h + dh) % HEADS
        target = place.device(w=(w + dw) % ways, h=h2)
        send(w_in.at[h2], w_all.at[x, w, h, c], wa.at[k], wr.at[x, w, h, c], target)
        send(m_in.at[h2], m_all.at[x, w, h, c], ma.at[k], mr.at[x, w, h, c], target)
    send(w_in.at[h], w_all.at[x, w, h, c], wx.at[w, h], wr.at[x, w, h, c], place.peer_x())
    send(m_in.at[h], m_all.at[x, w, h, c], mx.at[w, h], mr.at[x, w, h, c], place.peer_x())
    send(w_in.at[h], w_all.at[x, w, h, c], wc.at[x, w, h], wr.at[x, w, h, c], place.peer_c())
    send(m_in.at[h], m_all.at[x, w, h, c], mc.at[x, w, h], mr.at[x, w, h, c], place.peer_c())
    g_first()
    for copy in copies:
        copy.start()

    def arrived(full, recv, xs, ws, hs, cs):
        place_ref = full.at[xs, ws, hs, cs]
        remote(place_ref, place_ref, local.at[0], recv.at[xs, ws, hs, cs], place.peer_x()).wait_recv()

    for s in range(LINE - 1):
        n_step(s)
    for dw, dh in stage_a:
        ws, hs = (w - dw) % ways, (h - dh) % HEADS
        for full, _, to_x, to_c, recv in pairs:
            arrived(full, recv, x, ws, hs, c)
            block = full.at[x, ws, hs, c]
            send(block, block, to_x.at[ws, hs], recv.at[x, ws, hs, c], place.peer_x())
            send(block, block, to_c.at[x, ws, hs], recv.at[x, ws, hs, c], place.peer_c())
    for s in range(LINE - 1):
        g_step(s)
    for dw, dh in [(0, 0)] + stage_a:
        ws, hs = (w - dw) % ways, (h - dh) % HEADS
        for full, _, _, to_c, recv in pairs:
            arrived(full, recv, 1 - x, ws, hs, c)
            block = full.at[1 - x, ws, hs, c]
            send(block, block, to_c.at[1 - x, ws, hs], recv.at[1 - x, ws, hs, c], place.peer_c())
    n_finish()
    g_finish()
    for dw, dh in [(0, 0)] + stage_a:
        ws, hs = (w - dw) % ways, (h - dh) % HEADS
        for full, _, _, _, recv in pairs:
            for xs in (x, 1 - x):
                arrived(full, recv, xs, ws, hs, 1 - c)
    for copy in copies:
        copy.wait()
    for copy in sends:
        copy.wait_send()
    n_sent()
    g_sent()


def gather_all(ways, normed, grads, weights, notes):
    runs, _, width = normed.shape
    _, rows, columns = weights.shape
    blocks = (2, ways, HEADS, 2)
    shapes = (
        jax.ShapeDtypeStruct((runs, HEADS, STRIPE, width), BF),
        jax.ShapeDtypeStruct((runs, HEADS, STRIPE, width), BF),
        jax.ShapeDtypeStruct(blocks + (rows, columns), BF),
        jax.ShapeDtypeStruct(blocks + notes.shape[1:], F32),
    )
    row_sems = [DMA((LINE,)), DMA((LINE,)), DMA((LINE + 1,)), DMA((HEADS,))]
    block_sems = [DMA((ways * HEADS,)), DMA((ways, HEADS)), DMA((2, ways, HEADS)), DMA(blocks)]
    return call(
        functools.partial(gather_kernel, ways),
        shapes,
        (normed, grads, weights, notes),
        [DMA((4,))] + row_sems + row_sems + block_sems + block_sems,
        0,
    )


def exchange_kernel(ways, own, full, local, to_w, to_x, to_c, recv):
    place = Place(ways)
    x, w, c = place.x, place.w, place.c
    runs = own.shape[0]
    parts = 4
    span = runs // parts
    greet(place.peers_w() + [place.peer_x(), place.peer_c()])

    def spot(ws, xs, cs, p):
        return full.at[pl.ds(p * span, span), ws * 4 + xs * 2 + cs]

    sends = []

    def send(src, ws, xs, cs, p, sem, device):
        copy = remote(src, spot(ws, xs, cs, p), sem, recv.at[ws, xs, cs, p], device)
        copy.start()
        sends.append(copy)

    def arrived(ws, xs, cs, p):
        remote(spot(ws, xs, cs, p), spot(ws, xs, cs, p), local.at[0], recv.at[ws, xs, cs, p], place.peer_x()).wait_recv()

    keep = pltpu.make_async_copy(own, full.at[:, w * 4 + x * 2 + c], local.at[0])
    for p in range(parts):
        src = own.at[pl.ds(p * span, span)]
        for k, device in enumerate(place.peers_w()):
            send(src, w, x, c, p, to_w.at[k, p], device)
        send(src, w, x, c, p, to_x.at[w, p], place.peer_x())
    for p in range(parts):
        send(own.at[pl.ds(p * span, span)], w, x, c, p, to_c.at[w, x, p], place.peer_c())
    keep.start()
    for k in range(1, ways):
        ws = (w - k) % ways
        for p in range(parts):
            arrived(ws, x, c, p)
            send(spot(ws, x, c, p), ws, x, c, p, to_x.at[ws, p], place.peer_x())
            send(spot(ws, x, c, p), ws, x, c, p, to_c.at[ws, x, p], place.peer_c())
    for k in range(ways):
        ws = (w - k) % ways
        for p in range(parts):
            arrived(ws, 1 - x, c, p)
            send(spot(ws, 1 - x, c, p), ws, 1 - x, c, p, to_c.at[ws, 1 - x, p], place.peer_c())
    for k in range(ways):
        ws = (w - k) % ways
        for p in range(parts):
            arrived(ws, x, 1 - c, p)
            arrived(ws, 1 - x, 1 - c, p)
    keep.wait()
    for copy in sends:
        copy.wait_send()


def exchange(ways, own):
    runs, rows, columns = own.shape
    return call(
        functools.partial(exchange_kernel, ways),
        jax.ShapeDtypeStruct((runs, 4 * ways, rows, columns), BF),
        (own,),
        [DMA((1,)), DMA((ways, 4)), DMA((ways, 4)), DMA((ways, 2, 4)), DMA((ways, 2, 2, 4))],
        1,
    )


def fold_kernel(ways, part, total, from_c, from_x, from_w, s_c, r_c, s_x, r_x, s_w, r_w):
    place = Place(ways)
    x, w, c = place.x, place.w, place.c
    runs = part.shape[0]
    greet(place.peers_w() + [place.peer_x(), place.peer_c()])

    def slot(ws, xs, cs):
        return ws * 4 + xs * 2 + cs

    sends = []

    def send(src, dst, s, r, device):
        copy = remote(src, dst, s, r, device)
        copy.start()
        sends.append(copy)
        return copy

    order = [(w + k) % ways for k in range(1, ways)] + [w]
    first = []
    for i, ws in enumerate(order):
        for xs, k in ((1 - x, 0), (x, 1)):
            first.append(
                send(part.at[:, slot(ws, xs, 1 - c)], from_c.at[:, i, k], s_c.at[i, k], r_c.at[i, k], place.peer_c())
            )

    def add(i, k, ws, xs, extra):
        @pl.loop(0, runs)
        def _(run):
            value = part[run, slot(ws, xs, c)].astype(F32) + from_c[run, i, k].astype(F32)
            if extra:
                value = value + from_x[run, i].astype(F32)
            if extra and i == ways - 1:
                for q in range(ways - 1):
                    value = value + from_w[run, q].astype(F32)
                total[run] = value
            else:
                from_c[run, i, k] = value.astype(BF)

    for i, ws in enumerate(order):
        first[2 * i].wait_recv()
        add(i, 0, ws, 1 - x, False)
        send(from_c.at[:, i, 0], from_x.at[:, i], s_x.at[i], r_x.at[i], place.peer_x())
    for i, ws in enumerate(order):
        first[2 * i + 1].wait_recv()
        remote(from_x.at[:, i], from_x.at[:, i], s_x.at[i], r_x.at[i], place.peer_x()).wait_recv()
        if i == ways - 1:
            for q in range(ways - 1):
                remote(from_w.at[:, q], from_w.at[:, q], s_w.at[q], r_w.at[q], place.peer_x()).wait_recv()
        add(i, 1, ws, x, True)
        if i < ways - 1:
            send(from_c.at[:, i, 1], from_w.at[:, i], s_w.at[i], r_w.at[i], place.device(w=ws))
    for copy in sends:
        copy.wait_send()


def fold(ways, part):
    runs, _, rows, columns = part.shape
    extra = max(ways - 1, 1)
    return call(
        functools.partial(fold_kernel, ways),
        jax.ShapeDtypeStruct((runs, rows, columns), F32),
        (part,),
        [
            pltpu.VMEM((runs, ways, 2, rows, columns), BF),
            pltpu.VMEM((runs, ways, rows, columns), BF),
            pltpu.VMEM((runs, extra, rows, columns), BF),
            DMA((ways, 2)), DMA((ways, 2)), DMA((ways,)), DMA((ways,)), DMA((extra,)), DMA((extra,)),
        ],
        2,
        VMEM,
        VMEM,
    )


def collect_kernel(ways, part, total, from_y, from_z, s_y, r_y, s_z, r_z):
    place = Place(ways)
    hz, hy = place.hz, place.hy
    runs = part.shape[0]
    others = [(hz + k) % LINE for k in range(1, LINE)]
    greet([place.peer_y()] + [place.device(h=z * 2 + hy) for z in others])
    order = others + [hz]
    sends, first = [], []
    for i, z in enumerate(order):
        copy = remote(part.at[:, z * 2 + 1 - hy], from_y.at[:, i], s_y.at[i], r_y.at[i], place.peer_y())
        copy.start()
        sends.append(copy)
    for i, z in enumerate(order):
        sends[i].wait_recv()
        if i < LINE - 1:
            @pl.loop(0, runs)
            def _(run):
                value = part[run, z * 2 + hy].astype(F32) + from_y[run, i].astype(F32)
                from_y[run, i] = value.astype(BF)

            copy = remote(from_y.at[:, i], from_z.at[:, i], s_z.at[i], r_z.at[i], place.device(h=z * 2 + hy))
            copy.start()
            first.append(copy)
    for copy in first:
        copy.wait_recv()

    @pl.loop(0, runs)
    def _(run):
        value = part[run, hz * 2 + hy].astype(F32) + from_y[run, LINE - 1].astype(F32)
        for i in range(LINE - 1):
            value = value + from_z[run, i].astype(F32)
        total[run] = value

    for copy in sends + first:
        copy.wait_send()


def collect(ways, part, ident):
    runs, _, rows, width = part.shape
    return call(
        functools.partial(collect_kernel, ways),
        jax.ShapeDtypeStruct((runs, rows, width), F32),
        (part,),
        [
            pltpu.VMEM((runs, LINE, rows, width), BF),
            pltpu.VMEM((runs, LINE - 1, rows, width), BF),
            DMA((LINE,)), DMA((LINE,)), DMA((LINE - 1,)), DMA((LINE - 1,)),
        ],
        ident,
        VMEM,
        VMEM,
    )


def owners_kernel(ways, part, note, out, note_out, from_c, from_x, from_w, note_c, note_x, note_w,
                  local, s_c, r_c, s_x, r_x, s_w, r_w, s_h, r_h, ns_c, nr_c, ns_x, nr_x, ns_w, nr_w, ns_h, nr_h):
    place = Place(ways)
    x, w, h, c = place.x, place.w, place.h, place.c
    rows = part.shape[4]
    piece = min(rows, 16)
    greet(place.peers_h() + place.peers_w() + [place.peer_x(), place.peer_c()])
    order = [(dw, dh) for dh in list(range(1, HEADS)) + [0] for dw in list(range(1, ways)) + [0]]
    sends = []

    def send(src, dst, s, r, device):
        copy = remote(src, dst, s, r, device)
        copy.start()
        sends.append(copy)
        return copy

    def both(src, nsrc, dst, ndst, s, ns, r, nr, device):
        return send(src, dst, s, r, device), send(nsrc, ndst, ns, nr, device)

    first = {}
    for k, xs in ((0, 1 - x), (1, x)):
        for dw, dh in order:
            ws, hs = (w + dw) % ways, (h + dh) % HEADS
            first[k, dw, dh] = both(
                part.at[xs, ws, hs, 1 - c], note.at[xs, ws, hs, 1 - c],
                from_c.at[k, dw, dh], note_c.at[k, dw, dh],
                s_c.at[k, dw, dh], ns_c.at[k, dw, dh], r_c.at[k, dw, dh], nr_c.at[k, dw, dh], place.peer_c(),
            )

    def add(k, dw, dh, xs, more):
        ws, hs = (w + dw) % ways, (h + dh) % HEADS

        @pl.loop(0, rows // piece)
        def _(q):
            at = pl.ds(pl.multiple_of(q * piece, piece), piece)
            value = part[xs, ws, hs, c, at].astype(F32) + from_c[k, dw, dh, at].astype(F32)
            for ref in more:
                value = value + ref[at].astype(F32)
            from_c[k, dw, dh, at] = value.astype(BF)

    second = {}
    for dw, dh in order:
        ws, hs = (w + dw) % ways, (h + dh) % HEADS
        for copy in first[0, dw, dh]:
            copy.wait_recv()
        add(0, dw, dh, 1 - x, [])
        note_c[0, dw, dh] = note_c[0, dw, dh] + note[1 - x, ws, hs, c]
        second[dw, dh] = both(
            from_c.at[0, dw, dh], note_c.at[0, dw, dh], from_x.at[dw, dh], note_x.at[dw, dh],
            s_x.at[dw, dh], ns_x.at[dw, dh], r_x.at[dw, dh], nr_x.at[dw, dh], place.peer_x(),
        )
    third = {}
    last = []
    for dw, dh in order:
        ws, hs = (w + dw) % ways, (h + dh) % HEADS
        for copy in first[1, dw, dh] + second[dw, dh]:
            copy.wait_recv()
        more = [from_x.at[dw, dh]]
        summed = note_c[1, dw, dh] + note[x, ws, hs, c] + note_x[dw, dh]
        if dw == 0:
            for dv in range(1, ways):
                for copy in third[dv, dh]:
                    copy.wait_recv()
                more.append(from_w.at[dv - 1, dh])
                summed = summed + note_w[dv - 1, dh]
        add(1, dw, dh, x, more)
        note_c[1, dw, dh] = summed
        if dw != 0:
            third[dw, dh] = both(
                from_c.at[1, dw, dh], note_c.at[1, dw, dh], from_w.at[dw - 1, dh], note_w.at[dw - 1, dh],
                s_w.at[dw - 1, dh], ns_w.at[dw - 1, dh], r_w.at[dw - 1, dh], nr_w.at[dw - 1, dh], place.device(w=ws),
            )
        elif dh != 0:
            last.append(both(
                from_c.at[1, 0, dh], note_c.at[1, 0, dh], out.at[h], note_out.at[h],
                s_h.at[dh], ns_h.at[dh], r_h.at[h], nr_h.at[h], place.device(h=hs),
            ))
        else:
            keep = [
                pltpu.make_async_copy(from_c.at[1, 0, 0], out.at[h], local.at[0]),
                pltpu.make_async_copy(note_c.at[1, 0, 0], note_out.at[h], local.at[1]),
            ]
            for copy in keep:
                copy.start()
    for dh in range(1, HEADS):
        hs = (h - dh) % HEADS
        remote(out.at[hs], out.at[hs], s_h.at[0], r_h.at[hs], place.peer_x()).wait_recv()
        remote(note_out.at[hs], note_out.at[hs], ns_h.at[0], nr_h.at[hs], place.peer_x()).wait_recv()
    for copy in keep:
        copy.wait()
    for copy in sends:
        copy.wait_send()


def to_owners(ways, part, note):
    rows, columns = part.shape[4:]
    extra = max(ways - 1, 1)

    def sems():
        return [
            DMA((2, ways, HEADS)), DMA((2, ways, HEADS)), DMA((ways, HEADS)), DMA((ways, HEADS)),
            DMA((extra, HEADS)), DMA((extra, HEADS)), DMA((HEADS,)), DMA((HEADS,)),
        ]

    def slots(shape, kind):
        return [
            pltpu.VMEM((2, ways, HEADS) + shape, kind),
            pltpu.VMEM((ways, HEADS) + shape, kind),
            pltpu.VMEM((extra, HEADS) + shape if ways > 1 else (1, 1) + shape, kind),
        ]

    return call(
        functools.partial(owners_kernel, ways),
        (
            jax.ShapeDtypeStruct((HEADS, rows, columns), BF),
            jax.ShapeDtypeStruct((HEADS,) + note.shape[4:], F32),
        ),
        (part, note),
        slots((rows, columns), BF) + slots(note.shape[4:], F32) + [DMA((2,))] + sems() + sems(),
        5,
        VMEM,
        VMEM,
    )


def attention_kernel(prompt_runs, one_prompt, q_ref, do_ref, k_ref, v_ref, row_ref, col_ref,
                     o_ref, dq_ref, dk_ref, dv_ref, s_ref):
    runs, m, _ = q_ref.shape
    keys = k_ref.shape[1]
    by_rows = (((1,), (1,)), ((), ()))
    by_tokens = (((0,), (0,)), ((), ()))

    def dot(a, b, dims):
        return lax.dot_general(a, b, dims, preferred_element_type=F32)

    def mask(i, k):
        rows, cols = row_ref[i], col_ref[k]
        if isinstance(i, int) and isinstance(k, int) and i == k:
            return (rows[:, 1:2] == cols[1:2, :]) & (cols[0:1, :] <= rows[:, 0:1])
        if one_prompt:
            return None
        return rows[:, 2:3] == cols[2:3, :]

    for i in range(runs):
        pieces = list(range(min(i + 1, prompt_runs))) + ([i] if i >= prompt_runs else [])
        q = q_ref[i]
        peak = None
        for at, k in enumerate(pieces):
            s = dot(q, k_ref[k], by_rows)
            keep = mask(i, k)
            if keep is not None:
                s = jnp.where(keep, s, -1e30)
            s_ref[:, at * keys : (at + 1) * keys] = s
            top = jnp.max(s, -1, keepdims=True)
            peak = top if peak is None else jnp.maximum(peak, top)
        total = jnp.zeros((m, 1), F32)
        out = jnp.zeros((m, HEAD_DIM), F32)
        for at, k in enumerate(pieces):
            s = s_ref[:, at * keys : (at + 1) * keys]
            p = jnp.exp(s - peak)
            keep = mask(i, k)
            if keep is not None:
                p = jnp.where(keep, p, 0.0)
            s_ref[:, at * keys : (at + 1) * keys] = p
            total = total + jnp.sum(p, -1, keepdims=True)
            out = out + dot(p.astype(BF), v_ref[k], (((1,), (0,)), ((), ())))
        inverse = 1.0 / total
        out = out * inverse
        o_ref[i] = out.astype(BF)
        do = do_ref[i]
        delta = jnp.sum(out * do.astype(F32), -1, keepdims=True)
        dq = jnp.zeros((m, HEAD_DIM), F32)
        for at, k in enumerate(pieces):
            p = s_ref[:, at * keys : (at + 1) * keys] * inverse
            dp = dot(do, v_ref[k], by_rows)
            ds = (p * (dp - delta)).astype(BF)
            dq = dq + dot(ds, k_ref[k], (((1,), (0,)), ((), ())))
            dk = dot(ds, q, by_tokens)
            dv = dot(p.astype(BF), do, by_tokens)
            if i == k:
                dk_ref[k] = dk
                dv_ref[k] = dv
            else:
                dk_ref[k] = dk_ref[k] + dk
                dv_ref[k] = dv_ref[k] + dv
        dq_ref[i] = dq * (1.0 / math.sqrt(HEAD_DIM))


def attention(prompt_runs, one_prompt, queries, d_out, keys, values, row_meta, col_meta):
    runs, m, _ = queries.shape
    count = keys.shape[1]
    return pl.pallas_call(
        functools.partial(attention_kernel, prompt_runs, one_prompt),
        out_shape=(
            jax.ShapeDtypeStruct(queries.shape, BF),
            jax.ShapeDtypeStruct(queries.shape, F32),
            jax.ShapeDtypeStruct(keys.shape, F32),
            jax.ShapeDtypeStruct(keys.shape, F32),
        ),
        in_specs=[VMEM] * 6,
        out_specs=(VMEM,) * 4,
        scratch_shapes=[pltpu.VMEM((m, (prompt_runs + 1) * count), F32)],
        compiler_params=pltpu.CompilerParams(vmem_limit_bytes=60 * 2**20),
    )(queries, d_out, keys, values, row_meta, col_meta)


def angles_of(positions):
    frequency = 10000.0 ** (-jnp.arange(0, ROT, 2, dtype=F32) / ROT)
    return positions.astype(F32)[:, None] * frequency[None, :]


def rotate(values, cosine, sine):
    half = ROT // 2
    leading, behind = values[:, :half], values[:, half:ROT]
    return jnp.concatenate(
        [leading * cosine - behind * sine, behind * cosine + leading * sine, values[:, ROT:]], -1
    )


def per_device(
    inputs, attn_norm_gain, attn_norm_bias, mlp_norm_gain, mlp_norm_bias, qkv_weight, qkv_bias, dense_weight,
    dense_bias, expand_weight, expand_bias, shrink_weight, shrink_bias, token_of_row, cont_parent, position_ids,
    cotangent,
):
    heads, blocks = lax.axis_size("head"), lax.axis_size("blk")
    devices = heads * blocks
    ways = blocks // (2 * HEADS)
    assert heads == 2 and blocks == ways * 2 * HEADS
    x = lax.axis_index("head")
    b = lax.axis_index("blk")
    me = x * blocks + b
    c, h, w = b % 2, (b // 2) % HEADS, b // (2 * HEADS)
    tok_dev, width = inputs.shape
    rows = qkv_weight.shape[0]
    hidden = expand_weight.shape[1] // HEADS
    runs = tok_dev // STRIPE
    run_size = devices * STRIPE
    prompt_total = token_of_row.shape[0] - cont_parent.shape[0] * CONT
    prompt_runs = prompt_total // run_size
    one_prompt = prompt_total == PROMPT
    assert prompt_runs * run_size == prompt_total
    group_rows = runs * HEADS * STRIPE
    head3 = 3 * HEAD_DIM
    block_columns = head3 + hidden

    by_device = token_of_row.reshape(devices, tok_dev)
    run_of = by_device // run_size
    big = jnp.int32(2**30)
    each_run = jnp.arange(runs, dtype=jnp.int32)
    base = jnp.min(jnp.where(run_of[:, :, None] == each_run, by_device[:, :, None], big), 1)
    mine = lax.dynamic_index_in_dim(by_device, me, 0, False)
    sorted_at = mine // run_size * STRIPE + mine % STRIPE
    pick = (sorted_at[None, :] == jnp.arange(tok_dev, dtype=jnp.int32)[:, None]).astype(BF)
    base_position = jnp.min(
        jnp.where((mine // run_size)[:, None] == each_run, position_ids[:, None], big), 0
    )

    def ordered(rows_in):
        return jnp.dot(pick, rows_in, preferred_element_type=F32).astype(BF)

    def restored(rows_in):
        return lax.dot_general(pick, rows_in, (((0,), (0,)), ((), ())), preferred_element_type=F32).astype(BF)

    states = ordered(inputs).astype(F32)
    grad_low = ordered(cotangent)
    grad_out = grad_low.astype(F32)
    average = jnp.mean(states, -1, keepdims=True)
    centered = states - average
    inverse_spread = lax.rsqrt(jnp.mean(centered * centered, -1, keepdims=True) + 1e-05)
    normed = centered * inverse_spread
    normed_low = normed.astype(BF)

    gain_one, shift_one = attn_norm_gain.astype(F32), attn_norm_bias.astype(F32)
    gain_two, shift_two = mlp_norm_gain.astype(F32), mlp_norm_bias.astype(F32)
    qkv_wide, expand_wide = qkv_weight.astype(F32), expand_weight.astype(F32)

    def split_qkv(values):
        return values.reshape(-1, 3, HEADS, HEAD_DIM).transpose(2, 0, 1, 3).reshape(HEADS, -1, head3)

    def split(values):
        return values.reshape(values.shape[0], HEADS, -1).transpose(1, 0, 2)

    weights = jnp.concatenate(
        [
            split_qkv((qkv_wide * gain_one[:, None]).astype(BF)),
            split((expand_wide * gain_two[:, None]).astype(BF)),
            split(dense_weight),
            split(shrink_weight),
        ],
        -1,
    )
    own_qkv_bias = lax.dynamic_update_slice_in_dim(
        jnp.zeros((3 * width,), F32), qkv_bias.astype(F32), me * qkv_bias.shape[0], 0
    )
    own_expand_bias = lax.dynamic_update_slice_in_dim(
        jnp.zeros((HEADS * hidden,), F32), expand_bias.astype(F32), me * expand_bias.shape[0], 0
    )
    bias_parts = jnp.concatenate(
        [
            split_qkv((jnp.sum(qkv_wide * shift_one[:, None], 0) + own_qkv_bias)[None])[:, 0],
            split((jnp.sum(expand_wide * shift_two[:, None], 0) + own_expand_bias)[None])[:, 0],
        ],
        -1,
    )
    lanes = 128
    note_rows = block_columns // lanes

    def padded(values):
        return jnp.pad(values, (0, lanes - values.shape[0]))

    tail = jnp.stack([padded(dense_bias.astype(F32) + shrink_bias.astype(F32)), padded(base_position.astype(F32))])
    notes = jnp.concatenate(
        [bias_parts.reshape(HEADS, note_rows, lanes), jnp.broadcast_to(tail[None], (HEADS, 2, lanes))], 1
    )

    n_all, g_all, w_all, m_all = gather_all(
        ways, normed_low.reshape(runs, STRIPE, width), grad_low.reshape(runs, STRIPE, width), weights, notes
    )
    n_all = n_all.reshape(group_rows, width)
    g_all = g_all.reshape(group_rows, width)
    w_all = w_all.reshape(width, block_columns + HEAD_DIM + hidden)
    bias_block = jnp.sum(m_all[..., :note_rows, :], (0, 1, 2, 3)).reshape(block_columns)
    out_bias = m_all[..., note_rows, :rows].reshape(width)
    group_position = lax.dynamic_index_in_dim(m_all[:, :, :, :, note_rows + 1, :runs], x, 0, False)
    group_position = lax.dynamic_index_in_dim(group_position, w, 0, False)
    group_position = lax.dynamic_index_in_dim(group_position, c, 1, False)
    within = jnp.arange(STRIPE, dtype=jnp.int32)
    position = (group_position.T[:, :, None] + within.astype(F32)).reshape(group_rows)
    angles = angles_of(position)
    cosine, sine = jnp.cos(angles), jnp.sin(angles)

    w_in = w_all[:, :block_columns]
    w_out = w_all[:, block_columns:]
    mixed = jnp.dot(n_all, w_in[:, :head3], preferred_element_type=F32) + bias_block[:head3]
    queries = (rotate(mixed[:, :HEAD_DIM], cosine, sine) * (1.0 / math.sqrt(HEAD_DIM))).astype(BF)
    keys = rotate(mixed[:, HEAD_DIM : 2 * HEAD_DIM], cosine, sine).astype(BF)
    values = mixed[:, 2 * HEAD_DIM :].astype(BF)
    rows_run = group_rows // runs
    pairs = exchange(ways, jnp.concatenate([keys, values], 1).reshape(runs, rows_run, 2 * HEAD_DIM))
    pairs = pairs.reshape(runs, run_size, 2 * HEAD_DIM)

    d_attended = jnp.dot(g_all, w_out[:, :HEAD_DIM], preferred_element_type=F32).astype(BF)
    expanded = jnp.dot(n_all, w_in[:, head3:], preferred_element_type=F32) + bias_block[head3:]
    activated, gelu_back = jax.vjp(lambda v: jax.nn.gelu(v, approximate=False), expanded)
    activated = activated.astype(BF)
    d_activated = jnp.dot(g_all, w_out[:, HEAD_DIM:], preferred_element_type=F32)
    d_expanded = gelu_back(d_activated)[0].astype(BF)

    bases = base.reshape(2, ways, HEADS, 2, runs)
    own_base = lax.dynamic_index_in_dim(bases, x, 0, False)
    own_base = lax.dynamic_index_in_dim(own_base, w, 0, False)
    own_base = lax.dynamic_index_in_dim(own_base, c, 1, False)
    row_tokens = (own_base.T[:, :, None] + within).reshape(runs, rows_run)
    col_tokens = (bases.transpose(4, 1, 0, 3, 2)[..., None] + within).reshape(runs, run_size)

    def meta(tokens):
        is_prompt = tokens < prompt_total
        cont = (tokens - prompt_total) // CONT
        if one_prompt:
            prompt = jnp.zeros_like(tokens)
        else:
            matches = cont[..., None] == jnp.arange(cont_parent.shape[0], dtype=jnp.int32)
            prompt = jnp.where(is_prompt, tokens // PROMPT, jnp.sum(jnp.where(matches, cont_parent, 0), -1))
        segment = jnp.where(is_prompt, -1 - tokens // PROMPT, cont)
        return tokens, segment, prompt

    row_meta = jnp.stack(meta(row_tokens), -1)
    col_meta = jnp.stack(meta(col_tokens), 1)
    attended, d_queries, d_keys, d_values = attention(
        prompt_runs, one_prompt,
        queries.reshape(runs, rows_run, HEAD_DIM), d_attended.reshape(runs, rows_run, HEAD_DIM),
        pairs[..., :HEAD_DIM], pairs[..., HEAD_DIM:], row_meta, col_meta,
    )
    attended = attended.reshape(group_rows, HEAD_DIM)

    contract = (((1,), (1,)), ((), ()))
    tokens_dims = (((0,), (0,)), ((), ()))
    left = jnp.concatenate([attended, activated], 1)
    out_part = lax.dot_general(left, w_out, contract, preferred_element_type=F32).astype(BF)
    out_sum = collect(ways, out_part.reshape(runs, HEADS, STRIPE, width), 3).reshape(tok_dev, width)
    output = restored((states + out_sum + out_bias).astype(BF))

    d_pairs = jnp.concatenate([d_keys, d_values], -1).astype(BF)
    d_pairs = fold(ways, d_pairs.reshape(runs, 4 * ways, rows_run, 2 * HEAD_DIM)).reshape(group_rows, 2 * HEAD_DIM)
    d_mixed = jnp.concatenate(
        [
            rotate(d_queries.reshape(group_rows, HEAD_DIM).astype(BF).astype(F32), cosine, -sine),
            rotate(d_pairs[:, :HEAD_DIM].astype(BF).astype(F32), cosine, -sine),
            d_pairs[:, HEAD_DIM:],
        ],
        1,
    ).astype(BF)

    right = jnp.concatenate([d_mixed, d_expanded], 1)
    e_part = lax.dot_general(right, w_in, contract, preferred_element_type=F32).astype(BF)
    e_sum = collect(ways, e_part.reshape(runs, HEADS, STRIPE, width), 4).reshape(tok_dev, width)
    dx = inverse_spread * (
        e_sum - jnp.mean(e_sum, -1, keepdims=True) - normed * jnp.mean(e_sum * normed, -1, keepdims=True)
    )
    input_grad = restored((grad_out + dx).astype(BF))

    part = jnp.concatenate(
        [
            lax.dot_general(n_all, right, tokens_dims, preferred_element_type=F32).astype(BF),
            lax.dot_general(g_all, left, tokens_dims, preferred_element_type=F32).astype(BF),
        ],
        1,
    )
    part = part.reshape(2, ways, HEADS, 2, rows, part.shape[1])
    sums = jnp.sum(right.astype(F32), 0).reshape(note_rows, lanes)
    g_sums = jnp.pad(jnp.sum(grad_out, 0).reshape(devices, 1, rows), ((0, 0), (0, 0), (0, lanes - rows)))
    sum_notes = jnp.concatenate(
        [
            jnp.broadcast_to(sums[None], (devices, note_rows, lanes)),
            g_sums,
            jnp.zeros((devices, 1, lanes), F32),
        ],
        1,
    ).reshape(2, ways, HEADS, 2, note_rows + 2, lanes)
    owned, owned_notes = to_owners(ways, part, sum_notes)
    owned = owned.astype(F32)

    def join_qkv(values):
        return values.reshape(HEADS, -1, 3, HEAD_DIM).transpose(1, 2, 0, 3).reshape(-1, 3 * width)

    def join(values):
        return values.transpose(1, 0, 2).reshape(values.shape[1], -1)

    raw_qkv = join_qkv(owned[..., :head3])
    raw_expand = join(owned[..., head3:block_columns])
    dense_grad = join(owned[..., block_columns : block_columns + HEAD_DIM])
    shrink_grad = join(owned[..., block_columns + HEAD_DIM :])
    column_sums = owned_notes[:, :note_rows].reshape(HEADS, 1, block_columns)
    qkv_sum = join_qkv(column_sums[..., :head3])
    expand_sum = join(column_sums[..., head3:])
    bias_grad = jnp.sum(owned_notes[:, note_rows, :rows], 0)
    qkv_grad = gain_one[:, None] * raw_qkv + shift_one[:, None] * qkv_sum
    expand_grad = gain_two[:, None] * raw_expand + shift_two[:, None] * expand_sum

    def own(values, count):
        return lax.dynamic_slice_in_dim(values, me * count, count, 0)

    return (
        output,
        input_grad,
        jnp.sum(qkv_wide * raw_qkv, 1),
        jnp.sum(qkv_wide * qkv_sum, 1),
        jnp.sum(expand_wide * raw_expand, 1),
        jnp.sum(expand_wide * expand_sum, 1),
        qkv_grad,
        own(qkv_sum[0, : 2 * width], 2 * width // devices),
        own(qkv_sum[0, 2 * width :], width // devices),
        dense_grad,
        bias_grad,
        expand_grad,
        own(expand_sum[0], HEADS * hidden // devices),
        shrink_grad,
        bias_grad,
    )


def solution(mesh):
    matrix, vector = P(("head", "blk"), None), P(("head", "blk"))
    return jax.shard_map(
        per_device,
        mesh=mesh,
        in_specs=(
            matrix, vector, vector, vector, vector, matrix, vector, matrix, vector, matrix, vector, matrix, vector,
            P(), P(), vector, matrix,
        ),
        out_specs=(
            matrix, matrix, vector, vector, vector, vector, matrix, vector, vector, matrix, vector, matrix, vector,
            matrix, vector,
        ),
        check_vma=False,
    )
```

```python
import functools
import math

import jax
import jax.numpy as jnp
from jax import lax
from jax.experimental import pallas as pl
from jax.experimental.pallas import tpu as pltpu
from jax.sharding import PartitionSpec as P

HEADS = 8
HEAD_DIM = 256
ROT = 64
PROMPT = 2048
CONT = 256
STRIPE = 16
MESH = pl.DeviceIdType.MESH
BF = jnp.bfloat16
F32 = jnp.float32
ANY = pl.BlockSpec(memory_space=pl.ANY)
VMEM = pl.BlockSpec(memory_space=pltpu.VMEM)
DMA = pltpu.SemaphoreType.DMA


class Place:
    def __init__(self, ways):
        self.ways = ways
        self.x = lax.axis_index("head")
        b = lax.axis_index("blk")
        self.c = b % 2
        self.h = (b // 2) % HEADS
        self.w = b // (2 * HEADS)
        self.hy = self.h % 2
        self.hz = self.h // 2

    def device(self, x=None, w=None, h=None, c=None):
        x = self.x if x is None else x
        w = self.w if w is None else w
        h = self.h if h is None else h
        c = self.c if c is None else c
        return (x, w * (2 * HEADS) + h * 2 + c)

    def peers_h(self):
        return [self.device(h=(self.h + k) % HEADS) for k in range(1, HEADS)]

    def peers_w(self):
        return [self.device(w=(self.w + k) % self.ways) for k in range(1, self.ways)]

    def peer_x(self):
        return self.device(x=1 - self.x)

    def peer_c(self):
        return self.device(c=1 - self.c)

    def peer_y(self):
        return self.device(h=self.h + 1 - 2 * self.hy)


def greet(devices):
    barrier = pltpu.get_barrier_semaphore()
    for one in devices:
        pl.semaphore_signal(barrier, inc=1, device_id=one, device_id_type=MESH)
    pl.semaphore_wait(barrier, len(devices))


def remote(src, dst, send, recv, device):
    return pltpu.make_async_remote_copy(
        src_ref=src, dst_ref=dst, send_sem=send, recv_sem=recv, device_id=device, device_id_type=MESH
    )


def call(body, out_shape, ins, scratch, ident, out_spec=ANY, in_spec=ANY):
    return pl.pallas_call(
        body,
        out_shape=out_shape,
        in_specs=[in_spec] * len(ins),
        out_specs=jax.tree.map(lambda _: out_spec, out_shape),
        scratch_shapes=scratch,
        compiler_params=pltpu.CompilerParams(
            collective_id=ident, has_side_effects=True, vmem_limit_bytes=60 * 2**20
        ),
    )(*ins)


LINE = HEADS // 2


def spread_rows(place, own, full, up, down, side, recv):
    hz, hy = place.hz, place.hy

    def piece(src, z, target, send):
        idx = z * 2 + hy
        return remote(src, full.at[:, idx], send, recv.at[idx], target)

    def up_to():
        return place.device(h=place.h + 2)

    def down_to():
        return place.device(h=place.h - 2)

    def first():
        @pl.when(hz < LINE - 1)
        def _():
            piece(own, hz, up_to(), up.at[0]).start()

        @pl.when(hz > 0)
        def _():
            piece(own, hz, down_to(), down.at[0]).start()

        piece(own, hz, place.peer_y(), side.at[0]).start()

    def arrived(idx):
        remote(full.at[:, idx], full.at[:, idx], side.at[0], recv.at[idx], place.peer_y()).wait_recv()

    def step(s):
        low, high = hz - s - 1, hz + s + 1

        @pl.when(low >= 0)
        def _():
            arrived(low * 2 + hy)
            src = full.at[:, low * 2 + hy]

            @pl.when(hz < LINE - 1)
            def _():
                piece(src, low, up_to(), up.at[s + 1]).start()

            piece(src, low, place.peer_y(), side.at[low + 1]).start()

        @pl.when(high < LINE)
        def _():
            arrived(high * 2 + hy)
            src = full.at[:, high * 2 + hy]

            @pl.when(hz > 0)
            def _():
                piece(src, high, down_to(), down.at[s + 1]).start()

            piece(src, high, place.peer_y(), side.at[high + 1]).start()

    def finish():
        for z in range(LINE):
            arrived(z * 2 + 1 - hy)

    def sent():
        piece(own, hz, place.peer_y(), side.at[0]).wait_send()
        for z in range(LINE):
            @pl.when(z != hz)
            def _():
                piece(own, z, place.peer_y(), side.at[z + 1]).wait_send()
        for s in range(LINE - 1):
            @pl.when((hz < LINE - 1) & (hz - s >= 0))
            def _():
                piece(own, hz, up_to(), up.at[s]).wait_send()

            @pl.when((hz > 0) & (hz + s < LINE))
            def _():
                piece(own, hz, down_to(), down.at[s]).wait_send()

    return first, step, finish, sent


def gather_kernel(ways, n_in, g_in, w_in, m_in, n_all, g_all, w_all, m_all,
                  local, nu, nd, ns, nr, gu, gd, gs, gr, wa, wx, wc, wr, ma, mx, mc, mr):
    place = Place(ways)
    x, w, h, c = place.x, place.w, place.h, place.c
    stage_a = [(dw, dh) for dw in range(ways) for dh in range(HEADS) if (dw, dh) != (0, 0)]
    greet(
        [place.device(w=(w + dw) % ways, h=(h + dh) % HEADS) for dw, dh in stage_a]
        + [place.peer_x(), place.peer_c()]
    )
    n_first, n_step, n_finish, n_sent = spread_rows(place, n_in, n_all, nu, nd, ns, nr)
    g_first, g_step, g_finish, g_sent = spread_rows(place, g_in, g_all, gu, gd, gs, gr)
    copies = [
        pltpu.make_async_copy(n_in, n_all.at[:, h], local.at[0]),
        pltpu.make_async_copy(g_in, g_all.at[:, h], local.at[1]),
        pltpu.make_async_copy(w_in.at[h], w_all.at[x, w, h, c], local.at[2]),
        pltpu.make_async_copy(m_in.at[h], m_all.at[x, w, h, c], local.at[3]),
    ]
    n_first()
    sends = []

    def send(src, dst, s, r, device):
        copy = remote(src, dst, s, r, device)
        copy.start()
        sends.append(copy)

    pairs = ((w_all, wa, wx, wc, wr), (m_all, ma, mx, mc, mr))
    for k, (dw, dh) in enumerate(stage_a):
        h2 = (h + dh) % HEADS
        target = place.device(w=(w + dw) % ways, h=h2)
        send(w_in.at[h2], w_all.at[x, w, h, c], wa.at[k], wr.at[x, w, h, c], target)
        send(m_in.at[h2], m_all.at[x, w, h, c], ma.at[k], mr.at[x, w, h, c], target)
    send(w_in.at[h], w_all.at[x, w, h, c], wx.at[w, h], wr.at[x, w, h, c], place.peer_x())
    send(m_in.at[h], m_all.at[x, w, h, c], mx.at[w, h], mr.at[x, w, h, c], place.peer_x())
    send(w_in.at[h], w_all.at[x, w, h, c], wc.at[x, w, h], wr.at[x, w, h, c], place.peer_c())
    send(m_in.at[h], m_all.at[x, w, h, c], mc.at[x, w, h], mr.at[x, w, h, c], place.peer_c())
    g_first()
    for copy in copies:
        copy.start()

    def arrived(full, recv, xs, ws, hs, cs):
        place_ref = full.at[xs, ws, hs, cs]
        remote(place_ref, place_ref, local.at[0], recv.at[xs, ws, hs, cs], place.peer_x()).wait_recv()

    for s in range(LINE - 1):
        n_step(s)
    for dw, dh in stage_a:
        ws, hs = (w - dw) % ways, (h - dh) % HEADS
        for full, _, to_x, to_c, recv in pairs:
            arrived(full, recv, x, ws, hs, c)
            block = full.at[x, ws, hs, c]
            send(block, block, to_x.at[ws, hs], recv.at[x, ws, hs, c], place.peer_x())
            send(block, block, to_c.at[x, ws, hs], recv.at[x, ws, hs, c], place.peer_c())
    for s in range(LINE - 1):
        g_step(s)
    for dw, dh in [(0, 0)] + stage_a:
        ws, hs = (w - dw) % ways, (h - dh) % HEADS
        for full, _, _, to_c, recv in pairs:
            arrived(full, recv, 1 - x, ws, hs, c)
            block = full.at[1 - x, ws, hs, c]
            send(block, block, to_c.at[1 - x, ws, hs], recv.at[1 - x, ws, hs, c], place.peer_c())
    n_finish()
    g_finish()
    for dw, dh in [(0, 0)] + stage_a:
        ws, hs = (w - dw) % ways, (h - dh) % HEADS
        for full, _, _, _, recv in pairs:
            for xs in (x, 1 - x):
                arrived(full, recv, xs, ws, hs, 1 - c)
    for copy in copies:
        copy.wait()
    for copy in sends:
        copy.wait_send()
    n_sent()
    g_sent()


def gather_all(ways, normed, grads, weights, notes):
    runs, _, width = normed.shape
    _, rows, columns = weights.shape
    blocks = (2, ways, HEADS, 2)
    shapes = (
        jax.ShapeDtypeStruct((runs, HEADS, STRIPE, width), BF),
        jax.ShapeDtypeStruct((runs, HEADS, STRIPE, width), BF),
        jax.ShapeDtypeStruct(blocks + (rows, columns), BF),
        jax.ShapeDtypeStruct(blocks + notes.shape[1:], F32),
    )
    row_sems = [DMA((LINE,)), DMA((LINE,)), DMA((LINE + 1,)), DMA((HEADS,))]
    block_sems = [DMA((ways * HEADS,)), DMA((ways, HEADS)), DMA((2, ways, HEADS)), DMA(blocks)]
    return call(
        functools.partial(gather_kernel, ways),
        shapes,
        (normed, grads, weights, notes),
        [DMA((4,))] + row_sems + row_sems + block_sems + block_sems,
        0,
    )


def exchange_kernel(ways, own, full, local, to_w, to_x, to_c, recv):
    place = Place(ways)
    x, w, c = place.x, place.w, place.c
    runs = own.shape[0]
    parts = 4
    span = runs // parts
    greet(place.peers_w() + [place.peer_x(), place.peer_c()])

    def spot(ws, xs, cs, p):
        return full.at[pl.ds(p * span, span), ws * 4 + xs * 2 + cs]

    sends = []

    def send(src, ws, xs, cs, p, sem, device):
        copy = remote(src, spot(ws, xs, cs, p), sem, recv.at[ws, xs, cs, p], device)
        copy.start()
        sends.append(copy)

    def arrived(ws, xs, cs, p):
        remote(spot(ws, xs, cs, p), spot(ws, xs, cs, p), local.at[0], recv.at[ws, xs, cs, p], place.peer_x()).wait_recv()

    keep = pltpu.make_async_copy(own, full.at[:, w * 4 + x * 2 + c], local.at[0])
    for p in range(parts):
        src = own.at[pl.ds(p * span, span)]
        for k, device in enumerate(place.peers_w()):
            send(src, w, x, c, p, to_w.at[k, p], device)
        send(src, w, x, c, p, to_x.at[w, p], place.peer_x())
    for p in range(parts):
        send(own.at[pl.ds(p * span, span)], w, x, c, p, to_c.at[w, x, p], place.peer_c())
    keep.start()
    for k in range(1, ways):
        ws = (w - k) % ways
        for p in range(parts):
            arrived(ws, x, c, p)
            send(spot(ws, x, c, p), ws, x, c, p, to_x.at[ws, p], place.peer_x())
            send(spot(ws, x, c, p), ws, x, c, p, to_c.at[ws, x, p], place.peer_c())
    for k in range(ways):
        ws = (w - k) % ways
        for p in range(parts):
            arrived(ws, 1 - x, c, p)
            send(spot(ws, 1 - x, c, p), ws, 1 - x, c, p, to_c.at[ws, 1 - x, p], place.peer_c())
    for k in range(ways):
        ws = (w - k) % ways
        for p in range(parts):
            arrived(ws, x, 1 - c, p)
            arrived(ws, 1 - x, 1 - c, p)
    keep.wait()
    for copy in sends:
        copy.wait_send()


def exchange(ways, own):
    runs, rows, columns = own.shape
    return call(
        functools.partial(exchange_kernel, ways),
        jax.ShapeDtypeStruct((runs, 4 * ways, rows, columns), BF),
        (own,),
        [DMA((1,)), DMA((ways, 4)), DMA((ways, 4)), DMA((ways, 2, 4)), DMA((ways, 2, 2, 4))],
        1,
    )


def turn(u, tables, sign):
    cosine, lower, upper = tables
    front = u[:, :128]
    moved = pltpu.roll(front, 96, 1) * lower + pltpu.roll(front, 32, 1) * upper
    return jnp.concatenate([front * cosine + moved * sign, u[:, 128:]], 1)


def finish_kernel(ways, att, act, dexp, dq, dkv, tables, w_out, w_in, n_all, g_all, note,
                  out_sum, e_sum, own_a, own_b, note_all,
                  v_left, v_right, v_w, v_turn, kv_own, kv_c, kv_x,
                  o_p, o_y, o_1, o_2, e_p, e_y, e_1, e_2,
                  raw, flat, ring, a_c, a_x, a_w, b_c, b_x, b_w, n_mine, n_c, n_x, n_w,
                  load, load_raw, kv_load, kv_s, kv_r, kvx_s, kvx_r,
                  oy_s, oy_r, o1_s, o1_r, o2_s, o2_r, ey_s, ey_r, e1_s, e1_r, e2_s, e2_r,
                  ac_s, ac_r, ax_s, ax_r, aw_s, aw_r, ah_s, ah_r,
                  bc_s, bc_r, bx_s, bx_r, bw_s, bw_r, bh_s, bh_r, keep, n_s, n_r):
    place = Place(ways)
    x, w, h, c, hy, hz = place.x, place.w, place.h, place.c, place.hy, place.hz
    d0, d1 = hz % 2, hz // 2
    runs = v_left.shape[0]
    chunks = o_p.shape[0]
    wide = o_p.shape[-1]
    rows = own_a.shape[1]
    hp = 256 // (2 * rows)
    tiles = HEADS // hp
    a_cols, b_cols = own_a.shape[2], own_b.shape[2]
    inner = w_out.shape[1]
    head3 = 3 * HEAD_DIM
    group = runs * HEADS * STRIPE
    sends = []

    def send(src, dst, s, r, device):
        copy = remote(src, dst, s, r, device)
        copy.start()
        sends.append(copy)
        return copy

    greet(place.peers_h() + place.peers_w() + [place.peer_x(), place.peer_c()])

    def fetch(src, dst, k):
        copy = pltpu.make_async_copy(src, dst, load.at[k])
        copy.start()
        return copy

    early = [
        fetch(att, v_left.at[..., :HEAD_DIM], 0),
        fetch(act, v_left.at[..., HEAD_DIM:], 1),
        fetch(w_out, v_w.at[:, :inner], 2),
    ]

    kv_first, kv_mine = [], []
    for k, xs in ((0, 1 - x), (1, x)):
        kv_first.append(send(dkv.at[:, xs * 2 + 1 - c], kv_c.at[:, k], kv_s.at[k], kv_r.at[k], place.peer_c()))
        kv_mine.append(pltpu.make_async_copy(dkv.at[:, xs * 2 + c], kv_own.at[:, k], kv_load.at[k]))
        kv_mine[k].start()
    late = [
        fetch(dexp, v_right.at[..., head3:], 3),
        fetch(dq, v_right.at[..., :HEAD_DIM], 4),
        fetch(tables, v_turn, 5),
    ]

    def partial(src, q, buf, depth):
        @pl.loop(0, wide // 256)
        def _(k):
            at = pl.multiple_of(k * 256, 256)
            value = lax.dot_general(
                src[...].reshape(group, depth),
                v_w[pl.ds(pl.multiple_of(q * wide + at, 256), 256), :depth],
                (((1,), (1,)), ((), ())),
                preferred_element_type=F32,
            )
            buf[q, :, :, :, :, :, pl.ds(at, 256)] = value.astype(BF).reshape(runs, 2, 2, 2, STRIPE, 256)

    def sums(buf, y, one, two, s_y, r_y, s_1, r_1, s_2, r_2, total):
        def start(q):
            return send(buf.at[q, :, :, :, 1 - hy], y.at[q], s_y.at[q], r_y.at[q], place.peer_y())

        def after_y(q, copy):
            copy.wait_recv()

            @pl.loop(0, runs)
            def _(run):
                for t in range(LINE):
                    value = y[q, run, t // 2, t % 2].astype(F32) + buf[q, run, t // 2, t % 2, hy].astype(F32)
                    y[q, run, t // 2, t % 2] = value.astype(BF)

            target = place.device(h=(hz + 1 - 2 * d0) * 2 + hy)
            return send(y.at[q, :, :, 1 - d0], one.at[q], s_1.at[q], r_1.at[q], target)

        def after_1(q, copy):
            copy.wait_recv()

            @pl.loop(0, runs)
            def _(run):
                for t in range(2):
                    value = one[q, run, t].astype(F32) + y[q, run, t, d0].astype(F32)
                    one[q, run, t] = value.astype(BF)

            target = place.device(h=((1 - d1) * 2 + d0) * 2 + hy)
            return send(one.at[q, :, 1 - d1], two.at[q], s_2.at[q], r_2.at[q], target)

        def after_2(q, copy):
            copy.wait_recv()

            @pl.loop(0, runs)
            def _(run):
                total[run, :, q * wide : (q + 1) * wide] = two[q, run].astype(F32) + one[q, run, d1].astype(F32)

        return start, after_y, after_1, after_2

    o_start, o_after_y, o_after_1, o_after_2 = sums(o_p, o_y, o_1, o_2, oy_s, oy_r, o1_s, o1_r, o2_s, o2_r, out_sum)
    e_start, e_after_y, e_after_1, e_after_2 = sums(e_p, e_y, e_1, e_2, ey_s, ey_r, e1_s, e1_r, e2_s, e2_r, e_sum)

    for copy in early:
        copy.wait()
    o_step = {}
    for q in range(chunks):
        partial(v_left, q, o_p, inner)
        o_step[q] = o_start(q)
    w_load = fetch(w_in, v_w, 6)

    def kv_add(k, final):
        kv_mine[k].wait()
        kv_first[k].wait_recv()

        @pl.loop(0, runs)
        def _(run):
            value = kv_own[run, k].astype(F32) + kv_c[run, k].astype(F32)
            if final:
                value = value + kv_x[run].astype(F32)
                back = turn(value[:, :HEAD_DIM].astype(BF).astype(F32), [v_turn[t, run] for t in range(3)], -1.0)
                shape = (LINE, 2, STRIPE, HEAD_DIM)
                v_right[run, :, :, :, HEAD_DIM : 2 * HEAD_DIM] = back.astype(BF).reshape(shape)
                v_right[run, :, :, :, 2 * HEAD_DIM : head3] = value[:, HEAD_DIM:].astype(BF).reshape(shape)
            else:
                kv_c[run, k] = value.astype(BF)

    kv_add(0, False)
    kv_second = remote(kv_c.at[:, 0], kv_x, kvx_s.at[0], kvx_r.at[0], place.peer_x())
    kv_second.start()
    for copy in late:
        copy.wait()

    order_t = [(k, dw, dt) for k in range(2) for dw in list(range(1, ways)) + [0] for dt in list(range(1, tiles)) + [0]]
    own_t = h // hp

    def where(k, dw, dt):
        return (1 - x if k == 0 else x), (w + dw) % ways, (own_t + dt) % tiles

    def raw_copy(n, src, buf):
        xs, ws, t = where(*order_t[n])
        at = pl.multiple_of(((xs * ways + ws) * tiles + t) * 256, 256)
        return pltpu.make_async_copy(src.at[:, pl.ds(at, 256)], raw.at[n % 2, buf], load_raw.at[n % 2, buf])

    def product(n, buf, src, first, count, at):
        flat[...] = raw[n % 2, buf].T

        @pl.loop(0, count // 256)
        def _(k):
            col = pl.multiple_of(k * 256, 256)
            value = jnp.dot(
                flat[...], src[..., pl.ds(first + col, 256)].reshape(group, 256), preferred_element_type=F32
            )
            ring[n % 3, :, :, :, pl.ds(at + col, 256)] = value.astype(BF).reshape(hp, 2, rows, 256)

    def grads(cols, from_c, from_x, from_w, c_s, c_r, x_s, x_r, w_s, w_r, h_s, h_r, out, fill, need, flag):
        first, second, third, last = {}, {}, {}, []

        def begin(n):
            for buf, src in need:
                raw_copy(n, src, buf).start()

        def make(n):
            if n >= 3:
                first[n - 3].wait_send()
            for buf, src in need:
                raw_copy(n, src, buf).wait()
            fill(n)
            if n + 1 < len(order_t):
                begin(n + 1)
            k, dw, dt = order_t[n]
            first[n] = remote(
                ring.at[n % 3, :, 1 - c, :, pl.ds(0, cols)], from_c.at[k, dw, dt], c_s.at[n], c_r.at[n], place.peer_c()
            )
            first[n].start()

        def mine(n):
            k, dw, dt = order_t[n]
            first[n].wait_recv()

            @pl.loop(0, hp)
            def _(q):
                value = from_c[k, dw, dt, q].astype(F32) + ring[n % 3, q, c, :, :cols].astype(F32)
                from_c[k, dw, dt, q] = value.astype(BF)

        def cross(n):
            k, dw, dt = order_t[n]
            second[dw, dt] = send(from_c.at[0, dw, dt], from_x.at[dw, dt], x_s.at[dw, dt], x_r.at[dw, dt], place.peer_x())

        def close(n):
            k, dw, dt = order_t[n]
            _, ws, t = where(k, dw, dt)
            second[dw, dt].wait_recv()
            more = [from_x.at[dw, dt]]
            if dw == 0:
                for dv in range(1, ways):
                    third[dv, dt].wait_recv()
                    more.append(from_w.at[dv - 1, dt])

            @pl.loop(0, hp)
            def _(q):
                value = from_c[1, dw, dt, q].astype(F32)
                for ref in more:
                    value = value + ref[q].astype(F32)
                from_c[1, dw, dt, q] = value.astype(BF)

            if dw != 0:
                third[dw, dt] = send(from_c.at[1, dw, dt], from_w.at[dw - 1, dt], w_s.at[dw - 1, dt], w_r.at[dw - 1, dt], place.device(w=ws))
                return
            for q in range(hp):
                hs = t * hp + q
                at = dt * hp + q

                @pl.when(hs != h)
                def _():
                    remote(from_c.at[1, 0, dt, q], out.at[h], h_s.at[at], h_r.at[h], place.device(h=hs)).start()

                @pl.when(hs == h)
                def _():
                    pltpu.make_async_copy(from_c.at[1, 0, dt, q], out.at[h], keep.at[flag]).start()

        def drain():
            for n in range(max(len(order_t) - 3, 0), len(order_t)):
                first[n].wait_send()

        def end():
            for n in range(len(order_t)):
                k, dw, dt = order_t[n]
                if k == 1 and dw == 0:
                    _, _, t = where(k, dw, dt)
                    for q in range(hp):
                        hs = t * hp + q

                        @pl.when(hs != h)
                        def _():
                            remote(from_c.at[1, 0, dt, q], out.at[h], h_s.at[dt * hp + q], h_r.at[h], place.device(h=hs)).wait_send()
            for dh in range(1, HEADS):
                hs = (h + dh) % HEADS
                remote(out.at[hs], out.at[hs], h_s.at[0], h_r.at[hs], place.peer_x()).wait_recv()
            pltpu.make_async_copy(from_c.at[1, 0, 0, 0], out.at[h], keep.at[flag]).wait()

        return begin, make, mine, cross, close, drain, end

    def fill_a(n):
        product(n, 1, v_left, 0, inner, 0)
        product(n, 0, v_right, head3, a_cols - inner, inner)

    def fill_b(n):
        product(n, 0, v_right, 0, head3, 0)

    a_begin, a_make, a_mine, a_cross, a_close, a_drain, a_end = grads(
        a_cols, a_c, a_x, a_w, ac_s, ac_r, ax_s, ax_r, aw_s, aw_r, ah_s, ah_r, own_a, fill_a, ((0, n_all), (1, g_all)), 0
    )
    b_begin, b_make, b_mine, b_cross, b_close, b_drain, b_end = grads(
        b_cols, b_c, b_x, b_w, bc_s, bc_r, bx_s, bx_r, bw_s, bw_r, bh_s, bh_r, own_b, fill_b, ((0, n_all),), 1
    )
    count = len(order_t)
    half = count // 2
    a_begin(0)
    for n in range(half):
        a_make(n)
        a_mine(n)
        if n == 0:
            kv_second.wait_send()
        a_cross(n)
        if n == 1:
            o_step[0] = o_after_y(0, o_step[0])
    o_step[1] = o_after_y(1, o_step[1])
    o_step[0] = o_after_1(0, o_step[0])

    kv_second.wait_recv()
    kv_add(1, True)
    w_load.wait()
    e_step = {}
    for q in range(chunks):
        partial(v_right, q, e_p, v_right.shape[-1])
        e_step[q] = e_start(q)
        if q == 1:
            o_step[2] = o_after_y(2, o_step[2])
            o_step[1] = o_after_1(1, o_step[1])
    o_after_2(0, o_step[0])

    def fold_columns(first, cols, row):
        @pl.loop(0, cols // 128)
        def _(k):
            at = pl.multiple_of(k * 128, 128)
            value = v_right[..., pl.ds(first + at, 128)].reshape(group, 128).astype(F32)
            n_mine[pl.ds(row + k, 1), :] = jnp.sum(value, 0, keepdims=True)

    n_load = pltpu.make_async_copy(note, n_mine, keep.at[2])
    n_load.start()
    n_load.wait()
    fold_columns(0, v_right.shape[-1], 0)
    note_copy = send(n_mine, n_c, n_s.at[0], n_r.at[0], place.peer_c())

    note_w = []
    for n in range(half, count):
        a_make(n)
        a_mine(n)
        if n == half:
            note_copy.wait_recv()
            n_c[...] = n_c[...] + n_mine[...]
            note_copy = send(n_c, n_x, n_s.at[1], n_r.at[1], place.peer_x())
        a_close(n)
        if n == half + 1:
            note_copy.wait_recv()
            n_x[...] = n_x[...] + n_c[...]
            for k, device in enumerate(place.peers_w()):
                note_w.append(send(n_x, n_w.at[k], n_s.at[2 + k], n_r.at[2 + k], device))
            o_step[3] = o_after_y(3, o_step[3])
            o_step[2] = o_after_1(2, o_step[2])
    o_after_2(1, o_step[1])
    o_step[3] = o_after_1(3, o_step[3])
    for k, copy in enumerate(note_w):
        copy.wait()
    total = n_x[...]
    for k in range(ways - 1):
        total = total + n_w[k]
    n_x[...] = total
    base = 1 + ways
    for dh in range(1, HEADS):
        send(n_x, note_all.at[h], n_s.at[base + dh], n_r.at[base + h], place.device(h=(h + dh) % HEADS))
    n_keep = pltpu.make_async_copy(n_x, note_all.at[h], keep.at[3])
    n_keep.start()

    a_drain()
    b_begin(0)
    for n in range(half):
        b_make(n)
        b_mine(n)
        b_cross(n)
        if n == 0:
            e_step[0] = e_after_y(0, e_step[0])
        if n == 1:
            o_after_2(2, o_step[2])
    e_step[1] = e_after_y(1, e_step[1])
    e_step[0] = e_after_1(0, e_step[0])
    o_after_2(3, o_step[3])
    for n in range(half, count):
        b_make(n)
        b_mine(n)
    e_step[2] = e_after_y(2, e_step[2])
    e_step[1] = e_after_1(1, e_step[1])
    e_after_2(0, e_step[0])
    for n in range(half, count):
        b_close(n)
    e_step[3] = e_after_y(3, e_step[3])
    e_step[2] = e_after_1(2, e_step[2])
    e_after_2(1, e_step[1])
    e_step[3] = e_after_1(3, e_step[3])
    e_after_2(2, e_step[2])
    e_after_2(3, e_step[3])
    a_end()
    b_drain()
    b_end()
    n_keep.wait()
    for dh in range(1, HEADS):
        hs = (h + dh) % HEADS
        remote(note_all.at[hs], note_all.at[hs], n_s.at[0], n_r.at[base + hs], place.peer_x()).wait_recv()
    for copy in sends:
        if not any(copy is other for other in note_w):
            copy.wait_send()


def finish(ways, rows, att, act, dexp, dq, dkv, tables, w_out, w_in, n_all, g_all, note):
    width, inner = w_out.shape
    right = w_in.shape[1]
    head3 = 3 * HEAD_DIM
    a_cols, b_cols = inner + right - head3, head3
    group = n_all.shape[0]
    runs, _, per_run, pair = dkv.shape
    lines = (runs, LINE, 2, STRIPE)
    hp = 256 // (2 * rows)
    tiles = HEADS // hp
    chunks, wide = 4, width // 4
    extra = max(ways - 1, 1)
    count = 2 * ways * tiles

    def vm(shape, kind=BF):
        return pltpu.VMEM(shape, kind)

    def row_buffers():
        return [
            vm((chunks, runs, 2, 2, 2, STRIPE, wide)),
            vm((chunks, runs, 2, 2, STRIPE, wide)),
            vm((chunks, runs, 2, STRIPE, wide)),
            vm((chunks, runs, STRIPE, wide)),
        ]

    def spare(shape):
        return shape if ways > 1 else (1,) * (len(shape) - 2) + (16, 128)

    def gradient_buffers(cols):
        return [
            vm((2, ways, tiles, hp, rows, cols)),
            vm((ways, tiles, hp, rows, cols)),
            vm(spare((extra, tiles, hp, rows, cols))),
        ]

    def gradient_sems():
        return [
            DMA((count,)), DMA((count,)), DMA((ways, tiles)), DMA((ways, tiles)), DMA((extra, tiles)), DMA((extra, tiles)),
            DMA((HEADS,)), DMA((HEADS,)),
        ]

    scratch = (
        [
            vm(lines + (inner,)), vm(lines + (right,)), vm((width, right)), vm(tables.shape, F32),
            vm((runs, 2, per_run, pair)), vm((runs, 2, per_run, pair)), vm((runs, per_run, pair)),
        ]
        + row_buffers() + row_buffers()
        + [vm((2, 2, group, 256)), vm((256, group)), vm((3, hp, 2, rows, a_cols))]
        + gradient_buffers(a_cols) + gradient_buffers(b_cols)
        + [vm(note.shape, F32)] * 3 + [vm((extra,) + note.shape, F32)]
        + [DMA((7,)), DMA((2, 2)), DMA((2,)), DMA((2,)), DMA((2,)), DMA((1,)), DMA((1,))]
        + [DMA((chunks,))] * 12
        + gradient_sems() + gradient_sems()
        + [DMA((4,)), DMA((1 + ways + HEADS,)), DMA((1 + ways + HEADS,))]
    )
    shapes = (
        jax.ShapeDtypeStruct((runs, STRIPE, width), F32),
        jax.ShapeDtypeStruct((runs, STRIPE, width), F32),
        jax.ShapeDtypeStruct((HEADS, rows, a_cols), BF),
        jax.ShapeDtypeStruct((HEADS, rows, b_cols), BF),
        jax.ShapeDtypeStruct((HEADS,) + note.shape, F32),
    )
    ins = (
        att.reshape(lines + (HEAD_DIM,)), act.reshape(lines + (inner - HEAD_DIM,)), dexp.reshape(lines + (right - head3,)),
        dq.reshape(lines + (HEAD_DIM,)), dkv, tables, w_out, w_in, n_all, g_all, note,
    )
    return pl.pallas_call(
        functools.partial(finish_kernel, ways),
        out_shape=shapes,
        in_specs=[ANY] * len(ins),
        out_specs=(VMEM, VMEM, ANY, ANY, ANY),
        scratch_shapes=scratch,
        compiler_params=pltpu.CompilerParams(collective_id=2, has_side_effects=True, vmem_limit_bytes=62 * 2**20),
    )(*ins)


def attention_kernel(prompt_runs, one_prompt, q_ref, do_ref, kv_ref, row_ref, col_ref, turn_ref,
                     o_ref, dq_ref, dkv_ref, s_ref, sum_ref):
    runs, m, _ = q_ref.shape
    keys = kv_ref.shape[1]
    by_rows = (((1,), (1,)), ((), ()))
    by_tokens = (((0,), (0,)), ((), ()))

    def dot(a, b, dims):
        return lax.dot_general(a, b, dims, preferred_element_type=F32)

    def mask(i, k):
        rows, cols = row_ref[i], col_ref[k]
        if i == k:
            return (rows[:, 1:2] == cols[1:2, :]) & (cols[0:1, :] <= rows[:, 0:1])
        if one_prompt:
            return None
        return rows[:, 2:3] == cols[2:3, :]

    for i in range(runs):
        pieces = list(range(min(i + 1, prompt_runs))) + ([i] if i >= prompt_runs else [])
        q = q_ref[i]
        peak = None
        for at, k in enumerate(pieces):
            s = dot(q, kv_ref[k, :, :HEAD_DIM], by_rows)
            keep = mask(i, k)
            if keep is not None:
                s = jnp.where(keep, s, -1e30)
            s_ref[:, at * keys : (at + 1) * keys] = s
            top = jnp.max(s, -1, keepdims=True)
            peak = top if peak is None else jnp.maximum(peak, top)
        total = jnp.zeros((m, 1), F32)
        out = jnp.zeros((m, HEAD_DIM), F32)
        for at, k in enumerate(pieces):
            s = s_ref[:, at * keys : (at + 1) * keys]
            p = jnp.exp(s - peak)
            keep = mask(i, k)
            if keep is not None:
                p = jnp.where(keep, p, 0.0)
            s_ref[:, at * keys : (at + 1) * keys] = p
            total = total + jnp.sum(p, -1, keepdims=True)
            out = out + dot(p.astype(BF), kv_ref[k, :, HEAD_DIM:], (((1,), (0,)), ((), ())))
        inverse = 1.0 / total
        out = out * inverse
        o_ref[i] = out.astype(BF)
        do = do_ref[i]
        delta = jnp.sum(out * do.astype(F32), -1, keepdims=True)
        dq = jnp.zeros((m, HEAD_DIM), F32)
        for at, k in enumerate(pieces):
            p = s_ref[:, at * keys : (at + 1) * keys] * inverse
            dp = dot(do, kv_ref[k, :, HEAD_DIM:], by_rows)
            ds = (p * (dp - delta)).astype(BF)
            dq = dq + dot(ds, kv_ref[k, :, :HEAD_DIM], (((1,), (0,)), ((), ())))
            dk = dot(ds, q, by_tokens)
            dv = dot(p.astype(BF), do, by_tokens)
            if i == k:
                sum_ref[k, :, :HEAD_DIM] = dk
                sum_ref[k, :, HEAD_DIM:] = dv
            else:
                sum_ref[k, :, :HEAD_DIM] = sum_ref[k, :, :HEAD_DIM] + dk
                sum_ref[k, :, HEAD_DIM:] = sum_ref[k, :, HEAD_DIM:] + dv
        dq = (dq * (1.0 / math.sqrt(HEAD_DIM))).astype(BF).astype(F32)
        dq_ref[i] = turn(dq, [turn_ref[t, i] for t in range(3)], -1.0).astype(BF)
    dkv_ref[...] = sum_ref[...].astype(BF)


def attention(prompt_runs, one_prompt, queries, d_out, pairs, row_meta, col_meta, tables):
    m = queries.shape[1]
    count = pairs.shape[1]
    return pl.pallas_call(
        functools.partial(attention_kernel, prompt_runs, one_prompt),
        out_shape=(
            jax.ShapeDtypeStruct(queries.shape, BF),
            jax.ShapeDtypeStruct(queries.shape, BF),
            jax.ShapeDtypeStruct(pairs.shape, BF),
        ),
        in_specs=[VMEM] * 6,
        out_specs=(VMEM,) * 3,
        scratch_shapes=[pltpu.VMEM((m, (prompt_runs + 1) * count), F32), pltpu.VMEM(pairs.shape, F32)],
        compiler_params=pltpu.CompilerParams(vmem_limit_bytes=60 * 2**20),
    )(queries, d_out, pairs, row_meta, col_meta, tables)


def angles_of(positions):
    frequency = 10000.0 ** (-jnp.arange(0, ROT, 2, dtype=F32) / ROT)
    return positions.astype(F32)[:, None] * frequency[None, :]


def rotate(values, cosine, sine):
    half = ROT // 2
    leading, behind = values[:, :half], values[:, half:ROT]
    return jnp.concatenate(
        [leading * cosine - behind * sine, behind * cosine + leading * sine, values[:, ROT:]], -1
    )


def per_device(
    inputs, attn_norm_gain, attn_norm_bias, mlp_norm_gain, mlp_norm_bias, qkv_weight, qkv_bias, dense_weight,
    dense_bias, expand_weight, expand_bias, shrink_weight, shrink_bias, token_of_row, cont_parent, position_ids,
    cotangent,
):
    heads, blocks = lax.axis_size("head"), lax.axis_size("blk")
    devices = heads * blocks
    ways = blocks // (2 * HEADS)
    assert heads == 2 and blocks == ways * 2 * HEADS
    x = lax.axis_index("head")
    b = lax.axis_index("blk")
    me = x * blocks + b
    c, h, w = b % 2, (b // 2) % HEADS, b // (2 * HEADS)
    tok_dev, width = inputs.shape
    rows = qkv_weight.shape[0]
    hidden = expand_weight.shape[1] // HEADS
    runs = tok_dev // STRIPE
    run_size = devices * STRIPE
    prompt_total = token_of_row.shape[0] - cont_parent.shape[0] * CONT
    prompt_runs = prompt_total // run_size
    one_prompt = prompt_total == PROMPT
    assert prompt_runs * run_size == prompt_total
    group_rows = runs * HEADS * STRIPE
    head3 = 3 * HEAD_DIM
    block_columns = head3 + hidden

    by_device = token_of_row.reshape(devices, tok_dev)
    run_of = by_device // run_size
    big = jnp.int32(2**30)
    each_run = jnp.arange(runs, dtype=jnp.int32)
    base = jnp.min(jnp.where(run_of[:, :, None] == each_run, by_device[:, :, None], big), 1)
    mine = lax.dynamic_index_in_dim(by_device, me, 0, False)
    sorted_at = mine // run_size * STRIPE + mine % STRIPE
    pick = (sorted_at[None, :] == jnp.arange(tok_dev, dtype=jnp.int32)[:, None]).astype(BF)
    base_position = jnp.min(
        jnp.where((mine // run_size)[:, None] == each_run, position_ids[:, None], big), 0
    )

    def ordered(rows_in):
        return jnp.dot(pick, rows_in, preferred_element_type=F32).astype(BF)

    def restored(rows_in):
        return lax.dot_general(pick, rows_in, (((0,), (0,)), ((), ())), preferred_element_type=F32).astype(BF)

    states = ordered(inputs).astype(F32)
    grad_low = ordered(cotangent)
    grad_out = grad_low.astype(F32)
    average = jnp.mean(states, -1, keepdims=True)
    centered = states - average
    inverse_spread = lax.rsqrt(jnp.mean(centered * centered, -1, keepdims=True) + 1e-05)
    normed = centered * inverse_spread
    normed_low = normed.astype(BF)

    gain_one, shift_one = attn_norm_gain.astype(F32), attn_norm_bias.astype(F32)
    gain_two, shift_two = mlp_norm_gain.astype(F32), mlp_norm_bias.astype(F32)
    qkv_wide, expand_wide = qkv_weight.astype(F32), expand_weight.astype(F32)

    def split_qkv(values):
        return values.reshape(-1, 3, HEADS, HEAD_DIM).transpose(2, 0, 1, 3).reshape(HEADS, -1, head3)

    def split(values):
        return values.reshape(values.shape[0], HEADS, -1).transpose(1, 0, 2)

    weights = jnp.concatenate(
        [
            split_qkv((qkv_wide * gain_one[:, None]).astype(BF)),
            split((expand_wide * gain_two[:, None]).astype(BF)),
            split(dense_weight),
            split(shrink_weight),
        ],
        -1,
    )
    own_qkv_bias = lax.dynamic_update_slice_in_dim(
        jnp.zeros((3 * width,), F32), qkv_bias.astype(F32), me * qkv_bias.shape[0], 0
    )
    own_expand_bias = lax.dynamic_update_slice_in_dim(
        jnp.zeros((HEADS * hidden,), F32), expand_bias.astype(F32), me * expand_bias.shape[0], 0
    )
    bias_parts = jnp.concatenate(
        [
            split_qkv((jnp.sum(qkv_wide * shift_one[:, None], 0) + own_qkv_bias)[None])[:, 0],
            split((jnp.sum(expand_wide * shift_two[:, None], 0) + own_expand_bias)[None])[:, 0],
        ],
        -1,
    )
    lanes = 128
    note_rows = block_columns // lanes

    def padded(values):
        return jnp.pad(values, (0, lanes - values.shape[0]))

    tail = jnp.stack([padded(dense_bias.astype(F32) + shrink_bias.astype(F32)), padded(base_position.astype(F32))])
    notes = jnp.concatenate(
        [bias_parts.reshape(HEADS, note_rows, lanes), jnp.broadcast_to(tail[None], (HEADS, 2, lanes))], 1
    )

    n_all, g_all, w_all, m_all = gather_all(
        ways, normed_low.reshape(runs, STRIPE, width), grad_low.reshape(runs, STRIPE, width), weights, notes
    )
    n_all = n_all.reshape(group_rows, width)
    g_all = g_all.reshape(group_rows, width)
    w_all = w_all.reshape(width, block_columns + HEAD_DIM + hidden)
    bias_block = jnp.sum(m_all[..., :note_rows, :], (0, 1, 2, 3)).reshape(block_columns)
    out_bias = m_all[..., note_rows, :rows].reshape(width)
    group_position = lax.dynamic_index_in_dim(m_all[:, :, :, :, note_rows + 1, :runs], x, 0, False)
    group_position = lax.dynamic_index_in_dim(group_position, w, 0, False)
    group_position = lax.dynamic_index_in_dim(group_position, c, 1, False)
    within = jnp.arange(STRIPE, dtype=jnp.int32)
    position = (group_position.T[:, :, None] + within.astype(F32)).reshape(group_rows)
    angles = angles_of(position)
    cosine, sine = jnp.cos(angles), jnp.sin(angles)
    rows_run = group_rows // runs
    rest = ((0, 0), (0, 128 - ROT))
    tables = jnp.stack(
        [
            jnp.pad(jnp.concatenate([cosine, cosine], 1), rest, constant_values=1.0),
            jnp.pad(-sine, ((0, 0), (0, 128 - ROT // 2))),
            jnp.pad(sine, ((0, 0), (ROT // 2, 128 - ROT))),
        ]
    ).reshape(3, runs, rows_run, 128)

    w_in = w_all[:, :block_columns]
    w_out = w_all[:, block_columns:]
    mixed = jnp.dot(n_all, w_in[:, :head3], preferred_element_type=F32) + bias_block[:head3]
    queries = (rotate(mixed[:, :HEAD_DIM], cosine, sine) * (1.0 / math.sqrt(HEAD_DIM))).astype(BF)
    keys = rotate(mixed[:, HEAD_DIM : 2 * HEAD_DIM], cosine, sine).astype(BF)
    values = mixed[:, 2 * HEAD_DIM :].astype(BF)
    pairs = exchange(ways, jnp.concatenate([keys, values], 1).reshape(runs, rows_run, 2 * HEAD_DIM))
    pairs = pairs.reshape(runs, run_size, 2 * HEAD_DIM)

    d_attended = jnp.dot(g_all, w_out[:, :HEAD_DIM], preferred_element_type=F32).astype(BF)
    expanded = jnp.dot(n_all, w_in[:, head3:], preferred_element_type=F32) + bias_block[head3:]
    activated, gelu_back = jax.vjp(lambda v: jax.nn.gelu(v, approximate=False), expanded)
    activated = activated.astype(BF)
    d_activated = jnp.dot(g_all, w_out[:, HEAD_DIM:], preferred_element_type=F32)
    d_expanded = gelu_back(d_activated)[0].astype(BF)

    bases = base.reshape(2, ways, HEADS, 2, runs)
    own_base = lax.dynamic_index_in_dim(bases, x, 0, False)
    own_base = lax.dynamic_index_in_dim(own_base, w, 0, False)
    own_base = lax.dynamic_index_in_dim(own_base, c, 1, False)
    row_tokens = (own_base.T[:, :, None] + within).reshape(runs, rows_run)
    col_tokens = (bases.transpose(4, 1, 0, 3, 2)[..., None] + within).reshape(runs, run_size)

    def meta(tokens):
        is_prompt = tokens < prompt_total
        cont = (tokens - prompt_total) // CONT
        if one_prompt:
            prompt = jnp.zeros_like(tokens)
        else:
            matches = cont[..., None] == jnp.arange(cont_parent.shape[0], dtype=jnp.int32)
            prompt = jnp.where(is_prompt, tokens // PROMPT, jnp.sum(jnp.where(matches, cont_parent, 0), -1))
        segment = jnp.where(is_prompt, -1 - tokens // PROMPT, cont)
        return tokens, segment, prompt

    row_meta = jnp.stack(meta(row_tokens), -1)
    col_meta = jnp.stack(meta(col_tokens), 1)
    attended, d_queries, d_pairs = attention(
        prompt_runs, one_prompt,
        queries.reshape(runs, rows_run, HEAD_DIM), d_attended.reshape(runs, rows_run, HEAD_DIM),
        pairs, row_meta, col_meta, tables,
    )

    d_pairs = d_pairs.reshape(runs, ways, 4, rows_run, 2 * HEAD_DIM)
    if ways > 1:
        alike = [[w2 * 2 * HEADS + k for w2 in range(ways)] for k in range(2 * HEADS)]
        d_pairs = lax.psum_scatter(
            d_pairs.astype(F32), "blk", scatter_dimension=1, axis_index_groups=alike, tiled=True
        ).astype(BF)
    d_pairs = d_pairs[:, 0]
    own_sums = jnp.sum(grad_out, 0).reshape(width // lanes, lanes)
    sum_note = jnp.concatenate(
        [jnp.zeros((note_rows, lanes), F32), own_sums, jnp.zeros((-(note_rows + width // lanes) % 8, lanes), F32)]
    )
    out_sum, e_sum, owned_a, owned_b, owned_notes = finish(
        ways, rows, attended, activated, d_expanded, d_queries, d_pairs,
        tables, w_out, w_in, n_all, g_all, sum_note,
    )
    output = restored((states + out_sum.reshape(tok_dev, width) + out_bias).astype(BF))
    e_sum = e_sum.reshape(tok_dev, width)
    dx = inverse_spread * (
        e_sum - jnp.mean(e_sum, -1, keepdims=True) - normed * jnp.mean(e_sum * normed, -1, keepdims=True)
    )
    input_grad = restored((grad_out + dx).astype(BF))
    owned_a, owned_b = owned_a.astype(F32), owned_b.astype(F32)

    def join_qkv(values):
        return values.reshape(HEADS, -1, 3, HEAD_DIM).transpose(1, 2, 0, 3).reshape(-1, 3 * width)

    def join(values):
        return values.transpose(1, 0, 2).reshape(values.shape[1], -1)

    raw_qkv = join_qkv(owned_b)
    dense_grad = join(owned_a[..., :HEAD_DIM])
    shrink_grad = join(owned_a[..., HEAD_DIM : HEAD_DIM + hidden])
    raw_expand = join(owned_a[..., HEAD_DIM + hidden :])
    column_sums = owned_notes[:, :note_rows].reshape(HEADS, 1, block_columns)
    qkv_sum = join_qkv(column_sums[..., :head3])
    expand_sum = join(column_sums[..., head3:])
    all_sums = jnp.sum(owned_notes[:, note_rows : note_rows + width // lanes], 0).reshape(width)
    bias_grad = lax.dynamic_slice_in_dim(all_sums, me * rows, rows, 0)
    qkv_grad = gain_one[:, None] * raw_qkv + shift_one[:, None] * qkv_sum
    expand_grad = gain_two[:, None] * raw_expand + shift_two[:, None] * expand_sum

    def own(values, count):
        return lax.dynamic_slice_in_dim(values, me * count, count, 0)

    return (
        output,
        input_grad,
        jnp.sum(qkv_wide * raw_qkv, 1),
        jnp.sum(qkv_wide * qkv_sum, 1),
        jnp.sum(expand_wide * raw_expand, 1),
        jnp.sum(expand_wide * expand_sum, 1),
        qkv_grad,
        own(qkv_sum[0, : 2 * width], 2 * width // devices),
        own(qkv_sum[0, 2 * width :], width // devices),
        dense_grad,
        bias_grad,
        expand_grad,
        own(expand_sum[0], HEADS * hidden // devices),
        shrink_grad,
        bias_grad,
    )


def solution(mesh):
    matrix, vector = P(("head", "blk"), None), P(("head", "blk"))
    return jax.shard_map(
        per_device,
        mesh=mesh,
        in_specs=(
            matrix, vector, vector, vector, vector, matrix, vector, matrix, vector, matrix, vector, matrix, vector,
            P(), P(), vector, matrix,
        ),
        out_specs=(
            matrix, matrix, vector, vector, vector, vector, matrix, vector, vector, matrix, vector, matrix, vector,
            matrix, vector,
        ),
        check_vma=False,
    )
```

```python
import functools
import math

import jax
import jax.numpy as jnp
from jax import lax
from jax.experimental import pallas as pl
from jax.experimental.pallas import tpu as pltpu
from jax.sharding import PartitionSpec as P

HEADS = 8
HEAD_DIM = 256
ROT = 64
PROMPT = 2048
CONT = 256
STRIPE = 16
MESH = pl.DeviceIdType.MESH
BF = jnp.bfloat16
F32 = jnp.float32
ANY = pl.BlockSpec(memory_space=pl.ANY)
VMEM = pl.BlockSpec(memory_space=pltpu.VMEM)
DMA = pltpu.SemaphoreType.DMA


class Place:
    def __init__(self, ways):
        self.ways = ways
        self.x = lax.axis_index("head")
        b = lax.axis_index("blk")
        self.c = b % 2
        self.h = (b // 2) % HEADS
        self.w = b // (2 * HEADS)
        self.hy = self.h % 2
        self.hz = self.h // 2

    def device(self, x=None, w=None, h=None, c=None):
        x = self.x if x is None else x
        w = self.w if w is None else w
        h = self.h if h is None else h
        c = self.c if c is None else c
        return (x, w * (2 * HEADS) + h * 2 + c)

    def peers_h(self):
        return [self.device(h=(self.h + k) % HEADS) for k in range(1, HEADS)]

    def peers_w(self):
        return [self.device(w=(self.w + k) % self.ways) for k in range(1, self.ways)]

    def peer_x(self):
        return self.device(x=1 - self.x)

    def peer_c(self):
        return self.device(c=1 - self.c)

    def peer_y(self):
        return self.device(h=self.h + 1 - 2 * self.hy)


def greet(devices):
    barrier = pltpu.get_barrier_semaphore()
    for one in devices:
        pl.semaphore_signal(barrier, inc=1, device_id=one, device_id_type=MESH)
    pl.semaphore_wait(barrier, len(devices))


def remote(src, dst, send, recv, device):
    return pltpu.make_async_remote_copy(
        src_ref=src, dst_ref=dst, send_sem=send, recv_sem=recv, device_id=device, device_id_type=MESH
    )


def call(body, out_shape, ins, scratch, ident, out_spec=ANY, in_spec=ANY):
    return pl.pallas_call(
        body,
        out_shape=out_shape,
        in_specs=[in_spec] * len(ins),
        out_specs=jax.tree.map(lambda _: out_spec, out_shape),
        scratch_shapes=scratch,
        compiler_params=pltpu.CompilerParams(
            collective_id=ident, has_side_effects=True, vmem_limit_bytes=60 * 2**20
        ),
    )(*ins)


LINE = HEADS // 2


def relay_rows(place, own, full, s, r):
    hz, hy = place.hz, place.hy
    d0, d1 = hz % 2, hz // 2

    def index(e1, e0, y):
        return (e1 * 2 + e0) * 2 + y

    far = place.device(h=index(1 - d1, d0, hy))
    near = place.device(h=index(d1, 1 - d0, hy))
    side = place.peer_y()
    made = []

    def push(src, idx, k, device):
        copy = remote(src, full.at[:, idx], s.at[k], r.at[idx], device)
        copy.start()
        made.append(copy)

    def arrived(idx):
        remote(full.at[:, idx], full.at[:, idx], s.at[0], r.at[idx], side).wait_recv()

    def first():
        for k, device in enumerate((far, near, side)):
            push(own, place.h, k, device)

    def from_far():
        idx = index(1 - d1, d0, hy)
        arrived(idx)
        push(full.at[:, idx], idx, 3, near)
        push(full.at[:, idx], idx, 4, side)

    def from_near():
        idx = index(d1, 1 - d0, hy)
        arrived(idx)
        push(full.at[:, idx], idx, 5, side)

    def from_near_far():
        idx = index(1 - d1, 1 - d0, hy)
        arrived(idx)
        push(full.at[:, idx], idx, 6, side)

    def from_side():
        for z in range(LINE):
            arrived(z * 2 + 1 - hy)

    def sent():
        for copy in made:
            copy.wait_send()

    return first, from_far, from_near, from_near_far, from_side, sent


def gelu_slope(v):
    return 0.5 * (1.0 + lax.erf(v * math.sqrt(0.5))) + v * jnp.exp(-0.5 * v * v) * (1.0 / math.sqrt(2 * math.pi))


def open_kernel(ways, cuts, fuse, prompt_runs, prompt_total, *refs):
    names = ["n_in", "g_in", "w_in", "note_in", "trig_in", "step_in", "row_tok", "col_tok", "n_out", "g_out", "w_out", "note_out", "turn_out"]
    if fuse:
        names += ["att_out", "act_out", "dexp_out", "dq_out", "dkv_out"]
    names += ["v_n", "v_g", "v_w", "v_turn", "trig", "note", "note_c", "note_x", "note_w", "note_h", "own", "put"]
    names += ["ns", "nr", "gs", "gr", "wa", "wr", "xs", "xr", "cs", "cr", "t_s", "t_r", "nc_s", "nc_r", "nx_s", "nx_r", "nw_s", "nw_r", "nh_s", "nh_r"]
    if fuse:
        names += ["v_q", "v_do", "v_kv", "v_exp", "v_act", "v_dexp", "v_att", "v_dq", "v_dkv", "s_ref", "sum_ref", "kx_s", "kx_r", "kc_s", "kc_r"]
    at = dict(zip(names, refs, strict=True))
    (n_in, g_in, w_in, note_in, trig_in, step_in, n_out, g_out, w_out, note_out, turn_out, v_n, v_g, v_w, v_turn) = (
        at[k] for k in ["n_in", "g_in", "w_in", "note_in", "trig_in", "step_in", "n_out", "g_out", "w_out", "note_out", "turn_out", "v_n", "v_g", "v_w", "v_turn"]
    )
    trig, note, note_c, note_x, note_w, note_h, own, put = (
        at[k] for k in ["trig", "note", "note_c", "note_x", "note_w", "note_h", "own", "put"]
    )
    place = Place(ways)
    x, w, h, c = place.x, place.w, place.h, place.c
    runs = v_n.shape[0]
    width = v_n.shape[-1]
    per_run = HEADS * STRIPE
    stage_a = [(dw, dh) for dw in range(ways) for dh in range(HEADS) if (dw, dh) != (0, 0)]
    greet(
        [place.device(w=(w + dw) % ways, h=(h + dh) % HEADS) for dw, dh in stage_a]
        + [place.peer_x(), place.peer_c()]
    )
    sends, puts = [], []

    def send(src, dst, s, r, device):
        copy = remote(src, dst, s, r, device)
        copy.start()
        sends.append(copy)
        return copy

    def save(src, dst):
        copy = pltpu.make_async_copy(src, dst, put.at[len(puts)])
        copy.start()
        puts.append(copy)

    mine = [
        pltpu.make_async_copy(w_in.at[h], v_w.at[x, w, h, c], own.at[0]),
        pltpu.make_async_copy(n_in, v_n.at[:, h], own.at[1]),
        pltpu.make_async_copy(g_in, v_g.at[:, h], own.at[2]),
        pltpu.make_async_copy(trig_in, trig.at[h], own.at[3]),
        pltpu.make_async_copy(note_in, note, own.at[4]),
    ]
    for copy in (mine[4], mine[0], mine[3], mine[1], mine[2]):
        copy.start()
    n_first, n_far, n_near, n_last, n_side, n_sent = relay_rows(place, n_in, v_n, at["ns"], at["nr"])
    g_first, g_far, g_near, g_last, g_side, g_sent = relay_rows(place, g_in, v_g, at["gs"], at["gr"])
    wa, wr, xs, xr, cs, cr = (at[k] for k in ["wa", "wr", "xs", "xr", "cs", "cr"])

    def columns(g):
        return pl.ds(cuts[g][0], cuts[g][1])

    def w_first(g):
        for k, (dw, dh) in enumerate(stage_a):
            h2 = (h + dh) % HEADS
            send(w_in.at[h2, :, columns(g)], v_w.at[x, w, h, c, :, columns(g)], wa.at[g, k], wr.at[g, w, h],
                 place.device(w=(w + dw) % ways, h=h2))

    def w_across(g):
        for dw, dh in stage_a:
            ws, hs = (w - dw) % ways, (h - dh) % HEADS
            spot = v_w.at[x, ws, hs, c, :, columns(g)]
            remote(spot, spot, wa.at[g, 0], wr.at[g, ws, hs], place.peer_x()).wait_recv()
        block = v_w.at[x, :, :, c, :, columns(g)]
        send(block, block, xs.at[g], xr.at[g], place.peer_x())
        send(block, block, cs.at[g, 0], cr.at[g, 0], place.peer_c())

    def w_beside(g):
        block = v_w.at[1 - x, :, :, c, :, columns(g)]
        remote(block, block, xs.at[g], xr.at[g], place.peer_x()).wait_recv()
        send(block, block, cs.at[g, 1], cr.at[g, 1], place.peer_c())

    def w_ready(g):
        for k, xx in ((0, x), (1, 1 - x)):
            block = v_w.at[xx, :, :, 1 - c, :, columns(g)]
            remote(block, block, cs.at[g, k], cr.at[g, k], place.peer_c()).wait_recv()
        save(v_w.at[..., columns(g)], w_out.at[..., columns(g)])

    n_first()
    for k in range(1, HEADS):
        send(trig_in, trig.at[h], at["t_s"].at[k], at["t_r"].at[h], place.device(h=(h + k) % HEADS))
    mine[4].wait()
    send(note, note_c, at["nc_s"].at[0], at["nc_r"].at[0], place.peer_c())
    w_first(0)
    mine[0].wait()
    sends[HEADS - 1].wait_recv()
    note_c[...] = note_c[...] + note[...]
    copy = send(note_c, note_x, at["nx_s"].at[0], at["nx_r"].at[0], place.peer_x())
    n_far()
    n_near()
    copy.wait_recv()
    note_x[...] = note_x[...] + note_c[...]
    if ways > 1:
        crossed = [
            send(note_x, note_w.at[k], at["nw_s"].at[k], at["nw_r"].at[k], device)
            for k, device in enumerate(place.peers_w())
        ]
        for copy in crossed:
            copy.wait_recv()
        total = note_x[...]
        for k in range(ways - 1):
            total = total + note_w[k]
        note_c_sent = [one for one in sends if one.src_ref is note_c]
        for copy in note_c_sent:
            copy.wait_send()
        sends[:] = [one for one in sends if one.src_ref is not note_c]
        note_c[...] = total
        summed = note_c
    else:
        summed = note_x
    for k in range(1, HEADS):
        h2 = (h + k) % HEADS
        send(summed.at[h2], note_h.at[h], at["nh_s"].at[k], at["nh_r"].at[h], place.device(h=h2))
    n_last()
    w_across(0)
    w_first(1)

    mine[3].wait()
    for k in range(1, HEADS):
        hs = (h - k) % HEADS
        remote(trig.at[hs], trig.at[hs], at["t_s"].at[k], at["t_r"].at[hs], place.peer_x()).wait_recv()
    lane = lax.broadcasted_iota(jnp.int32, (STRIPE, 128), 1)
    for hh in range(HEADS):
        @pl.loop(0, runs)
        def _(run):
            cosine, sine = trig[hh, 0, pl.ds(run, 1)], trig[hh, 1, pl.ds(run, 1)]
            full = sine * step_in[0] + cosine * step_in[1]
            here = pl.ds(hh * STRIPE, STRIPE)
            v_turn[0, run, here] = cosine * step_in[0] - sine * step_in[1]
            v_turn[1, run, here] = jnp.where(lane < ROT // 2, -full, 0.0)
            v_turn[2, run, here] = jnp.where(lane < ROT // 2, 0.0, full)
    save(v_turn, turn_out)
    w_beside(0)
    g_first()
    w_first(2)
    bias = summed[h]
    for k in range(1, HEADS):
        hs = (h - k) % HEADS
        remote(note_h.at[hs], note_h.at[hs], at["nh_s"].at[k], at["nh_r"].at[hs], place.peer_x()).wait_recv()
        bias = bias + note_h[hs]
    note_h[h] = bias
    save(note_h.at[h], note_out)
    mine[1].wait()
    n_side()
    save(v_n, n_out)
    w_ready(0)

    shrink = list(range(3, len(cuts)))
    if not fuse:
        g_far()
        w_across(1)
        for g in shrink:
            w_first(g)
        g_near()
        g_last()
        w_beside(1)
        w_ready(1)
        w_across(2)
        w_beside(2)
        for g in shrink:
            w_across(g)
        mine[2].wait()
        g_side()
        save(v_g, g_out)
        w_ready(2)
        for g in shrink:
            w_beside(g)
            w_ready(g)
    else:
        v_q, v_do, v_kv, v_exp, v_act, v_dexp, v_att, v_dq, v_dkv, s_ref, sum_ref, kx_s, kx_r, kc_s, kc_r = (
            at[k] for k in ["v_q", "v_do", "v_kv", "v_exp", "v_act", "v_dexp", "v_att", "v_dq", "v_dkv", "s_ref", "sum_ref", "kx_s", "kx_r", "kc_s", "kc_r"]
        )
        tile = 256

        def weight(first):
            return v_w[..., first : first + tile].reshape(width, tile)

        def bias_of(t):
            return jnp.concatenate([note_h[h, 2 * t : 2 * t + 1], note_h[h, 2 * t + 1 : 2 * t + 2]], 1)

        parts = 4
        span = runs // parts
        slot = x * 2 + c

        def project(p):
            lo = p * span
            left = v_n[lo : lo + span].reshape(span * per_run, width)
            tables = [v_turn[t, lo : lo + span].reshape(span * per_run, 128) for t in range(3)]
            for t in range(3):
                value = jnp.dot(left, weight(t * HEAD_DIM), preferred_element_type=F32) + bias_of(t)
                if t < 2:
                    value = turn(value, tables, 1.0)
                if t == 0:
                    v_q[lo : lo + span] = (value * (1.0 / math.sqrt(HEAD_DIM))).astype(BF).reshape(span, per_run, HEAD_DIM)
                else:
                    here = pl.ds((t - 1) * HEAD_DIM, HEAD_DIM)
                    v_kv[lo : lo + span, slot, :, here] = value.astype(BF).reshape(span, per_run, HEAD_DIM)
            block = v_kv.at[lo : lo + span, slot]
            send(block, block, kx_s.at[p], kx_r.at[p], place.peer_x())
            send(block, block, kc_s.at[0, p], kc_r.at[0, p], place.peer_c())

        def kv_beside(p):
            block = v_kv.at[pl.ds(p * span, span), (1 - x) * 2 + c]
            remote(block, block, kx_s.at[p], kx_r.at[p], place.peer_x()).wait_recv()
            send(block, block, kc_s.at[1, p], kc_r.at[1, p], place.peer_c())

        def kv_ready(p):
            for k, xx in ((0, x), (1, 1 - x)):
                block = v_kv.at[pl.ds(p * span, span), xx * 2 + 1 - c]
                remote(block, block, kc_s.at[k, p], kc_r.at[k, p], place.peer_c()).wait_recv()

        half = runs * per_run // 2

        def expand(m, t):
            left = v_n[m * runs // 2 : (m + 1) * runs // 2].reshape(half, width)
            value = jnp.dot(left, weight(cuts[1][0] + t * tile), preferred_element_type=F32) + bias_of(3 + t)
            v_exp[m * half : (m + 1) * half, t * tile : (t + 1) * tile] = value
            active = 0.5 * value * (1.0 + lax.erf(value * math.sqrt(0.5)))
            v_act[m * half : (m + 1) * half, t * tile : (t + 1) * tile] = active.astype(BF)

        def shrink_back(m, t):
            left = v_g[m * runs // 2 : (m + 1) * runs // 2].reshape(half, width)
            value = jnp.dot(left, weight(cuts[3][0] + t * tile), preferred_element_type=F32)
            slope = gelu_slope(v_exp[m * half : (m + 1) * half, t * tile : (t + 1) * tile])
            v_dexp[m * half : (m + 1) * half, t * tile : (t + 1) * tile] = (value * slope).astype(BF)

        for p in range(parts):
            project(p)
        g_far()
        w_across(1)
        for g in shrink:
            w_first(g)
        g_near()
        for p in range(parts):
            kv_beside(p)
        g_last()
        w_beside(1)
        for p in range(parts):
            kv_ready(p)
        w_ready(1)
        w_across(2)
        for t in range(v_act.shape[1] // tile):
            for m in range(2):
                expand(m, t)
            if t == 0:
                w_beside(2)
        save(v_act, at["act_out"])
        mine[2].wait()
        g_side()
        save(v_g, g_out)
        w_ready(2)
        for m in range(2):
            left = v_g[m * runs // 2 : (m + 1) * runs // 2].reshape(half, width)
            value = jnp.dot(left, weight(cuts[2][0]), preferred_element_type=F32)
            v_do[m * runs // 2 : (m + 1) * runs // 2] = value.astype(BF).reshape(runs // 2, per_run, HEAD_DIM)

        row_tok, col_tok = at["row_tok"], at["col_tok"]

        def segment(tokens):
            return jnp.where(tokens < prompt_total, -1 - tokens // PROMPT, (tokens - prompt_total) // CONT)

        def mask(i, k):
            if i != k:
                return None
            rows, cols = row_tok[i], col_tok[k]
            return (segment(rows) == segment(cols)) & (cols <= rows)

        for i in range(runs):
            attention_step(
                i, prompt_runs, mask, v_q, v_do, lambda k: v_kv[k, :, :, :HEAD_DIM].reshape(4 * per_run, HEAD_DIM),
                lambda k: v_kv[k, :, :, HEAD_DIM:].reshape(4 * per_run, HEAD_DIM), v_turn, v_att, v_dq, s_ref, sum_ref,
            )
            if i < len(shrink):
                w_across(shrink[i])
            elif i < 2 * len(shrink):
                w_beside(shrink[i - len(shrink)])
        v_dkv[...] = sum_ref[...].astype(BF).reshape(v_dkv.shape)
        save(v_att, at["att_out"])
        save(v_dq, at["dq_out"])
        save(v_dkv, at["dkv_out"])
        for t, g in enumerate(shrink):
            w_ready(g)
            for m in range(2):
                shrink_back(m, t)
        save(v_dexp, at["dexp_out"])
    for copy in puts:
        copy.wait()
    for copy in sends:
        copy.wait_send()
    n_sent()
    g_sent()


def open_all(ways, rows, hidden, prompt_runs, prompt_total, normed, grads, weights, notes, trig, steps, row_tok, col_tok):
    runs, _, width = normed.shape
    columns = weights.shape[2]
    fuse = ways == 1 and prompt_total == PROMPT
    head3 = 3 * HEAD_DIM
    cuts = [(0, head3), (head3, hidden), (head3 + hidden, HEAD_DIM)]
    cuts += [(head3 + hidden + HEAD_DIM + k * 256, 256) for k in range(hidden // 256)]
    blocks = (2, ways, HEADS, 2, rows, columns)
    group = runs * HEADS * STRIPE
    per_run = HEADS * STRIPE

    def shape(dims, kind=BF):
        return jax.ShapeDtypeStruct(dims, kind)

    gathered = (runs, HEADS, STRIPE, width)
    tables = (3, runs, per_run, 128)
    outs = [shape(gathered), shape(gathered), shape(blocks), shape(notes.shape[1:], F32), shape(tables, F32)]
    if fuse:
        outs += [
            shape((runs, per_run, HEAD_DIM)), shape((group, hidden)), shape((group, hidden)),
            shape((runs, per_run, HEAD_DIM)), shape((runs, 4, per_run, 2 * HEAD_DIM)),
        ]
    extra = max(ways - 1, 1)
    count = len(cuts)
    scratch = [
        pltpu.VMEM(gathered, BF), pltpu.VMEM(gathered, BF), pltpu.VMEM(blocks, BF), pltpu.VMEM(tables, F32),
        pltpu.VMEM((HEADS,) + trig.shape, F32),
        pltpu.VMEM(notes.shape, F32), pltpu.VMEM(notes.shape, F32), pltpu.VMEM(notes.shape, F32),
        pltpu.VMEM((extra,) + notes.shape, F32), pltpu.VMEM(notes.shape, F32),
        DMA((5,)), DMA((count + 10,)),
        DMA((7,)), DMA((HEADS,)), DMA((7,)), DMA((HEADS,)),
        DMA((count, ways * HEADS)), DMA((count, ways, HEADS)), DMA((count,)), DMA((count,)), DMA((count, 2)), DMA((count, 2)),
        DMA((HEADS,)), DMA((HEADS,)), DMA((1,)), DMA((1,)), DMA((1,)), DMA((1,)), DMA((extra,)), DMA((extra,)),
        DMA((HEADS,)), DMA((HEADS,)),
    ]
    if fuse:
        scratch += [
            pltpu.VMEM((runs, per_run, HEAD_DIM), BF), pltpu.VMEM((runs, per_run, HEAD_DIM), BF),
            pltpu.VMEM((runs, 4, per_run, 2 * HEAD_DIM), BF), pltpu.VMEM((group, hidden), F32),
            pltpu.VMEM((group, hidden), BF), pltpu.VMEM((group, hidden), BF),
            pltpu.VMEM((runs, per_run, HEAD_DIM), BF), pltpu.VMEM((runs, per_run, HEAD_DIM), BF),
            pltpu.VMEM((runs, 4, per_run, 2 * HEAD_DIM), BF),
            pltpu.VMEM((per_run, (prompt_runs + 1) * 4 * per_run), F32),
            pltpu.VMEM((runs, 4 * per_run, 2 * HEAD_DIM), F32),
            DMA((4,)), DMA((4,)), DMA((2, 4)), DMA((2, 4)),
        ]
    return fuse, pl.pallas_call(
        functools.partial(open_kernel, ways, tuple(cuts), fuse, prompt_runs, prompt_total),
        out_shape=tuple(outs),
        in_specs=[ANY] * 5 + [VMEM] * 3,
        out_specs=(ANY,) * len(outs),
        scratch_shapes=scratch,
        compiler_params=pltpu.CompilerParams(collective_id=0, has_side_effects=True, vmem_limit_bytes=62 * 2**20),
    )(normed, grads, weights, notes, trig, steps, row_tok, col_tok)


def exchange_kernel(ways, own, full, local, to_w, to_x, to_c, recv):
    place = Place(ways)
    x, w, c = place.x, place.w, place.c
    runs = own.shape[0]
    parts = 4
    span = runs // parts
    greet(place.peers_w() + [place.peer_x(), place.peer_c()])

    def spot(ws, xs, cs, p):
        return full.at[pl.ds(p * span, span), ws * 4 + xs * 2 + cs]

    sends = []

    def send(src, ws, xs, cs, p, sem, device):
        copy = remote(src, spot(ws, xs, cs, p), sem, recv.at[ws, xs, cs, p], device)
        copy.start()
        sends.append(copy)

    def arrived(ws, xs, cs, p):
        remote(spot(ws, xs, cs, p), spot(ws, xs, cs, p), local.at[0], recv.at[ws, xs, cs, p], place.peer_x()).wait_recv()

    keep = pltpu.make_async_copy(own, full.at[:, w * 4 + x * 2 + c], local.at[0])
    for p in range(parts):
        src = own.at[pl.ds(p * span, span)]
        for k, device in enumerate(place.peers_w()):
            send(src, w, x, c, p, to_w.at[k, p], device)
        send(src, w, x, c, p, to_x.at[w, p], place.peer_x())
    for p in range(parts):
        send(own.at[pl.ds(p * span, span)], w, x, c, p, to_c.at[w, x, p], place.peer_c())
    keep.start()
    for k in range(1, ways):
        ws = (w - k) % ways
        for p in range(parts):
            arrived(ws, x, c, p)
            send(spot(ws, x, c, p), ws, x, c, p, to_x.at[ws, p], place.peer_x())
            send(spot(ws, x, c, p), ws, x, c, p, to_c.at[ws, x, p], place.peer_c())
    for k in range(ways):
        ws = (w - k) % ways
        for p in range(parts):
            arrived(ws, 1 - x, c, p)
            send(spot(ws, 1 - x, c, p), ws, 1 - x, c, p, to_c.at[ws, 1 - x, p], place.peer_c())
    for k in range(ways):
        ws = (w - k) % ways
        for p in range(parts):
            arrived(ws, x, 1 - c, p)
            arrived(ws, 1 - x, 1 - c, p)
    keep.wait()
    for copy in sends:
        copy.wait_send()


def exchange(ways, own):
    runs, rows, columns = own.shape
    return call(
        functools.partial(exchange_kernel, ways),
        jax.ShapeDtypeStruct((runs, 4 * ways, rows, columns), BF),
        (own,),
        [DMA((1,)), DMA((ways, 4)), DMA((ways, 4)), DMA((ways, 2, 4)), DMA((ways, 2, 2, 4))],
        1,
    )


def turn(u, tables, sign):
    cosine, lower, upper = tables
    front = u[:, :128]
    moved = pltpu.roll(front, 96, 1) * lower + pltpu.roll(front, 32, 1) * upper
    return jnp.concatenate([front * cosine + moved * sign, u[:, 128:]], 1)


def finish_kernel(ways, att, act, dexp, dq, dkv, tables, w_all, n_all, g_all, note,
                  out_sum, e_sum, own_a, own_b, note_all,
                  v_left, v_right, v_w, v_turn, kv_own, kv_c, kv_x,
                  o_p, o_y, o_1, o_2, e_p, e_y, e_1, e_2,
                  raw, flat, ring, a_c, a_x, a_w, b_c, b_x, b_w, n_mine, n_c, n_x, n_w,
                  load, load_raw, kv_load, kv_s, kv_r, kvx_s, kvx_r,
                  oy_s, oy_r, o1_s, o1_r, o2_s, o2_r, ey_s, ey_r, e1_s, e1_r, e2_s, e2_r,
                  ac_s, ac_r, ax_s, ax_r, aw_s, aw_r, ah_s, ah_r,
                  bc_s, bc_r, bx_s, bx_r, bw_s, bw_r, bh_s, bh_r, keep, n_s, n_r):
    place = Place(ways)
    x, w, h, c, hy, hz = place.x, place.w, place.h, place.c, place.hy, place.hz
    d0, d1 = hz % 2, hz // 2
    runs = v_left.shape[0]
    chunks = o_p.shape[0]
    wide = o_p.shape[-1]
    rows = own_a.shape[1]
    hp = 256 // (2 * rows)
    tiles = HEADS // hp
    a_cols, b_cols = own_a.shape[2], own_b.shape[2]
    inner = v_left.shape[-1]
    head3 = 3 * HEAD_DIM
    group = runs * HEADS * STRIPE
    sends = []

    def send(src, dst, s, r, device):
        copy = remote(src, dst, s, r, device)
        copy.start()
        sends.append(copy)
        return copy

    greet(place.peers_h() + place.peers_w() + [place.peer_x(), place.peer_c()])

    def fetch(src, dst, k):
        copy = pltpu.make_async_copy(src, dst, load.at[k])
        copy.start()
        return copy

    early = [
        fetch(att, v_left.at[..., :HEAD_DIM], 0),
        fetch(act, v_left.at[..., HEAD_DIM:], 1),
        fetch(w_all.at[:, pl.ds(v_right.shape[-1], inner)], v_w.at[:, :inner], 2),
    ]

    kv_first, kv_mine = [], []
    for k, xs in ((0, 1 - x), (1, x)):
        kv_first.append(send(dkv.at[:, xs * 2 + 1 - c], kv_c.at[:, k], kv_s.at[k], kv_r.at[k], place.peer_c()))
        kv_mine.append(pltpu.make_async_copy(dkv.at[:, xs * 2 + c], kv_own.at[:, k], kv_load.at[k]))
        kv_mine[k].start()
    late = [
        fetch(dexp, v_right.at[..., head3:], 3),
        fetch(dq, v_right.at[..., :HEAD_DIM], 4),
        fetch(tables, v_turn, 5),
    ]

    def partial(src, q, buf, depth):
        @pl.loop(0, wide // 256)
        def _(k):
            at = pl.multiple_of(k * 256, 256)
            value = lax.dot_general(
                src[...].reshape(group, depth),
                v_w[pl.ds(pl.multiple_of(q * wide + at, 256), 256), :depth],
                (((1,), (1,)), ((), ())),
                preferred_element_type=F32,
            )
            buf[q, :, :, :, :, :, pl.ds(at, 256)] = value.astype(BF).reshape(runs, 2, 2, 2, STRIPE, 256)

    def sums(buf, y, one, two, s_y, r_y, s_1, r_1, s_2, r_2, total):
        def start(q):
            return send(buf.at[q, :, :, :, 1 - hy], y.at[q], s_y.at[q], r_y.at[q], place.peer_y())

        def after_y(q, copy):
            copy.wait_recv()

            @pl.loop(0, runs)
            def _(run):
                for t in range(LINE):
                    value = y[q, run, t // 2, t % 2].astype(F32) + buf[q, run, t // 2, t % 2, hy].astype(F32)
                    y[q, run, t // 2, t % 2] = value.astype(BF)

            target = place.device(h=(hz + 1 - 2 * d0) * 2 + hy)
            return send(y.at[q, :, :, 1 - d0], one.at[q], s_1.at[q], r_1.at[q], target)

        def after_1(q, copy):
            copy.wait_recv()

            @pl.loop(0, runs)
            def _(run):
                for t in range(2):
                    value = one[q, run, t].astype(F32) + y[q, run, t, d0].astype(F32)
                    one[q, run, t] = value.astype(BF)

            target = place.device(h=((1 - d1) * 2 + d0) * 2 + hy)
            return send(one.at[q, :, 1 - d1], two.at[q], s_2.at[q], r_2.at[q], target)

        def after_2(q, copy):
            copy.wait_recv()

            @pl.loop(0, runs)
            def _(run):
                total[run, :, q * wide : (q + 1) * wide] = two[q, run].astype(F32) + one[q, run, d1].astype(F32)

        return start, after_y, after_1, after_2

    o_start, o_after_y, o_after_1, o_after_2 = sums(o_p, o_y, o_1, o_2, oy_s, oy_r, o1_s, o1_r, o2_s, o2_r, out_sum)
    e_start, e_after_y, e_after_1, e_after_2 = sums(e_p, e_y, e_1, e_2, ey_s, ey_r, e1_s, e1_r, e2_s, e2_r, e_sum)

    for copy in early:
        copy.wait()
    o_step = {}
    for q in range(chunks):
        partial(v_left, q, o_p, inner)
        o_step[q] = o_start(q)
    w_load = fetch(w_all.at[:, pl.ds(0, v_right.shape[-1])], v_w, 6)

    def kv_add(k, final):
        kv_mine[k].wait()
        kv_first[k].wait_recv()

        @pl.loop(0, runs)
        def _(run):
            value = kv_own[run, k].astype(F32) + kv_c[run, k].astype(F32)
            if final:
                value = value + kv_x[run].astype(F32)
                back = turn(value[:, :HEAD_DIM].astype(BF).astype(F32), [v_turn[t, run] for t in range(3)], -1.0)
                shape = (LINE, 2, STRIPE, HEAD_DIM)
                v_right[run, :, :, :, HEAD_DIM : 2 * HEAD_DIM] = back.astype(BF).reshape(shape)
                v_right[run, :, :, :, 2 * HEAD_DIM : head3] = value[:, HEAD_DIM:].astype(BF).reshape(shape)
            else:
                kv_c[run, k] = value.astype(BF)

    kv_add(0, False)
    kv_second = remote(kv_c.at[:, 0], kv_x, kvx_s.at[0], kvx_r.at[0], place.peer_x())
    kv_second.start()
    for copy in late:
        copy.wait()

    order_t = [(k, dw, dt) for k in range(2) for dw in list(range(1, ways)) + [0] for dt in list(range(1, tiles)) + [0]]
    own_t = h // hp

    def where(k, dw, dt):
        return (1 - x if k == 0 else x), (w + dw) % ways, (own_t + dt) % tiles

    def raw_copy(n, src, buf):
        xs, ws, t = where(*order_t[n])
        at = pl.multiple_of(((xs * ways + ws) * tiles + t) * 256, 256)
        return pltpu.make_async_copy(src.at[:, pl.ds(at, 256)], raw.at[n % 2, buf], load_raw.at[n % 2, buf])

    def product(n, buf, src, first, count, at):
        flat[...] = raw[n % 2, buf].T

        @pl.loop(0, count // 256)
        def _(k):
            col = pl.multiple_of(k * 256, 256)
            value = jnp.dot(
                flat[...], src[..., pl.ds(first + col, 256)].reshape(group, 256), preferred_element_type=F32
            )
            ring[n % 3, :, :, :, pl.ds(at + col, 256)] = value.astype(BF).reshape(hp, 2, rows, 256)

    def grads(cols, from_c, from_x, from_w, c_s, c_r, x_s, x_r, w_s, w_r, h_s, h_r, out, fill, need, flag):
        first, second, third, last = {}, {}, {}, []

        def begin(n):
            for buf, src in need:
                raw_copy(n, src, buf).start()

        def make(n):
            if n >= 3:
                first[n - 3].wait_send()
            for buf, src in need:
                raw_copy(n, src, buf).wait()
            fill(n)
            if n + 1 < len(order_t):
                begin(n + 1)
            k, dw, dt = order_t[n]
            first[n] = remote(
                ring.at[n % 3, :, 1 - c, :, pl.ds(0, cols)], from_c.at[k, dw, dt], c_s.at[n], c_r.at[n], place.peer_c()
            )
            first[n].start()

        def mine(n):
            k, dw, dt = order_t[n]
            first[n].wait_recv()

            @pl.loop(0, hp)
            def _(q):
                value = from_c[k, dw, dt, q].astype(F32) + ring[n % 3, q, c, :, :cols].astype(F32)
                from_c[k, dw, dt, q] = value.astype(BF)

        def cross(n):
            k, dw, dt = order_t[n]
            second[dw, dt] = send(from_c.at[0, dw, dt], from_x.at[dw, dt], x_s.at[dw, dt], x_r.at[dw, dt], place.peer_x())

        def close(n):
            k, dw, dt = order_t[n]
            _, ws, t = where(k, dw, dt)
            second[dw, dt].wait_recv()
            more = [from_x.at[dw, dt]]
            if dw == 0:
                for dv in range(1, ways):
                    third[dv, dt].wait_recv()
                    more.append(from_w.at[dv - 1, dt])

            @pl.loop(0, hp)
            def _(q):
                value = from_c[1, dw, dt, q].astype(F32)
                for ref in more:
                    value = value + ref[q].astype(F32)
                from_c[1, dw, dt, q] = value.astype(BF)

            if dw != 0:
                third[dw, dt] = send(from_c.at[1, dw, dt], from_w.at[dw - 1, dt], w_s.at[dw - 1, dt], w_r.at[dw - 1, dt], place.device(w=ws))
                return
            for q in range(hp):
                hs = t * hp + q
                at = dt * hp + q

                @pl.when(hs != h)
                def _():
                    remote(from_c.at[1, 0, dt, q], out.at[h], h_s.at[at], h_r.at[h], place.device(h=hs)).start()

                @pl.when(hs == h)
                def _():
                    pltpu.make_async_copy(from_c.at[1, 0, dt, q], out.at[h], keep.at[flag]).start()

        def drain():
            for n in range(max(len(order_t) - 3, 0), len(order_t)):
                first[n].wait_send()

        def end():
            for n in range(len(order_t)):
                k, dw, dt = order_t[n]
                if k == 1 and dw == 0:
                    _, _, t = where(k, dw, dt)
                    for q in range(hp):
                        hs = t * hp + q

                        @pl.when(hs != h)
                        def _():
                            remote(from_c.at[1, 0, dt, q], out.at[h], h_s.at[dt * hp + q], h_r.at[h], place.device(h=hs)).wait_send()
            for dh in range(1, HEADS):
                hs = (h + dh) % HEADS
                remote(out.at[hs], out.at[hs], h_s.at[0], h_r.at[hs], place.peer_x()).wait_recv()
            pltpu.make_async_copy(from_c.at[1, 0, 0, 0], out.at[h], keep.at[flag]).wait()

        return begin, make, mine, cross, close, drain, end

    def fill_a(n):
        product(n, 1, v_left, 0, inner, 0)
        product(n, 0, v_right, head3, a_cols - inner, inner)

    def fill_b(n):
        product(n, 0, v_right, 0, head3, 0)

    a_begin, a_make, a_mine, a_cross, a_close, a_drain, a_end = grads(
        a_cols, a_c, a_x, a_w, ac_s, ac_r, ax_s, ax_r, aw_s, aw_r, ah_s, ah_r, own_a, fill_a, ((0, n_all), (1, g_all)), 0
    )
    b_begin, b_make, b_mine, b_cross, b_close, b_drain, b_end = grads(
        b_cols, b_c, b_x, b_w, bc_s, bc_r, bx_s, bx_r, bw_s, bw_r, bh_s, bh_r, own_b, fill_b, ((0, n_all),), 1
    )
    count = len(order_t)
    half = count // 2
    a_begin(0)
    for n in range(half):
        a_make(n)
        a_mine(n)
        if n == 0:
            kv_second.wait_send()
        a_cross(n)
        if n == 1:
            o_step[0] = o_after_y(0, o_step[0])
    o_step[1] = o_after_y(1, o_step[1])
    o_step[0] = o_after_1(0, o_step[0])

    kv_second.wait_recv()
    kv_add(1, True)
    w_load.wait()
    e_step = {}
    for q in range(chunks):
        partial(v_right, q, e_p, v_right.shape[-1])
        e_step[q] = e_start(q)
        if q == 1:
            o_step[2] = o_after_y(2, o_step[2])
            o_step[1] = o_after_1(1, o_step[1])
    o_after_2(0, o_step[0])

    def fold_columns(first, cols, row):
        @pl.loop(0, cols // 128)
        def _(k):
            at = pl.multiple_of(k * 128, 128)
            value = v_right[..., pl.ds(first + at, 128)].reshape(group, 128).astype(F32)
            n_mine[pl.ds(row + k, 1), :] = jnp.sum(value, 0, keepdims=True)

    n_load = pltpu.make_async_copy(note, n_mine, keep.at[2])
    n_load.start()
    n_load.wait()
    fold_columns(0, v_right.shape[-1], 0)
    note_copy = send(n_mine, n_c, n_s.at[0], n_r.at[0], place.peer_c())

    note_w = []
    for n in range(half, count):
        a_make(n)
        a_mine(n)
        if n == half:
            note_copy.wait_recv()
            n_c[...] = n_c[...] + n_mine[...]
            note_copy = send(n_c, n_x, n_s.at[1], n_r.at[1], place.peer_x())
        a_close(n)
        if n == half + 1:
            note_copy.wait_recv()
            n_x[...] = n_x[...] + n_c[...]
            for k, device in enumerate(place.peers_w()):
                note_w.append(send(n_x, n_w.at[k], n_s.at[2 + k], n_r.at[2 + k], device))
            o_step[3] = o_after_y(3, o_step[3])
            o_step[2] = o_after_1(2, o_step[2])
    o_after_2(1, o_step[1])
    o_step[3] = o_after_1(3, o_step[3])
    for k, copy in enumerate(note_w):
        copy.wait()
    total = n_x[...]
    for k in range(ways - 1):
        total = total + n_w[k]
    n_x[...] = total
    base = 1 + ways
    for dh in range(1, HEADS):
        send(n_x, note_all.at[h], n_s.at[base + dh], n_r.at[base + h], place.device(h=(h + dh) % HEADS))
    n_keep = pltpu.make_async_copy(n_x, note_all.at[h], keep.at[3])
    n_keep.start()

    a_drain()
    b_begin(0)
    for n in range(half):
        b_make(n)
        b_mine(n)
        b_cross(n)
        if n == 0:
            e_step[0] = e_after_y(0, e_step[0])
        if n == 1:
            o_after_2(2, o_step[2])
    e_step[1] = e_after_y(1, e_step[1])
    e_step[0] = e_after_1(0, e_step[0])
    o_after_2(3, o_step[3])
    for n in range(half, count):
        b_make(n)
        b_mine(n)
    e_step[2] = e_after_y(2, e_step[2])
    e_step[1] = e_after_1(1, e_step[1])
    e_after_2(0, e_step[0])
    for n in range(half, count):
        b_close(n)
    e_step[3] = e_after_y(3, e_step[3])
    e_step[2] = e_after_1(2, e_step[2])
    e_after_2(1, e_step[1])
    e_step[3] = e_after_1(3, e_step[3])
    e_after_2(2, e_step[2])
    e_after_2(3, e_step[3])
    a_end()
    b_drain()
    b_end()
    n_keep.wait()
    for dh in range(1, HEADS):
        hs = (h + dh) % HEADS
        remote(note_all.at[hs], note_all.at[hs], n_s.at[0], n_r.at[base + hs], place.peer_x()).wait_recv()
    for copy in sends:
        if not any(copy is other for other in note_w):
            copy.wait_send()


def finish(ways, rows, att, act, dexp, dq, dkv, tables, w_all, n_all, g_all, note):
    width = w_all.shape[0]
    inner = att.shape[-1] + act.shape[-1]
    right = w_all.shape[1] - inner
    head3 = 3 * HEAD_DIM
    a_cols, b_cols = inner + right - head3, head3
    group = n_all.shape[0]
    runs, _, per_run, pair = dkv.shape
    lines = (runs, LINE, 2, STRIPE)
    hp = 256 // (2 * rows)
    tiles = HEADS // hp
    chunks, wide = 4, width // 4
    extra = max(ways - 1, 1)
    count = 2 * ways * tiles

    def vm(shape, kind=BF):
        return pltpu.VMEM(shape, kind)

    def row_buffers():
        return [
            vm((chunks, runs, 2, 2, 2, STRIPE, wide)),
            vm((chunks, runs, 2, 2, STRIPE, wide)),
            vm((chunks, runs, 2, STRIPE, wide)),
            vm((chunks, runs, STRIPE, wide)),
        ]

    def spare(shape):
        return shape if ways > 1 else (1,) * (len(shape) - 2) + (16, 128)

    def gradient_buffers(cols):
        return [
            vm((2, ways, tiles, hp, rows, cols)),
            vm((ways, tiles, hp, rows, cols)),
            vm(spare((extra, tiles, hp, rows, cols))),
        ]

    def gradient_sems():
        return [
            DMA((count,)), DMA((count,)), DMA((ways, tiles)), DMA((ways, tiles)), DMA((extra, tiles)), DMA((extra, tiles)),
            DMA((HEADS,)), DMA((HEADS,)),
        ]

    scratch = (
        [
            vm(lines + (inner,)), vm(lines + (right,)), vm((width, right)), vm(tables.shape, F32),
            vm((runs, 2, per_run, pair)), vm((runs, 2, per_run, pair)), vm((runs, per_run, pair)),
        ]
        + row_buffers() + row_buffers()
        + [vm((2, 2, group, 256)), vm((256, group)), vm((3, hp, 2, rows, a_cols))]
        + gradient_buffers(a_cols) + gradient_buffers(b_cols)
        + [vm(note.shape, F32)] * 3 + [vm((extra,) + note.shape, F32)]
        + [DMA((7,)), DMA((2, 2)), DMA((2,)), DMA((2,)), DMA((2,)), DMA((1,)), DMA((1,))]
        + [DMA((chunks,))] * 12
        + gradient_sems() + gradient_sems()
        + [DMA((4,)), DMA((1 + ways + HEADS,)), DMA((1 + ways + HEADS,))]
    )
    shapes = (
        jax.ShapeDtypeStruct((runs, STRIPE, width), F32),
        jax.ShapeDtypeStruct((runs, STRIPE, width), F32),
        jax.ShapeDtypeStruct((HEADS, rows, a_cols), BF),
        jax.ShapeDtypeStruct((HEADS, rows, b_cols), BF),
        jax.ShapeDtypeStruct((HEADS,) + note.shape, F32),
    )
    ins = (
        att.reshape(lines + (HEAD_DIM,)), act.reshape(lines + (inner - HEAD_DIM,)), dexp.reshape(lines + (right - head3,)),
        dq.reshape(lines + (HEAD_DIM,)), dkv, tables, w_all, n_all, g_all, note,
    )
    return pl.pallas_call(
        functools.partial(finish_kernel, ways),
        out_shape=shapes,
        in_specs=[ANY] * len(ins),
        out_specs=(VMEM, VMEM, ANY, ANY, ANY),
        scratch_shapes=scratch,
        compiler_params=pltpu.CompilerParams(collective_id=2, has_side_effects=True, vmem_limit_bytes=62 * 2**20),
    )(*ins)


def attention_step(i, prompt_runs, mask, q_ref, do_ref, key, value_of, turn_ref, o_ref, dq_ref, s_ref, sum_ref):
    m = q_ref.shape[1]
    keys = sum_ref.shape[1]
    by_rows = (((1,), (1,)), ((), ()))
    by_tokens = (((0,), (0,)), ((), ()))

    def dot(a, b, dims=(((1,), (0,)), ((), ()))):
        return lax.dot_general(a, b, dims, preferred_element_type=F32)

    pieces = list(range(min(i + 1, prompt_runs))) + ([i] if i >= prompt_runs else [])
    q = q_ref[i]
    peak = None
    for at, k in enumerate(pieces):
        s = dot(q, key(k), by_rows)
        keep = mask(i, k)
        if keep is not None:
            s = jnp.where(keep, s, -1e30)
        s_ref[:, at * keys : (at + 1) * keys] = s
        top = jnp.max(s, -1, keepdims=True)
        peak = top if peak is None else jnp.maximum(peak, top)
    total = jnp.zeros((m, 1), F32)
    out = jnp.zeros((m, HEAD_DIM), F32)
    for at, k in enumerate(pieces):
        p = jnp.exp(s_ref[:, at * keys : (at + 1) * keys] - peak)
        keep = mask(i, k)
        if keep is not None:
            p = jnp.where(keep, p, 0.0)
        s_ref[:, at * keys : (at + 1) * keys] = p
        total = total + jnp.sum(p, -1, keepdims=True)
        out = out + dot(p.astype(BF), value_of(k))
    inverse = 1.0 / total
    out = out * inverse
    o_ref[i] = out.astype(BF)
    do = do_ref[i]
    delta = jnp.sum(out * do.astype(F32), -1, keepdims=True)
    dq = jnp.zeros((m, HEAD_DIM), F32)
    for at, k in enumerate(pieces):
        p = s_ref[:, at * keys : (at + 1) * keys] * inverse
        dp = dot(do, value_of(k), by_rows)
        ds = (p * (dp - delta)).astype(BF)
        dq = dq + dot(ds, key(k))
        dk = dot(ds, q, by_tokens)
        dv = dot(p.astype(BF), do, by_tokens)
        if i == k:
            sum_ref[k, :, :HEAD_DIM] = dk
            sum_ref[k, :, HEAD_DIM:] = dv
        else:
            sum_ref[k, :, :HEAD_DIM] = sum_ref[k, :, :HEAD_DIM] + dk
            sum_ref[k, :, HEAD_DIM:] = sum_ref[k, :, HEAD_DIM:] + dv
    dq = (dq * (1.0 / math.sqrt(HEAD_DIM))).astype(BF).astype(F32)
    dq_ref[i] = turn(dq, [turn_ref[t, i] for t in range(3)], -1.0).astype(BF)


def attention_kernel(prompt_runs, one_prompt, q_ref, do_ref, kv_ref, row_ref, col_ref, turn_ref,
                     o_ref, dq_ref, dkv_ref, s_ref, sum_ref):
    def mask(i, k):
        rows, cols = row_ref[i], col_ref[k]
        if i == k:
            return (rows[:, 1:2] == cols[1:2, :]) & (cols[0:1, :] <= rows[:, 0:1])
        if one_prompt:
            return None
        return rows[:, 2:3] == cols[2:3, :]

    for i in range(q_ref.shape[0]):
        attention_step(
            i, prompt_runs, mask, q_ref, do_ref, lambda k: kv_ref[k, :, :HEAD_DIM], lambda k: kv_ref[k, :, HEAD_DIM:],
            turn_ref, o_ref, dq_ref, s_ref, sum_ref,
        )
    dkv_ref[...] = sum_ref[...].astype(BF)


def attention(prompt_runs, one_prompt, queries, d_out, pairs, row_meta, col_meta, tables):
    m = queries.shape[1]
    count = pairs.shape[1]
    return pl.pallas_call(
        functools.partial(attention_kernel, prompt_runs, one_prompt),
        out_shape=(
            jax.ShapeDtypeStruct(queries.shape, BF),
            jax.ShapeDtypeStruct(queries.shape, BF),
            jax.ShapeDtypeStruct(pairs.shape, BF),
        ),
        in_specs=[VMEM] * 6,
        out_specs=(VMEM,) * 3,
        scratch_shapes=[pltpu.VMEM((m, (prompt_runs + 1) * count), F32), pltpu.VMEM(pairs.shape, F32)],
        compiler_params=pltpu.CompilerParams(vmem_limit_bytes=60 * 2**20),
    )(queries, d_out, pairs, row_meta, col_meta, tables)


def angles_of(positions):
    frequency = 10000.0 ** (-jnp.arange(0, ROT, 2, dtype=F32) / ROT)
    return positions.astype(F32)[:, None] * frequency[None, :]


def rotate(values, cosine, sine):
    half = ROT // 2
    leading, behind = values[:, :half], values[:, half:ROT]
    return jnp.concatenate(
        [leading * cosine - behind * sine, behind * cosine + leading * sine, values[:, ROT:]], -1
    )


def per_device(
    inputs, attn_norm_gain, attn_norm_bias, mlp_norm_gain, mlp_norm_bias, qkv_weight, qkv_bias, dense_weight,
    dense_bias, expand_weight, expand_bias, shrink_weight, shrink_bias, token_of_row, cont_parent, position_ids,
    cotangent,
):
    heads, blocks = lax.axis_size("head"), lax.axis_size("blk")
    devices = heads * blocks
    ways = blocks // (2 * HEADS)
    assert heads == 2 and blocks == ways * 2 * HEADS
    x = lax.axis_index("head")
    b = lax.axis_index("blk")
    me = x * blocks + b
    c, h, w = b % 2, (b // 2) % HEADS, b // (2 * HEADS)
    tok_dev, width = inputs.shape
    rows = qkv_weight.shape[0]
    hidden = expand_weight.shape[1] // HEADS
    runs = tok_dev // STRIPE
    run_size = devices * STRIPE
    prompt_total = token_of_row.shape[0] - cont_parent.shape[0] * CONT
    prompt_runs = prompt_total // run_size
    one_prompt = prompt_total == PROMPT
    assert prompt_runs * run_size == prompt_total
    group_rows = runs * HEADS * STRIPE
    head3 = 3 * HEAD_DIM
    block_columns = head3 + hidden

    by_device = token_of_row.reshape(devices, tok_dev)
    run_of = by_device // run_size
    big = jnp.int32(2**30)
    each_run = jnp.arange(runs, dtype=jnp.int32)
    base = jnp.min(jnp.where(run_of[:, :, None] == each_run, by_device[:, :, None], big), 1)
    mine = lax.dynamic_index_in_dim(by_device, me, 0, False)
    sorted_at = mine // run_size * STRIPE + mine % STRIPE
    pick = (sorted_at[None, :] == jnp.arange(tok_dev, dtype=jnp.int32)[:, None]).astype(BF)
    base_position = jnp.min(
        jnp.where((mine // run_size)[:, None] == each_run, position_ids[:, None], big), 0
    )

    def ordered(rows_in):
        return jnp.dot(pick, rows_in, preferred_element_type=F32).astype(BF)

    def restored(rows_in):
        return lax.dot_general(pick, rows_in, (((0,), (0,)), ((), ())), preferred_element_type=F32).astype(BF)

    states = ordered(inputs).astype(F32)
    grad_low = ordered(cotangent)
    grad_out = grad_low.astype(F32)
    average = jnp.mean(states, -1, keepdims=True)
    centered = states - average
    inverse_spread = lax.rsqrt(jnp.mean(centered * centered, -1, keepdims=True) + 1e-05)
    normed = centered * inverse_spread
    normed_low = normed.astype(BF)

    gain_one, shift_one = attn_norm_gain.astype(F32), attn_norm_bias.astype(F32)
    gain_two, shift_two = mlp_norm_gain.astype(F32), mlp_norm_bias.astype(F32)
    qkv_wide, expand_wide = qkv_weight.astype(F32), expand_weight.astype(F32)

    def split_qkv(values):
        return values.reshape(-1, 3, HEADS, HEAD_DIM).transpose(2, 0, 1, 3).reshape(HEADS, -1, head3)

    def split(values):
        return values.reshape(values.shape[0], HEADS, -1).transpose(1, 0, 2)

    weights = jnp.concatenate(
        [
            split_qkv((qkv_wide * gain_one[:, None]).astype(BF)),
            split((expand_wide * gain_two[:, None]).astype(BF)),
            split(dense_weight),
            split(shrink_weight),
        ],
        -1,
    )
    own_qkv_bias = lax.dynamic_update_slice_in_dim(
        jnp.zeros((3 * width,), F32), qkv_bias.astype(F32), me * qkv_bias.shape[0], 0
    )
    own_expand_bias = lax.dynamic_update_slice_in_dim(
        jnp.zeros((HEADS * hidden,), F32), expand_bias.astype(F32), me * expand_bias.shape[0], 0
    )
    bias_parts = jnp.concatenate(
        [
            split_qkv((jnp.sum(qkv_wide * shift_one[:, None], 0) + own_qkv_bias)[None])[:, 0],
            split((jnp.sum(expand_wide * shift_two[:, None], 0) + own_expand_bias)[None])[:, 0],
        ],
        -1,
    )
    lanes = 128
    note_rows = block_columns // lanes

    slice_rows = width // lanes
    own_out_bias = lax.dynamic_update_slice_in_dim(
        jnp.zeros((width,), F32), dense_bias.astype(F32) + shrink_bias.astype(F32), me * rows, 0
    )
    notes = jnp.concatenate(
        [
            bias_parts.reshape(HEADS, note_rows, lanes),
            jnp.broadcast_to(own_out_bias.reshape(1, slice_rows, lanes), (HEADS, slice_rows, lanes)),
            jnp.zeros((HEADS, -(note_rows + slice_rows) % 8, lanes), F32),
        ],
        1,
    )

    def trig_of(positions):
        angles = angles_of(positions)
        cosine, sine = jnp.cos(angles), jnp.sin(angles)
        rest = ((0, 0), (0, lanes - ROT))
        return jnp.stack(
            [
                jnp.pad(jnp.concatenate([cosine, cosine], 1), rest, constant_values=1.0),
                jnp.pad(jnp.concatenate([sine, sine], 1), rest),
            ]
        )

    within = jnp.arange(STRIPE, dtype=jnp.int32)
    rows_run = group_rows // runs

    bases = base.reshape(2, ways, HEADS, 2, runs)
    own_base = lax.dynamic_index_in_dim(bases, x, 0, False)
    own_base = lax.dynamic_index_in_dim(own_base, w, 0, False)
    own_base = lax.dynamic_index_in_dim(own_base, c, 1, False)
    row_tokens = (own_base.T[:, :, None] + within).reshape(runs, rows_run)
    col_tokens = (bases.transpose(4, 1, 0, 3, 2)[..., None] + within).reshape(runs, run_size)

    fuse, opened = open_all(
        ways, rows, hidden, prompt_runs, prompt_total,
        normed_low.reshape(runs, STRIPE, width), grad_low.reshape(runs, STRIPE, width), weights, notes,
        trig_of(base_position), trig_of(within), row_tokens[:, :, None], col_tokens[:, None, :],
    )
    n_all, g_all, w_all, note, tables = opened[:5]
    n_all = n_all.reshape(group_rows, width)
    g_all = g_all.reshape(group_rows, width)
    w_all = w_all.reshape(width, block_columns + HEAD_DIM + hidden)
    bias_block = note[:note_rows].reshape(block_columns)
    out_bias = note[note_rows : note_rows + slice_rows].reshape(width)
    if fuse:
        attended, activated, d_expanded, d_queries, d_pairs = opened[5:]
        attended = attended.reshape(group_rows, HEAD_DIM)
    else:
        flat = tables.reshape(3, group_rows, lanes)
        cosine, sine = flat[0, :, : ROT // 2], flat[2, :, ROT // 2 : ROT]
        w_in, w_out = w_all[:, :block_columns], w_all[:, block_columns:]
        mixed = jnp.dot(n_all, w_in[:, :head3], preferred_element_type=F32) + bias_block[:head3]
        queries = (rotate(mixed[:, :HEAD_DIM], cosine, sine) * (1.0 / math.sqrt(HEAD_DIM))).astype(BF)
        keys = rotate(mixed[:, HEAD_DIM : 2 * HEAD_DIM], cosine, sine).astype(BF)
        values = mixed[:, 2 * HEAD_DIM :].astype(BF)
        pairs = exchange(ways, jnp.concatenate([keys, values], 1).reshape(runs, rows_run, 2 * HEAD_DIM))
        pairs = pairs.reshape(runs, run_size, 2 * HEAD_DIM)
        d_attended = jnp.dot(g_all, w_out[:, :HEAD_DIM], preferred_element_type=F32).astype(BF)
        expanded = jnp.dot(n_all, w_in[:, head3:], preferred_element_type=F32) + bias_block[head3:]
        activated, gelu_back = jax.vjp(lambda v: jax.nn.gelu(v, approximate=False), expanded)
        activated = activated.astype(BF)
        d_activated = jnp.dot(g_all, w_out[:, HEAD_DIM:], preferred_element_type=F32)
        d_expanded = gelu_back(d_activated)[0].astype(BF)

        def meta(tokens):
            is_prompt = tokens < prompt_total
            cont = (tokens - prompt_total) // CONT
            matches = cont[..., None] == jnp.arange(cont_parent.shape[0], dtype=jnp.int32)
            prompt = jnp.where(is_prompt, tokens // PROMPT, jnp.sum(jnp.where(matches, cont_parent, 0), -1))
            segment = jnp.where(is_prompt, -1 - tokens // PROMPT, cont)
            return tokens, segment, prompt

        attended, d_queries, d_pairs = attention(
            prompt_runs, one_prompt,
            queries.reshape(runs, rows_run, HEAD_DIM), d_attended.reshape(runs, rows_run, HEAD_DIM),
            pairs, jnp.stack(meta(row_tokens), -1), jnp.stack(meta(col_tokens), 1), tables,
        )
        attended = attended.reshape(group_rows, HEAD_DIM)

    d_pairs = d_pairs.reshape(runs, ways, 4, rows_run, 2 * HEAD_DIM)
    if ways > 1:
        alike = [[w2 * 2 * HEADS + k for w2 in range(ways)] for k in range(2 * HEADS)]
        d_pairs = lax.psum_scatter(
            d_pairs.astype(F32), "blk", scatter_dimension=1, axis_index_groups=alike, tiled=True
        ).astype(BF)
    d_pairs = d_pairs[:, 0]
    own_sums = jnp.sum(grad_out, 0).reshape(width // lanes, lanes)
    sum_note = jnp.concatenate(
        [jnp.zeros((note_rows, lanes), F32), own_sums, jnp.zeros((-(note_rows + width // lanes) % 8, lanes), F32)]
    )
    out_sum, e_sum, owned_a, owned_b, owned_notes = finish(
        ways, rows, attended, activated, d_expanded, d_queries, d_pairs,
        tables, w_all, n_all, g_all, sum_note,
    )
    output = restored((states + out_sum.reshape(tok_dev, width) + out_bias).astype(BF))
    e_sum = e_sum.reshape(tok_dev, width)
    dx = inverse_spread * (
        e_sum - jnp.mean(e_sum, -1, keepdims=True) - normed * jnp.mean(e_sum * normed, -1, keepdims=True)
    )
    input_grad = restored((grad_out + dx).astype(BF))
    owned_a, owned_b = owned_a.astype(F32), owned_b.astype(F32)

    def join_qkv(values):
        return values.reshape(HEADS, -1, 3, HEAD_DIM).transpose(1, 2, 0, 3).reshape(-1, 3 * width)

    def join(values):
        return values.transpose(1, 0, 2).reshape(values.shape[1], -1)

    raw_qkv = join_qkv(owned_b)
    dense_grad = join(owned_a[..., :HEAD_DIM])
    shrink_grad = join(owned_a[..., HEAD_DIM : HEAD_DIM + hidden])
    raw_expand = join(owned_a[..., HEAD_DIM + hidden :])
    column_sums = owned_notes[:, :note_rows].reshape(HEADS, 1, block_columns)
    qkv_sum = join_qkv(column_sums[..., :head3])
    expand_sum = join(column_sums[..., head3:])
    all_sums = jnp.sum(owned_notes[:, note_rows : note_rows + width // lanes], 0).reshape(width)
    bias_grad = lax.dynamic_slice_in_dim(all_sums, me * rows, rows, 0)
    qkv_grad = gain_one[:, None] * raw_qkv + shift_one[:, None] * qkv_sum
    expand_grad = gain_two[:, None] * raw_expand + shift_two[:, None] * expand_sum

    def own(values, count):
        return lax.dynamic_slice_in_dim(values, me * count, count, 0)

    return (
        output,
        input_grad,
        jnp.sum(qkv_wide * raw_qkv, 1),
        jnp.sum(qkv_wide * qkv_sum, 1),
        jnp.sum(expand_wide * raw_expand, 1),
        jnp.sum(expand_wide * expand_sum, 1),
        qkv_grad,
        own(qkv_sum[0, : 2 * width], 2 * width // devices),
        own(qkv_sum[0, 2 * width :], width // devices),
        dense_grad,
        bias_grad,
        expand_grad,
        own(expand_sum[0], HEADS * hidden // devices),
        shrink_grad,
        bias_grad,
    )


def solution(mesh):
    matrix, vector = P(("head", "blk"), None), P(("head", "blk"))
    return jax.shard_map(
        per_device,
        mesh=mesh,
        in_specs=(
            matrix, vector, vector, vector, vector, matrix, vector, matrix, vector, matrix, vector, matrix, vector,
            P(), P(), vector, matrix,
        ),
        out_specs=(
            matrix, matrix, vector, vector, vector, vector, matrix, vector, vector, matrix, vector, matrix, vector,
            matrix, vector,
        ),
        check_vma=False,
    )
```

```python
import functools
import math

import jax
import jax.numpy as jnp
from jax import lax
from jax.experimental import pallas as pl
from jax.experimental.pallas import tpu as pltpu
from jax.sharding import PartitionSpec as P

HEADS = 8
HEAD_DIM = 256
ROT = 64
PROMPT = 2048
CONT = 256
STRIPE = 16
MESH = pl.DeviceIdType.MESH
BF = jnp.bfloat16
F32 = jnp.float32
ANY = pl.BlockSpec(memory_space=pl.ANY)
VMEM = pl.BlockSpec(memory_space=pltpu.VMEM)
DMA = pltpu.SemaphoreType.DMA


class Place:
    def __init__(self, ways):
        self.ways = ways
        self.x = lax.axis_index("head")
        b = lax.axis_index("blk")
        self.c = b % 2
        self.h = (b // 2) % HEADS
        self.w = b // (2 * HEADS)
        self.hy = self.h % 2
        self.hz = self.h // 2

    def device(self, x=None, w=None, h=None, c=None):
        x = self.x if x is None else x
        w = self.w if w is None else w
        h = self.h if h is None else h
        c = self.c if c is None else c
        return (x, w * (2 * HEADS) + h * 2 + c)

    def peers_h(self):
        return [self.device(h=(self.h + k) % HEADS) for k in range(1, HEADS)]

    def peers_w(self):
        return [self.device(w=(self.w + k) % self.ways) for k in range(1, self.ways)]

    def peer_x(self):
        return self.device(x=1 - self.x)

    def peer_c(self):
        return self.device(c=1 - self.c)

    def peer_y(self):
        return self.device(h=self.h + 1 - 2 * self.hy)


def greet(devices):
    barrier = pltpu.get_barrier_semaphore()
    for one in devices:
        pl.semaphore_signal(barrier, inc=1, device_id=one, device_id_type=MESH)
    pl.semaphore_wait(barrier, len(devices))


def remote(src, dst, send, recv, device):
    return pltpu.make_async_remote_copy(
        src_ref=src, dst_ref=dst, send_sem=send, recv_sem=recv, device_id=device, device_id_type=MESH
    )


def call(body, out_shape, ins, scratch, ident, out_spec=ANY, in_spec=ANY):
    return pl.pallas_call(
        body,
        out_shape=out_shape,
        in_specs=[in_spec] * len(ins),
        out_specs=jax.tree.map(lambda _: out_spec, out_shape),
        scratch_shapes=scratch,
        compiler_params=pltpu.CompilerParams(
            collective_id=ident, has_side_effects=True, vmem_limit_bytes=60 * 2**20
        ),
    )(*ins)


LINE = HEADS // 2
A_ORDER = (0, 4, 1, 5, 2, 6, 3, 7)
EARLY = 2


def relay_rows(place, own, full, s, r):
    hz, hy = place.hz, place.hy
    d0, d1 = hz % 2, hz // 2

    def index(e1, e0, y):
        return (e1 * 2 + e0) * 2 + y

    far = place.device(h=index(1 - d1, d0, hy))
    near = place.device(h=index(d1, 1 - d0, hy))
    side = place.peer_y()
    made = []

    def push(src, idx, k, device):
        copy = remote(src, full.at[:, idx], s.at[k], r.at[idx], device)
        copy.start()
        made.append(copy)

    def arrived(idx):
        remote(full.at[:, idx], full.at[:, idx], s.at[0], r.at[idx], side).wait_recv()

    def first_z():
        push(own, place.h, 0, far)
        push(own, place.h, 1, near)

    def first_y():
        push(own, place.h, 2, side)

    def from_far():
        idx = index(1 - d1, d0, hy)
        arrived(idx)
        push(full.at[:, idx], idx, 3, near)
        push(full.at[:, idx], idx, 4, side)

    def from_near():
        idx = index(d1, 1 - d0, hy)
        arrived(idx)
        push(full.at[:, idx], idx, 5, side)

    def from_near_far():
        idx = index(1 - d1, 1 - d0, hy)
        arrived(idx)
        push(full.at[:, idx], idx, 6, side)

    def from_side():
        for z in range(LINE):
            arrived(z * 2 + 1 - hy)

    def sent():
        for copy in made:
            copy.wait_send()

    return first_z, first_y, from_far, from_near, from_near_far, from_side, sent


def open_kernel(ways, cuts, fuse, prompt_runs, prompt_total, *refs):
    names = ["n_in", "g_in", "w_in", "note_in", "trig_in", "step_in", "row_tok", "col_tok", "n_out", "g_out", "w_out", "note_out", "turn_out"]
    if fuse:
        names += ["left_out", "right_out", "half_out", "part_out"]
    names += ["v_n", "v_g", "v_w", "v_turn", "trig", "note", "note_c", "note_x", "note_w", "note_h", "own", "put"]
    names += ["ns", "nr", "gs", "gr", "wa", "wr", "xs", "xr", "cs", "cr", "t_s", "t_r", "nc_s", "nc_r", "nx_s", "nx_r", "nw_s", "nw_r", "nh_s", "nh_r"]
    if fuse:
        names += ["v_q", "v_do", "v_kv", "v_slope", "v_left", "v_right", "v_out", "lse", "s_ref", "sum_ref", "kv_c", "kv_x", "o_p", "o_y", "flat", "flat_sem"]
        names += ["kx_s", "kx_r", "kc_s", "kc_r", "fc_s", "fc_r", "fx_s", "fx_r", "oy_s", "oy_r"]
    at = dict(zip(names, refs, strict=True))
    (n_in, g_in, w_in, note_in, trig_in, step_in, n_out, g_out, w_out, turn_out, v_n, v_g, v_w, v_turn) = (
        at[k] for k in ["n_in", "g_in", "w_in", "note_in", "trig_in", "step_in", "n_out", "g_out", "w_out", "turn_out", "v_n", "v_g", "v_w", "v_turn"]
    )
    trig, note, note_c, note_x, note_w, note_h, own, put = (
        at[k] for k in ["trig", "note", "note_c", "note_x", "note_w", "note_h", "own", "put"]
    )
    place = Place(ways)
    x, w, h, c = place.x, place.w, place.h, place.c
    runs = v_n.shape[0]
    width = v_n.shape[-1]
    per_run = HEADS * STRIPE
    stage_a = [(dw, dh) for dw in range(ways) for dh in range(HEADS) if (dw, dh) != (0, 0)]
    greet(
        [place.device(w=(w + dw) % ways, h=(h + dh) % HEADS) for dw, dh in stage_a]
        + [place.peer_x(), place.peer_c()]
    )
    sends, puts = [], []

    def send(src, dst, s, r, device):
        copy = remote(src, dst, s, r, device)
        copy.start()
        sends.append(copy)
        return copy

    def save(src, dst):
        copy = pltpu.make_async_copy(src, dst, put.at[len(puts)])
        copy.start()
        puts.append(copy)

    mine = [
        pltpu.make_async_copy(w_in.at[h], v_w.at[x, w, h, c], own.at[0]),
        pltpu.make_async_copy(n_in, v_n.at[:, h], own.at[1]),
        pltpu.make_async_copy(g_in, v_g.at[:, h], own.at[2]),
        pltpu.make_async_copy(trig_in, trig.at[h], own.at[3]),
        pltpu.make_async_copy(note_in, note, own.at[4]),
    ]
    for copy in (mine[4], mine[0], mine[3], mine[1], mine[2]):
        copy.start()
    n_first_z, n_first_y, n_far, n_near, n_last, n_side, n_sent = relay_rows(place, n_in, v_n, at["ns"], at["nr"])
    g_first_z, g_first_y, g_far, g_near, g_last, g_side, g_sent = relay_rows(place, g_in, v_g, at["gs"], at["gr"])
    wa, wr, xs, xr, cs, cr = (at[k] for k in ["wa", "wr", "xs", "xr", "cs", "cr"])

    def columns(g):
        return pl.ds(cuts[g][0], cuts[g][1])

    def w_first(g, odd):
        for k, (dw, dh) in enumerate(stage_a):
            if dh % 2 != odd:
                continue
            h2 = (h + dh) % HEADS
            send(w_in.at[h2, :, columns(g)], v_w.at[x, w, h, c, :, columns(g)], wa.at[g, k], wr.at[g, w, h],
                 place.device(w=(w + dw) % ways, h=h2))

    def w_across(g):
        for dw, dh in stage_a:
            ws, hs = (w - dw) % ways, (h - dh) % HEADS
            spot = v_w.at[x, ws, hs, c, :, columns(g)]
            remote(spot, spot, wa.at[g, 0], wr.at[g, ws, hs], place.peer_x()).wait_recv()
        block = v_w.at[x, :, :, c, :, columns(g)]
        send(block, block, xs.at[g], xr.at[g], place.peer_x())
        send(block, block, cs.at[g, 0], cr.at[g, 0], place.peer_c())

    def w_beside(g):
        block = v_w.at[1 - x, :, :, c, :, columns(g)]
        remote(block, block, xs.at[g], xr.at[g], place.peer_x()).wait_recv()
        send(block, block, cs.at[g, 1], cr.at[g, 1], place.peer_c())

    def w_ready(g):
        for k, xx in ((0, x), (1, 1 - x)):
            block = v_w.at[xx, :, :, 1 - c, :, columns(g)]
            remote(block, block, cs.at[g, k], cr.at[g, k], place.peer_c()).wait_recv()
        if cuts[g][0] < w_out.shape[-1]:
            save(v_w.at[..., columns(g)], w_out.at[..., columns(g)])

    plan = []

    def step(time, body, *given):
        plan.append((time, len(plan), body, given))

    state = {}

    def trig_send():
        for k in range(1, HEADS):
            send(trig_in, trig.at[h], at["t_s"].at[k], at["t_r"].at[h], place.device(h=(h + k) % HEADS))

    def note_first():
        mine[4].wait()
        state["note"] = send(note, note_c, at["nc_s"].at[0], at["nc_r"].at[0], place.peer_c())

    def note_cross():
        state["note"].wait_recv()
        note_c[...] = note_c[...] + note[...]
        state["note"] = send(note_c, note_x, at["nx_s"].at[0], at["nx_r"].at[0], place.peer_x())

    def note_out():
        state["note"].wait_recv()
        note_x[...] = note_x[...] + note_c[...]
        summed = note_x
        if ways > 1:
            crossed = [
                send(note_x, note_w.at[k], at["nw_s"].at[k], at["nw_r"].at[k], device)
                for k, device in enumerate(place.peers_w())
            ]
            for copy in crossed:
                copy.wait_recv()
            total = note_x[...]
            for k in range(ways - 1):
                total = total + note_w[k]
            state["note"].wait_send()
            sends[:] = [one for one in sends if one is not state["note"]]
            note_c[...] = total
            summed = note_c
        for k in range(1, HEADS):
            h2 = (h + k) % HEADS
            send(summed.at[h2], note_h.at[h], at["nh_s"].at[k], at["nh_r"].at[h], place.device(h=h2))
        state["summed"] = summed

    def note_sum():
        bias = state["summed"][h]
        for k in range(1, HEADS):
            hs = (h - k) % HEADS
            remote(note_h.at[hs], note_h.at[hs], at["nh_s"].at[k], at["nh_r"].at[hs], place.peer_x()).wait_recv()
            bias = bias + note_h[hs]
        note_h[h] = bias
        save(note_h.at[h], at["note_out"])

    def turn_tables():
        mine[3].wait()
        for k in range(1, HEADS):
            hs = (h - k) % HEADS
            remote(trig.at[hs], trig.at[hs], at["t_s"].at[k], at["t_r"].at[hs], place.peer_x()).wait_recv()
        lane = lax.broadcasted_iota(jnp.int32, (STRIPE, 128), 1)
        for hh in range(HEADS):
            @pl.loop(0, runs)
            def _(run):
                cosine, sine = trig[hh, 0, pl.ds(run, 1)], trig[hh, 1, pl.ds(run, 1)]
                full = sine * step_in[0] + cosine * step_in[1]
                here = pl.ds(hh * STRIPE, STRIPE)
                v_turn[0, run, here] = cosine * step_in[0] - sine * step_in[1]
                v_turn[1, run, here] = jnp.where(lane < ROT // 2, -full, 0.0)
                v_turn[2, run, here] = jnp.where(lane < ROT // 2, 0.0, full)
        if not fuse:
            save(v_turn, turn_out)

    def rows_done(copy, side, src, dst):
        copy.wait()
        side()
        if not fuse:
            save(src, dst)

    flipped = []

    def flip(src, dst, t):
        spot = at["flat"].at[len(flipped) % 2]
        if len(flipped) >= 2:
            flipped[-2].wait()
        spot[...] = src[..., t * 256 : (t + 1) * 256].reshape(runs * per_run, 256).T
        copy = pltpu.make_async_copy(spot, dst.at[t * 256 : (t + 1) * 256], at["flat_sem"].at[len(flipped) % 2])
        copy.start()
        flipped.append(copy)

    expand_at, dense_at = 3, 4
    shrink = list(range(5, len(cuts)))
    step(0, trig_send)
    step(0.01, n_first_z)
    step(0.01, n_first_y)
    for k in range(3):
        step(0.02, w_first, k, 1)
        step(0.02, w_first, k, 0)
    step(0.2, note_first)
    step(2, mine[0].wait)
    step(3, note_cross)
    step(6, note_out)
    for k in range(3):
        step(31 + 4 * k, w_across, k)
        step(43 + 5 * k, w_beside, k)
        step(66, w_ready, k)
    step(16, n_near)
    step(27, n_far)
    step(36.1, w_first, expand_at, 0)
    step(52, n_last)
    step(52.1, w_first, expand_at, 1)
    step(52.2, w_first, dense_at, 1)
    step(52.3, w_first, dense_at, 0)
    step(52.4, g_first_z)
    step(52.5, g_first_y)
    step(55, turn_tables)
    step(57, note_sum)
    step(65, rows_done, mine[1], n_side, v_n, n_out)
    step(75.5, w_across, expand_at)
    step(86, w_across, dense_at)
    step(86.1, g_near)
    step(98, g_far)
    for g in shrink:
        step(98.1, w_first, g, 1)
        step(98.2, w_first, g, 0)
    step(112, w_beside, expand_at)
    step(113, w_ready, expand_at)
    step(117, g_last)
    step(121.5, w_beside, dense_at)
    step(134, rows_done, mine[2], g_side, v_g, g_out)
    step(134.1, w_ready, dense_at)
    for k, g in enumerate(shrink):
        step((125, 130, 135, 140)[k], w_across, g)
        step((135.6, 142, 147, 152)[k], w_beside, g)
        step(156, w_ready, g)
    if fuse:
        v_q, v_do, v_kv, v_slope, v_left, v_right, v_out, lse, s_ref, sum_ref, kv_c, kv_x, o_p, o_y = (
            at[k] for k in ["v_q", "v_do", "v_kv", "v_slope", "v_left", "v_right", "v_out", "lse", "s_ref", "sum_ref", "kv_c", "kv_x", "o_p", "o_y"]
        )
        kx_s, kx_r, kc_s, kc_r = (at[k] for k in ["kx_s", "kx_r", "kc_s", "kc_r"])
        kv_sends = []
        tile = 256

        def weight(first):
            return v_w[..., first : first + tile].reshape(width, tile)

        def bias_of(t):
            return jnp.concatenate([note_h[h, 2 * t : 2 * t + 1], note_h[h, 2 * t + 1 : 2 * t + 2]], 1)

        parts = 4
        span = runs // parts
        slot = x * 2 + c

        def project(p):
            lo = p * span
            left = v_n[lo : lo + span].reshape(span * per_run, width)
            tables = [v_turn[t, lo : lo + span].reshape(span * per_run, 128) for t in range(3)]
            for t in range(3):
                value = jnp.dot(left, weight(t * HEAD_DIM), preferred_element_type=F32) + bias_of(t)
                if t < 2:
                    value = turn(value, tables, 1.0)
                if t == 0:
                    v_q[lo : lo + span] = (value * (1.0 / math.sqrt(HEAD_DIM))).astype(BF).reshape(span, per_run, HEAD_DIM)
                else:
                    here = pl.ds((t - 1) * HEAD_DIM, HEAD_DIM)
                    v_kv[lo : lo + span, slot, :, here] = value.astype(BF).reshape(span, per_run, HEAD_DIM)
            block = v_kv.at[lo : lo + span, slot]
            kv_sends.append(send(block, block, kx_s.at[p], kx_r.at[p], place.peer_x()))
            kv_sends.append(send(block, block, kc_s.at[0, p], kc_r.at[0, p], place.peer_c()))

        def kv_beside(p):
            block = v_kv.at[pl.ds(p * span, span), (1 - x) * 2 + c]
            remote(block, block, kx_s.at[p], kx_r.at[p], place.peer_x()).wait_recv()
            kv_sends.append(send(block, block, kc_s.at[1, p], kc_r.at[1, p], place.peer_c()))

        def kv_ready(p):
            for k, xx in ((0, x), (1, 1 - x)):
                block = v_kv.at[pl.ds(p * span, span), xx * 2 + 1 - c]
                remote(block, block, kc_s.at[k, p], kc_r.at[k, p], place.peer_c()).wait_recv()

        half = runs * per_run // 2

        def expand(m, t):
            left = v_n[m * runs // 2 : (m + 1) * runs // 2].reshape(half, width)
            value = jnp.dot(left, weight(cuts[expand_at][0] + t * tile), preferred_element_type=F32) + bias_of(3 + t)
            sigma = 0.5 * (1.0 + lax.erf(value * math.sqrt(0.5)))
            slope = sigma + value * jnp.exp(-0.5 * value * value) * (1.0 / math.sqrt(2 * math.pi))
            v_slope[m * half : (m + 1) * half, t * tile : (t + 1) * tile] = slope
            first = HEAD_DIM + t * tile
            v_left[m * half : (m + 1) * half, first : first + tile] = (value * sigma).astype(BF)

        def shrink_back(m, t):
            left = v_g[m * runs // 2 : (m + 1) * runs // 2].reshape(half, width)
            value = jnp.dot(left, weight(cuts[shrink[0]][0] + t * tile), preferred_element_type=F32)
            value = value * v_slope[m * half : (m + 1) * half, t * tile : (t + 1) * tile]
            first = 3 * HEAD_DIM + t * tile
            v_right[m * half : (m + 1) * half, first : first + tile] = value.astype(BF)

        row_tok, col_tok = at["row_tok"], at["col_tok"]

        def segment(tokens):
            return jnp.where(tokens < prompt_total, -1 - tokens // PROMPT, (tokens - prompt_total) // CONT)

        def mask(i, k):
            if i != k:
                return None
            rows, cols = row_tok[i], col_tok[k]
            return (segment(rows) == segment(cols)) & (cols <= rows)

        def attended_back():
            for m in range(2):
                left = v_g[m * runs // 2 : (m + 1) * runs // 2].reshape(half, width)
                value = jnp.dot(left, weight(cuts[dense_at][0]), preferred_element_type=F32)
                v_do[m * runs // 2 : (m + 1) * runs // 2] = value.astype(BF).reshape(runs // 2, per_run, HEAD_DIM)

        def key(k):
            return v_kv[k, :, :, :HEAD_DIM].reshape(4 * per_run, HEAD_DIM)

        def value_of(k):
            return v_kv[k, :, :, HEAD_DIM:].reshape(4 * per_run, HEAD_DIM)

        def attend(i):
            here = slice(i * per_run, (i + 1) * per_run)
            out, total = attention_forward(i, prompt_runs, mask, v_q, key, value_of, s_ref)
            v_out[here], lse[here] = out, total
            v_left[here, :HEAD_DIM] = out.astype(BF)

        def attend_back(i):
            here = slice(i * per_run, (i + 1) * per_run)
            back = attention_backward(
                i, prompt_runs, mask, v_q, v_do, key, value_of, v_out[here], lse[here], v_turn, sum_ref
            )
            v_right[here, :HEAD_DIM] = back.astype(BF)

        def fold_first():
            for copy in kv_sends:
                copy.wait_send()
            sends[:] = [one for one in sends if not any(one is other for other in kv_sends)]
            v_kv[...] = sum_ref[...].astype(BF).reshape(v_kv.shape)
            for k, xx in ((0, 1 - x), (1, x)):
                state["fold", k] = send(
                    v_kv.at[:, xx * 2 + 1 - c], kv_c.at[:, k], at["fc_s"].at[k], at["fc_r"].at[k], place.peer_c()
                )

        def fold_add(k, final):
            state["fold", k].wait_recv()
            mine_slot = (x if k else 1 - x) * 2 + c

            @pl.loop(0, runs)
            def _(run):
                value = v_kv[run, mine_slot].astype(F32) + kv_c[run, k].astype(F32)
                if final:
                    value = value + kv_x[run].astype(F32)
                    back = turn(value[:, :HEAD_DIM].astype(BF).astype(F32), [v_turn[t, run] for t in range(3)], -1.0)
                    here = pl.ds(pl.multiple_of(run * per_run, per_run), per_run)
                    v_right[here, HEAD_DIM : 2 * HEAD_DIM] = back.astype(BF)
                    v_right[here, 2 * HEAD_DIM : 3 * HEAD_DIM] = value[:, HEAD_DIM:].astype(BF)
                else:
                    kv_c[run, k] = value.astype(BF)

        def fold_cross():
            fold_add(0, False)
            state["fold_x"] = send(kv_c.at[:, 0], kv_x, at["fx_s"].at[0], at["fx_r"].at[0], place.peer_x())

        def fold_close():
            state["fold_x"].wait_recv()
            fold_add(1, True)
            save(v_right.at[:, pl.ds(0, 3 * HEAD_DIM)], at["right_out"].at[:, pl.ds(0, 3 * HEAD_DIM)])

        chunks, early, wide = o_p.shape[0], o_y.shape[0], o_p.shape[-1]

        def out_part(q):
            for k in range(wide // tile):
                n = q * (wide // tile) + k
                per_x = width // 2 // tile
                low = n % per_x * HEADS // per_x
                some = v_w[n // per_x, 0, low : low + HEADS // per_x, :, :, cuts[dense_at][0] :]
                value = lax.dot_general(
                    v_left[...], some.reshape(tile, v_left.shape[1]), (((1,), (1,)), ((), ())), preferred_element_type=F32
                )
                o_p[q, :, :, :, :, :, k * tile : (k + 1) * tile] = value.astype(BF).reshape(runs, 2, 2, 2, STRIPE, tile)
            if q < early:
                state["out", q] = send(
                    o_p.at[q, :, :, :, 1 - place.hy], o_y.at[q], at["oy_s"].at[q], at["oy_r"].at[q], place.peer_y()
                )
            else:
                save(o_p.at[q], at["part_out"].at[q - early])

        def out_side(q):
            state["out", q].wait_recv()

            @pl.loop(0, runs)
            def _(run):
                for t in range(LINE):
                    value = o_y[q, run, t // 2, t % 2].astype(F32) + o_p[q, run, t // 2, t % 2, place.hy].astype(F32)
                    o_y[q, run, t // 2, t % 2] = value.astype(BF)

            save(o_y.at[q], at["half_out"].at[q])

        for p in range(parts):
            step(67 + 2 * p, project, p)
            step(80.5 + 6 * p, kv_beside, p)
            step(101, kv_ready, p)
        for i in range(runs):
            step(105.5 + 1.2 * i, attend, i)
            step(135 + 2 * i, attend_back, i)
            step(75, flip, v_n, n_out, i)
            step(163, flip, v_g, g_out, i)
        count = v_slope.shape[1] // tile
        for t in range(count):
            for m in range(2):
                step(117.5 + 0.1 * t + 0.05 * m, expand, m, t)
                step(161 + 0.1 * t, shrink_back, m, t)
        step(134.5, attended_back)
        step(151.5, fold_first)
        step(155, fold_cross)
        for q in range(chunks):
            step(156.5 + 0.1 * q if q < early else 162, out_part, q)
        for q in range(early):
            step(172 + 12 * q, out_side, q)
        step(157, save, v_left, at["left_out"])
        step(161.9, save, v_right.at[:, pl.ds(3 * HEAD_DIM, v_slope.shape[1])], at["right_out"].at[:, pl.ds(3 * HEAD_DIM, v_slope.shape[1])])
        step(183, fold_close)
    for _, _, body, given in sorted(plan, key=lambda one: one[:2]):
        body(*given)
    for copy in puts + flipped[-2:]:
        copy.wait()
    for copy in sends:
        copy.wait_send()
    n_sent()
    g_sent()


def open_all(ways, rows, hidden, prompt_runs, prompt_total, normed, grads, weights, notes, trig, steps, row_tok, col_tok):
    runs, _, width = normed.shape
    columns = weights.shape[2]
    fuse = ways == 1 and prompt_total == PROMPT
    head3 = 3 * HEAD_DIM
    cuts = [(k * HEAD_DIM, HEAD_DIM) for k in range(3)] + [(head3, hidden), (head3 + hidden, HEAD_DIM)]
    cuts += [(head3 + hidden + HEAD_DIM + k * 256, 256) for k in range(hidden // 256)]
    blocks = (2, ways, HEADS, 2, rows, columns)
    group = runs * HEADS * STRIPE
    per_run = HEADS * STRIPE

    def shape(dims, kind=BF):
        return jax.ShapeDtypeStruct(dims, kind)

    gathered = (runs, HEADS, STRIPE, width)
    tables = (3, runs, per_run, 128)
    chunks, wide = 4, width // 4
    kept = head3 + hidden if fuse else columns
    outs = [
        shape((width, group) if fuse else gathered), shape((width, group) if fuse else gathered), shape(blocks[:-1] + (kept,)), shape(notes.shape[1:], F32),
        shape((1, 1, 8, 128) if fuse else tables, F32),
    ]
    if fuse:
        outs += [
            shape((group, HEAD_DIM + hidden)), shape((group, head3 + hidden)),
            shape((EARLY, runs, 2, 2, STRIPE, wide)), shape((chunks - EARLY, runs, 2, 2, 2, STRIPE, wide)),
        ]
    extra = max(ways - 1, 1)
    count = len(cuts)
    scratch = [
        pltpu.VMEM(gathered, BF), pltpu.VMEM(gathered, BF), pltpu.VMEM(blocks, BF), pltpu.VMEM(tables, F32),
        pltpu.VMEM((HEADS,) + trig.shape, F32),
        pltpu.VMEM(notes.shape, F32), pltpu.VMEM(notes.shape, F32), pltpu.VMEM(notes.shape, F32),
        pltpu.VMEM((extra,) + notes.shape, F32), pltpu.VMEM(notes.shape, F32),
        DMA((5,)), DMA((count + 14,)),
        DMA((7,)), DMA((HEADS,)), DMA((7,)), DMA((HEADS,)),
        DMA((count, ways * HEADS)), DMA((count, ways, HEADS)), DMA((count,)), DMA((count,)), DMA((count, 2)), DMA((count, 2)),
        DMA((HEADS,)), DMA((HEADS,)), DMA((1,)), DMA((1,)), DMA((1,)), DMA((1,)), DMA((extra,)), DMA((extra,)),
        DMA((HEADS,)), DMA((HEADS,)),
    ]
    if fuse:
        scratch += [
            pltpu.VMEM((runs, per_run, HEAD_DIM), BF), pltpu.VMEM((runs, per_run, HEAD_DIM), BF),
            pltpu.VMEM((runs, 4, per_run, 2 * HEAD_DIM), BF), pltpu.VMEM((group, hidden), F32),
            pltpu.VMEM((group, HEAD_DIM + hidden), BF), pltpu.VMEM((group, head3 + hidden), BF),
            pltpu.VMEM((group, HEAD_DIM), F32), pltpu.VMEM((group, 1), F32),
            pltpu.VMEM((per_run, (prompt_runs + 1) * 4 * per_run), F32),
            pltpu.VMEM((runs, 4 * per_run, 2 * HEAD_DIM), F32),
            pltpu.VMEM((runs, 2, per_run, 2 * HEAD_DIM), BF), pltpu.VMEM((runs, per_run, 2 * HEAD_DIM), BF),
            pltpu.VMEM((chunks, runs, 2, 2, 2, STRIPE, wide), BF), pltpu.VMEM((EARLY, runs, 2, 2, STRIPE, wide), BF),
            pltpu.VMEM((2, 256, group), BF), DMA((2,)),
            DMA((4,)), DMA((4,)), DMA((2, 4)), DMA((2, 4)),
            DMA((2,)), DMA((2,)), DMA((1,)), DMA((1,)), DMA((EARLY,)), DMA((EARLY,)),
        ]
    return fuse, pl.pallas_call(
        functools.partial(open_kernel, ways, tuple(cuts), fuse, prompt_runs, prompt_total),
        out_shape=tuple(outs),
        in_specs=[ANY] * 5 + [VMEM] * 3,
        out_specs=(ANY,) * len(outs),
        scratch_shapes=scratch,
        compiler_params=pltpu.CompilerParams(collective_id=0, has_side_effects=True, vmem_limit_bytes=62 * 2**20),
    )(normed, grads, weights, notes, trig, steps, row_tok, col_tok)


def exchange_kernel(ways, own, full, local, to_w, to_x, to_c, recv):
    place = Place(ways)
    x, w, c = place.x, place.w, place.c
    runs = own.shape[0]
    parts = 4
    span = runs // parts
    greet(place.peers_w() + [place.peer_x(), place.peer_c()])

    def spot(ws, xs, cs, p):
        return full.at[pl.ds(p * span, span), ws * 4 + xs * 2 + cs]

    sends = []

    def send(src, ws, xs, cs, p, sem, device):
        copy = remote(src, spot(ws, xs, cs, p), sem, recv.at[ws, xs, cs, p], device)
        copy.start()
        sends.append(copy)

    def arrived(ws, xs, cs, p):
        remote(spot(ws, xs, cs, p), spot(ws, xs, cs, p), local.at[0], recv.at[ws, xs, cs, p], place.peer_x()).wait_recv()

    keep = pltpu.make_async_copy(own, full.at[:, w * 4 + x * 2 + c], local.at[0])
    for p in range(parts):
        src = own.at[pl.ds(p * span, span)]
        for k, device in enumerate(place.peers_w()):
            send(src, w, x, c, p, to_w.at[k, p], device)
        send(src, w, x, c, p, to_x.at[w, p], place.peer_x())
    for p in range(parts):
        send(own.at[pl.ds(p * span, span)], w, x, c, p, to_c.at[w, x, p], place.peer_c())
    keep.start()
    for k in range(1, ways):
        ws = (w - k) % ways
        for p in range(parts):
            arrived(ws, x, c, p)
            send(spot(ws, x, c, p), ws, x, c, p, to_x.at[ws, p], place.peer_x())
            send(spot(ws, x, c, p), ws, x, c, p, to_c.at[ws, x, p], place.peer_c())
    for k in range(ways):
        ws = (w - k) % ways
        for p in range(parts):
            arrived(ws, 1 - x, c, p)
            send(spot(ws, 1 - x, c, p), ws, 1 - x, c, p, to_c.at[ws, 1 - x, p], place.peer_c())
    for k in range(ways):
        ws = (w - k) % ways
        for p in range(parts):
            arrived(ws, x, 1 - c, p)
            arrived(ws, 1 - x, 1 - c, p)
    keep.wait()
    for copy in sends:
        copy.wait_send()


def exchange(ways, own):
    runs, rows, columns = own.shape
    return call(
        functools.partial(exchange_kernel, ways),
        jax.ShapeDtypeStruct((runs, 4 * ways, rows, columns), BF),
        (own,),
        [DMA((1,)), DMA((ways, 4)), DMA((ways, 4)), DMA((ways, 2, 4)), DMA((ways, 2, 2, 4))],
        1,
    )


def turn(u, tables, sign):
    cosine, lower, upper = tables
    front = u[:, :128]
    moved = pltpu.roll(front, 96, 1) * lower + pltpu.roll(front, 32, 1) * upper
    return jnp.concatenate([front * cosine + moved * sign, u[:, 128:]], 1)


def finish_kernel(ways, early, left, right, w_all, n_all, g_all, note, half_in, part_in,
                  out_sum, e_sum, own_a, own_b, note_all,
                  v_left, v_right, v_w, o_own, o_y, o_1, o_2, e_p, e_y, e_1, e_2,
                  raw, ring, a_c, a_x, a_w, b_c, b_x, b_w, n_mine, n_c, n_x, n_w,
                  load, load_raw, load_o,
                  oy_s, oy_r, o1_s, o1_r, o2_s, o2_r, ey_s, ey_r, e1_s, e1_r, e2_s, e2_r,
                  ac_s, ac_r, ax_s, ax_r, aw_s, aw_r, ah_s, ah_r,
                  bc_s, bc_r, bx_s, bx_r, bw_s, bw_r, bh_s, bh_r, keep, n_s, n_r):
    place = Place(ways)
    x, w, h, c, hy, hz = place.x, place.w, place.h, place.c, place.hy, place.hz
    d0, d1 = hz % 2, hz // 2
    runs = v_left.shape[0]
    chunks = e_p.shape[0]
    wide = e_p.shape[-1]
    rows = own_a.shape[1]
    hp = 256 // (2 * rows)
    tiles = HEADS // hp
    a_cols, b_cols = own_a.shape[2], own_b.shape[2]
    inner = v_left.shape[-1]
    head3 = 3 * HEAD_DIM
    group = runs * HEADS * STRIPE
    sends = []

    def send(src, dst, s, r, device):
        copy = remote(src, dst, s, r, device)
        copy.start()
        sends.append(copy)
        return copy

    greet(place.peers_h() + place.peers_w() + [place.peer_x(), place.peer_c()])

    def fetch(src, dst, sem):
        copy = pltpu.make_async_copy(src, dst, sem)
        copy.start()
        return copy


    def partial(src, q, buf, depth):
        @pl.loop(0, wide // 256)
        def _(k):
            at = pl.multiple_of(k * 256, 256)
            value = lax.dot_general(
                src[...].reshape(group, depth),
                v_w[pl.ds(pl.multiple_of(q * wide + at, 256), 256), :depth],
                (((1,), (1,)), ((), ())),
                preferred_element_type=F32,
            )
            buf[q, :, :, :, :, :, pl.ds(at, 256)] = value.astype(BF).reshape(runs, 2, 2, 2, STRIPE, 256)

    def sums(mine, y, one, two, s_1, r_1, s_2, r_2, total):
        def near(q):
            target = place.device(h=(hz + 1 - 2 * d0) * 2 + hy)
            return send(y.at[q, :, :, 1 - d0], one.at[q], s_1.at[q], r_1.at[q], target)

        def after_y(q, copy):
            copy.wait_recv()

            @pl.loop(0, runs)
            def _(run):
                for t in range(LINE):
                    value = y[q, run, t // 2, t % 2].astype(F32) + mine(q, run, t).astype(F32)
                    y[q, run, t // 2, t % 2] = value.astype(BF)

            return near(q)

        def after_1(q, copy):
            copy.wait_recv()

            @pl.loop(0, runs)
            def _(run):
                for t in range(2):
                    value = one[q, run, t].astype(F32) + y[q, run, t, d0].astype(F32)
                    one[q, run, t] = value.astype(BF)

            target = place.device(h=((1 - d1) * 2 + d0) * 2 + hy)
            return send(one.at[q, :, 1 - d1], two.at[q], s_2.at[q], r_2.at[q], target)

        def after_2(q, copy):
            copy.wait_recv()

            @pl.loop(0, runs)
            def _(run):
                total[run, :, q * wide : (q + 1) * wide] = two[q, run].astype(F32) + one[q, run, d1].astype(F32)

        return near, after_y, after_1, after_2

    o_near, o_after_y, o_after_1, o_after_2 = sums(
        lambda q, run, t: o_own[q - (early or 0), run, t // 2, t % 2], o_y, o_1, o_2, o1_s, o1_r, o2_s, o2_r, out_sum
    )
    _, e_after_y, e_after_1, e_after_2 = sums(
        lambda q, run, t: e_p[q, run, t // 2, t % 2, hy], e_y, e_1, e_2, e1_s, e1_r, e2_s, e2_r, e_sum
    )

    order_t = [(k, dw, dt) for k in range(2) for dw in list(range(1, ways)) + [0] for dt in list(range(1, tiles)) + [0]]
    own_t = h // hp

    def where(k, dw, dt):
        return (1 - x if k == 0 else x), (w + dw) % ways, (own_t + dt) % tiles

    def product(m, buf, src, first, count, at):
        @pl.loop(0, count // 256)
        def _(k):
            col = pl.multiple_of(k * 256, 256)
            value = jnp.dot(
                raw[m % 2, buf], src[..., pl.ds(first + col, 256)].reshape(group, 256), preferred_element_type=F32
            )
            ring[m % 3, :, :, :, pl.ds(at + col, 256)] = value.astype(BF).reshape(hp, 2, rows, 256)

    made, order_m = [], []

    def raw_copies(m):
        n, need = order_m[m]
        xs, ws, t = where(*order_t[n])
        at = pl.multiple_of(((xs * ways + ws) * tiles + t) * 256, 256)
        return [
            pltpu.make_async_copy(src.at[pl.ds(at, 256)], raw.at[m % 2, buf], load_raw.at[m % 2, buf])
            for buf, src in need
        ]

    def begin(m):
        if m < len(order_m):
            for copy in raw_copies(m):
                copy.start()

    def grads(cols, from_c, from_x, from_w, c_s, c_r, x_s, x_r, w_s, w_r, h_s, h_r, out, fill, flag):
        first, second, third, spot = {}, {}, {}, {}

        def make(n):
            m = len(made)
            if m >= 3:
                made[m - 3].wait_send()
            for copy in raw_copies(m):
                copy.wait()
            fill(m)
            begin(m + 1)
            k, dw, dt = order_t[n]
            first[n] = remote(
                ring.at[m % 3, :, 1 - c, :, pl.ds(0, cols)], from_c.at[k, dw, dt], c_s.at[n], c_r.at[n], place.peer_c()
            )
            first[n].start()
            spot[n] = m % 3
            made.append(first[n])

        def mine(n):
            k, dw, dt = order_t[n]
            first[n].wait_recv()

            @pl.loop(0, hp)
            def _(q):
                value = from_c[k, dw, dt, q].astype(F32) + ring[spot[n], q, c, :, :cols].astype(F32)
                from_c[k, dw, dt, q] = value.astype(BF)

        def cross(n):
            k, dw, dt = order_t[n]
            second[dw, dt] = send(from_c.at[0, dw, dt], from_x.at[dw, dt], x_s.at[dw, dt], x_r.at[dw, dt], place.peer_x())

        def close(n):
            k, dw, dt = order_t[n]
            _, ws, t = where(k, dw, dt)
            second[dw, dt].wait_recv()
            more = [from_x.at[dw, dt]]
            if dw == 0:
                for dv in range(1, ways):
                    third[dv, dt].wait_recv()
                    more.append(from_w.at[dv - 1, dt])

            @pl.loop(0, hp)
            def _(q):
                value = from_c[1, dw, dt, q].astype(F32)
                for ref in more:
                    value = value + ref[q].astype(F32)
                from_c[1, dw, dt, q] = value.astype(BF)

            if dw != 0:
                third[dw, dt] = send(from_c.at[1, dw, dt], from_w.at[dw - 1, dt], w_s.at[dw - 1, dt], w_r.at[dw - 1, dt], place.device(w=ws))
                return
            for q in range(hp):
                hs = t * hp + q
                at = dt * hp + q

                @pl.when(hs != h)
                def _():
                    remote(from_c.at[1, 0, dt, q], out.at[h], h_s.at[at], h_r.at[h], place.device(h=hs)).start()

                @pl.when(hs == h)
                def _():
                    pltpu.make_async_copy(from_c.at[1, 0, dt, q], out.at[h], keep.at[flag]).start()

        def end():
            for n in range(len(order_t)):
                k, dw, dt = order_t[n]
                if k == 1 and dw == 0:
                    _, _, t = where(k, dw, dt)
                    for q in range(hp):
                        hs = t * hp + q

                        @pl.when(hs != h)
                        def _():
                            remote(from_c.at[1, 0, dt, q], out.at[h], h_s.at[dt * hp + q], h_r.at[h], place.device(h=hs)).wait_send()
            for dh in range(1, HEADS):
                hs = (h + dh) % HEADS
                remote(out.at[hs], out.at[hs], h_s.at[0], h_r.at[hs], place.peer_x()).wait_recv()
            pltpu.make_async_copy(from_c.at[1, 0, 0, 0], out.at[h], keep.at[flag]).wait()

        return make, mine, cross, close, end

    def fill_a(m):
        product(m, 1, v_left, 0, inner, 0)
        product(m, 0, v_right, head3, a_cols - inner, inner)

    def fill_b(m):
        product(m, 0, v_right, 0, head3, 0)

    a_make, a_mine, a_cross, a_close, a_end = grads(
        a_cols, a_c, a_x, a_w, ac_s, ac_r, ax_s, ax_r, aw_s, aw_r, ah_s, ah_r, own_a, fill_a, 0
    )
    b_make, b_mine, b_cross, b_close, b_end = grads(
        b_cols, b_c, b_x, b_w, bc_s, bc_r, bx_s, bx_r, bw_s, bw_r, bh_s, bh_r, own_b, fill_b, 1
    )
    count = len(order_t)
    half = count // 2
    order_m += [(n, ((0, n_all), (1, g_all))) for n in A_ORDER] + [(n, ((0, n_all),)) for n in A_ORDER]

    plan = []

    def step(time, body, *given):
        plan.append((time, len(plan), body, given))

    state = {}

    def wait_all(copies):
        for copy in copies:
            copy.wait()

    def e_part(q):
        partial(v_right, q, e_p, v_right.shape[-1])
        state["e", q] = send(e_p.at[q, :, :, :, 1 - hy], e_y.at[q], ey_s.at[q], ey_r.at[q], place.peer_y())

    def o_start():
        for q in range(early, chunks):
            state["o", q] = send(part_in.at[q - early, :, :, :, 1 - hy], o_y.at[q], oy_s.at[q], oy_r.at[q], place.peer_y())
        for q in range(chunks):
            if q < early:
                state["o_load", q] = fetch(half_in.at[q], o_y.at[q], load_o.at[q])
            else:
                state["o_load", q] = fetch(part_in.at[q - early, :, :, :, hy], o_own.at[q - early], load_o.at[q])

    def o_first(q):
        state["o_load", q].wait()
        if q < early:
            state["o", q] = o_near(q)
        else:
            state["o", q] = o_after_y(q, state["o", q])

    def advance(key, body, q):
        state[key, q] = body(q, state[key, q])

    note_w = []
    base = 1 + ways

    def note_sums():
        state["note_load"].wait()

        @pl.loop(0, v_right.shape[-1] // 128)
        def _(k):
            at = pl.multiple_of(k * 128, 128)
            value = v_right[..., pl.ds(at, 128)].reshape(group, 128).astype(F32)
            n_mine[pl.ds(k, 1), :] = jnp.sum(value, 0, keepdims=True)

        state["note"] = send(n_mine, n_c, n_s.at[0], n_r.at[0], place.peer_c())

    def note_cross():
        state["note"].wait_recv()
        n_c[...] = n_c[...] + n_mine[...]
        state["note"] = send(n_c, n_x, n_s.at[1], n_r.at[1], place.peer_x())

    def note_ways():
        state["note"].wait_recv()
        n_x[...] = n_x[...] + n_c[...]
        for k, device in enumerate(place.peers_w()):
            note_w.append(send(n_x, n_w.at[k], n_s.at[2 + k], n_r.at[2 + k], device))

    def note_out():
        if ways > 1:
            wait_all(note_w)
            total = n_x[...]
            for k in range(ways - 1):
                total = total + n_w[k]
            n_x[...] = total
        for dh in range(1, HEADS):
            send(n_x, note_all.at[h], n_s.at[base + dh], n_r.at[base + h], place.device(h=(h + dh) % HEADS))
        state["note_keep"] = pltpu.make_async_copy(n_x, note_all.at[h], keep.at[3])
        state["note_keep"].start()

    if early is not None:
        o_start()
    state["note_load"] = fetch(note, n_mine, keep.at[2])
    loads = [fetch(right, v_right, load.at[0]), fetch(left, v_left, load.at[1])]
    begin(0)
    w_load = fetch(w_all.at[:, pl.ds(0, v_right.shape[-1])], v_w, load.at[2])
    if early is not None:
        for q, times in enumerate(((0.5, 9, 19.5), (0.6, 14.5, 25), (14.2, 37, 49), (26, 48.2, 62))):
            step(times[0], o_first, q)
            step(times[1], advance, "o", o_after_1, q)
            step(times[2], advance, "o", o_after_2, q)
    step(1, wait_all, loads)
    for i, (n, time) in enumerate(zip(A_ORDER, (2, 4.5, 10, 15, 19.6, 26.2, 31, 36), strict=True)):
        step(time, a_make, n)
        if i > 0:
            step(time, a_mine, A_ORDER[i - 1])
            if A_ORDER[i - 1] < half:
                step(time, a_cross, A_ORDER[i - 1])
    step(38, a_mine, A_ORDER[-1])
    step(7.2, w_load.wait)
    for q in range(chunks):
        step((7.3, 13, 17.5, 22.5)[q], e_part, q)
    step(25.5, note_sums)
    step(36.5, note_cross)
    step(60, note_ways)
    step(60, note_out)
    for i, (n, time) in enumerate(zip(A_ORDER, (39, 40, 41, 42, 44, 45, 46, 47), strict=True)):
        step(time, b_make, n)
        if i > 0:
            step(time, b_mine, A_ORDER[i - 1])
            if A_ORDER[i - 1] < half:
                step(time, b_cross, A_ORDER[i - 1])
    step(47.5, b_mine, A_ORDER[-1])
    for n, times in zip(range(half, count), ((22, 74), (35.5, 79), (49.5, 84), (63, 88)), strict=True):
        step(times[0], a_close, n)
        step(times[1], b_close, n)
    for q, times in enumerate(((48, 66, 80), (59, 77, 92), (71, 89, 104), (83, 101, 114))):
        step(times[0], advance, "e", e_after_y, q)
        step(times[1], advance, "e", e_after_1, q)
        step(times[2], advance, "e", e_after_2, q)
    for _, _, body, given in sorted(plan, key=lambda one: one[:2]):
        body(*given)
    for copy in made[-3:]:
        copy.wait_send()
    a_end()
    b_end()
    state["note_keep"].wait()
    for dh in range(1, HEADS):
        hs = (h + dh) % HEADS
        remote(note_all.at[hs], note_all.at[hs], n_s.at[0], n_r.at[base + hs], place.peer_x()).wait_recv()
    for copy in sends:
        if not any(copy is other for other in note_w):
            copy.wait_send()


def finish(ways, rows, left, right, w_all, n_all, g_all, note, half, part):
    width = w_all.shape[0]
    inner, right_cols = left.shape[1], right.shape[1]
    head3 = 3 * HEAD_DIM
    a_cols, b_cols = inner + right_cols - head3, head3
    group = n_all.shape[1]
    runs = group // (HEADS * STRIPE)
    lines = (runs, LINE, 2, STRIPE)
    hp = 256 // (2 * rows)
    tiles = HEADS // hp
    chunks, wide = 4, width // 4
    extra = max(ways - 1, 1)
    count = 2 * ways * tiles
    assert count == len(A_ORDER)
    early = None if half is None else half.shape[0]

    def vm(shape, kind=BF):
        return pltpu.VMEM(shape, kind)

    def row_buffers(first, used):
        return [
            vm(first),
            vm((chunks, runs, 2, 2, STRIPE, wide) if used else (1, 1, 1, 1, 16, 128)),
            vm((chunks, runs, 2, STRIPE, wide) if used else (1, 1, 1, 16, 128)),
            vm((chunks, runs, STRIPE, wide) if used else (1, 1, 16, 128)),
        ]

    def spare(shape):
        return shape if ways > 1 else (1,) * (len(shape) - 2) + (16, 128)

    def gradient_buffers(cols):
        return [
            vm((2, ways, tiles, hp, rows, cols)),
            vm((ways, tiles, hp, rows, cols)),
            vm(spare((extra, tiles, hp, rows, cols))),
        ]

    def gradient_sems():
        return [
            DMA((count,)), DMA((count,)), DMA((ways, tiles)), DMA((ways, tiles)), DMA((extra, tiles)), DMA((extra, tiles)),
            DMA((HEADS,)), DMA((HEADS,)),
        ]

    scratch = (
        [
            vm(lines + (inner,)), vm(lines + (right_cols,)), vm((width, right_cols)),
        ]
        + row_buffers((max(chunks - (early or 0), 1), runs, 2, 2, STRIPE, wide) if early is not None else (1, 1, 1, 1, 16, 128), early is not None)
        + row_buffers((chunks, runs, 2, 2, 2, STRIPE, wide), True)
        + [vm((2, 2, 256, group)), vm((3, hp, 2, rows, a_cols))]
        + gradient_buffers(a_cols) + gradient_buffers(b_cols)
        + [vm(note.shape, F32)] * 3 + [vm((extra,) + note.shape, F32)]
        + [DMA((3,)), DMA((2, 2)), DMA((chunks,))]
        + [DMA((chunks,))] * 12
        + gradient_sems() + gradient_sems()
        + [DMA((4,)), DMA((1 + ways + HEADS,)), DMA((1 + ways + HEADS,))]
    )
    shapes = (
        jax.ShapeDtypeStruct((runs, STRIPE, width), F32),
        jax.ShapeDtypeStruct((runs, STRIPE, width), F32),
        jax.ShapeDtypeStruct((HEADS, rows, a_cols), BF),
        jax.ShapeDtypeStruct((HEADS, rows, b_cols), BF),
        jax.ShapeDtypeStruct((HEADS,) + note.shape, F32),
    )
    empty = jnp.zeros((1, 1, 1, 1, 16, 128), BF)
    ins = (
        left.reshape(lines + (inner,)), right.reshape(lines + (right_cols,)), w_all, n_all, g_all, note,
        empty if half is None else half, empty if part is None else part,
    )
    return pl.pallas_call(
        functools.partial(finish_kernel, ways, early),
        out_shape=shapes,
        in_specs=[ANY] * len(ins),
        out_specs=(VMEM, VMEM, ANY, ANY, ANY),
        scratch_shapes=scratch,
        compiler_params=pltpu.CompilerParams(collective_id=2, has_side_effects=True, vmem_limit_bytes=62 * 2**20),
    )(*ins)


def pieces_of(i, prompt_runs):
    return list(range(min(i + 1, prompt_runs))) + ([i] if i >= prompt_runs else [])


def attention_forward(i, prompt_runs, mask, q_ref, key, value_of, s_ref):
    q = q_ref[i]
    peak, scores = None, []
    for at, k in enumerate(pieces_of(i, prompt_runs)):
        keys = key(k)
        s = lax.dot_general(q, keys, (((1,), (1,)), ((), ())), preferred_element_type=F32)
        keep = mask(i, k)
        if keep is not None:
            s = jnp.where(keep, s, -1e30)
        here = slice(at * keys.shape[0], (at + 1) * keys.shape[0])
        s_ref[:, here] = s
        top = jnp.max(s, -1, keepdims=True)
        peak = top if peak is None else jnp.maximum(peak, top)
        scores.append((k, here))
    total, out = 0.0, 0.0
    for k, here in scores:
        p = jnp.exp(s_ref[:, here] - peak)
        keep = mask(i, k)
        if keep is not None:
            p = jnp.where(keep, p, 0.0)
        total = total + jnp.sum(p, -1, keepdims=True)
        out = out + jnp.dot(p.astype(BF), value_of(k), preferred_element_type=F32)
    return out / total, peak + jnp.log(total)


def attention_backward(i, prompt_runs, mask, q_ref, do_ref, key, value_of, out, lse, turn_ref, sum_ref):
    by_rows = (((1,), (1,)), ((), ()))
    by_tokens = (((0,), (0,)), ((), ()))

    def dot(a, b, dims=(((1,), (0,)), ((), ()))):
        return lax.dot_general(a, b, dims, preferred_element_type=F32)

    q, do = q_ref[i], do_ref[i]
    delta = jnp.sum(out * do.astype(F32), -1, keepdims=True)
    dq = 0.0
    for k in pieces_of(i, prompt_runs):
        keys = key(k)
        p = jnp.exp(dot(q, keys, by_rows) - lse)
        keep = mask(i, k)
        if keep is not None:
            p = jnp.where(keep, p, 0.0)
        ds = (p * (dot(do, value_of(k), by_rows) - delta)).astype(BF)
        dq = dq + dot(ds, keys)
        dk = dot(ds, q, by_tokens)
        dv = dot(p.astype(BF), do, by_tokens)
        if i == k:
            sum_ref[k, :, :HEAD_DIM] = dk
            sum_ref[k, :, HEAD_DIM:] = dv
        else:
            sum_ref[k, :, :HEAD_DIM] = sum_ref[k, :, :HEAD_DIM] + dk
            sum_ref[k, :, HEAD_DIM:] = sum_ref[k, :, HEAD_DIM:] + dv
    dq = (dq * (1.0 / math.sqrt(HEAD_DIM))).astype(BF).astype(F32)
    return turn(dq, [turn_ref[t, i] for t in range(3)], -1.0)


def attention_kernel(prompt_runs, one_prompt, q_ref, do_ref, kv_ref, row_ref, col_ref, turn_ref,
                     o_ref, dq_ref, dkv_ref, s_ref, sum_ref):
    def mask(i, k):
        rows, cols = row_ref[i], col_ref[k]
        if i == k:
            return (rows[:, 1:2] == cols[1:2, :]) & (cols[0:1, :] <= rows[:, 0:1])
        if one_prompt:
            return None
        return rows[:, 2:3] == cols[2:3, :]

    def key(k):
        return kv_ref[k, :, :HEAD_DIM]

    def value_of(k):
        return kv_ref[k, :, HEAD_DIM:]

    for i in range(q_ref.shape[0]):
        out, lse = attention_forward(i, prompt_runs, mask, q_ref, key, value_of, s_ref)
        o_ref[i] = out.astype(BF)
        back = attention_backward(
            i, prompt_runs, mask, q_ref, do_ref, key, value_of, out, lse, turn_ref, sum_ref
        )
        dq_ref[i] = back.astype(BF)
    dkv_ref[...] = sum_ref[...].astype(BF)


def attention(prompt_runs, one_prompt, queries, d_out, pairs, row_meta, col_meta, tables):
    m = queries.shape[1]
    count = pairs.shape[1]
    return pl.pallas_call(
        functools.partial(attention_kernel, prompt_runs, one_prompt),
        out_shape=(
            jax.ShapeDtypeStruct(queries.shape, BF),
            jax.ShapeDtypeStruct(queries.shape, BF),
            jax.ShapeDtypeStruct(pairs.shape, BF),
        ),
        in_specs=[VMEM] * 6,
        out_specs=(VMEM,) * 3,
        scratch_shapes=[pltpu.VMEM((m, (prompt_runs + 1) * count), F32), pltpu.VMEM(pairs.shape, F32)],
        compiler_params=pltpu.CompilerParams(vmem_limit_bytes=60 * 2**20),
    )(queries, d_out, pairs, row_meta, col_meta, tables)


def angles_of(positions):
    frequency = 10000.0 ** (-jnp.arange(0, ROT, 2, dtype=F32) / ROT)
    return positions.astype(F32)[:, None] * frequency[None, :]


def rotate(values, cosine, sine):
    half = ROT // 2
    leading, behind = values[:, :half], values[:, half:ROT]
    return jnp.concatenate(
        [leading * cosine - behind * sine, behind * cosine + leading * sine, values[:, ROT:]], -1
    )


def per_device(
    inputs, attn_norm_gain, attn_norm_bias, mlp_norm_gain, mlp_norm_bias, qkv_weight, qkv_bias, dense_weight,
    dense_bias, expand_weight, expand_bias, shrink_weight, shrink_bias, token_of_row, cont_parent, position_ids,
    cotangent,
):
    heads, blocks = lax.axis_size("head"), lax.axis_size("blk")
    devices = heads * blocks
    ways = blocks // (2 * HEADS)
    assert heads == 2 and blocks == ways * 2 * HEADS
    x = lax.axis_index("head")
    b = lax.axis_index("blk")
    me = x * blocks + b
    c, h, w = b % 2, (b // 2) % HEADS, b // (2 * HEADS)
    tok_dev, width = inputs.shape
    rows = qkv_weight.shape[0]
    hidden = expand_weight.shape[1] // HEADS
    runs = tok_dev // STRIPE
    run_size = devices * STRIPE
    prompt_total = token_of_row.shape[0] - cont_parent.shape[0] * CONT
    prompt_runs = prompt_total // run_size
    one_prompt = prompt_total == PROMPT
    assert prompt_runs * run_size == prompt_total
    group_rows = runs * HEADS * STRIPE
    head3 = 3 * HEAD_DIM
    block_columns = head3 + hidden

    by_device = token_of_row.reshape(devices, tok_dev)
    run_of = by_device // run_size
    big = jnp.int32(2**30)
    each_run = jnp.arange(runs, dtype=jnp.int32)
    base = jnp.min(jnp.where(run_of[:, :, None] == each_run, by_device[:, :, None], big), 1)
    mine = lax.dynamic_index_in_dim(by_device, me, 0, False)
    sorted_at = mine // run_size * STRIPE + mine % STRIPE
    pick = (sorted_at[None, :] == jnp.arange(tok_dev, dtype=jnp.int32)[:, None]).astype(BF)
    base_position = jnp.min(
        jnp.where((mine // run_size)[:, None] == each_run, position_ids[:, None], big), 0
    )

    def ordered(rows_in):
        return jnp.dot(pick, rows_in, preferred_element_type=F32).astype(BF)

    def restored(rows_in):
        return lax.dot_general(pick, rows_in, (((0,), (0,)), ((), ())), preferred_element_type=F32).astype(BF)

    states = ordered(inputs).astype(F32)
    grad_low = ordered(cotangent)
    grad_out = grad_low.astype(F32)
    average = jnp.mean(states, -1, keepdims=True)
    centered = states - average
    inverse_spread = lax.rsqrt(jnp.mean(centered * centered, -1, keepdims=True) + 1e-05)
    normed = centered * inverse_spread
    normed_low = normed.astype(BF)

    gain_one, shift_one = attn_norm_gain.astype(F32), attn_norm_bias.astype(F32)
    gain_two, shift_two = mlp_norm_gain.astype(F32), mlp_norm_bias.astype(F32)
    qkv_wide, expand_wide = qkv_weight.astype(F32), expand_weight.astype(F32)

    def split_qkv(values):
        return values.reshape(-1, 3, HEADS, HEAD_DIM).transpose(2, 0, 1, 3).reshape(HEADS, -1, head3)

    def split(values):
        return values.reshape(values.shape[0], HEADS, -1).transpose(1, 0, 2)

    weights = jnp.concatenate(
        [
            split_qkv((qkv_wide * gain_one[:, None]).astype(BF)),
            split((expand_wide * gain_two[:, None]).astype(BF)),
            split(dense_weight),
            split(shrink_weight),
        ],
        -1,
    )
    own_qkv_bias = lax.dynamic_update_slice_in_dim(
        jnp.zeros((3 * width,), F32), qkv_bias.astype(F32), me * qkv_bias.shape[0], 0
    )
    own_expand_bias = lax.dynamic_update_slice_in_dim(
        jnp.zeros((HEADS * hidden,), F32), expand_bias.astype(F32), me * expand_bias.shape[0], 0
    )
    bias_parts = jnp.concatenate(
        [
            split_qkv((jnp.sum(qkv_wide * shift_one[:, None], 0) + own_qkv_bias)[None])[:, 0],
            split((jnp.sum(expand_wide * shift_two[:, None], 0) + own_expand_bias)[None])[:, 0],
        ],
        -1,
    )
    lanes = 128
    note_rows = block_columns // lanes

    slice_rows = width // lanes
    own_out_bias = lax.dynamic_update_slice_in_dim(
        jnp.zeros((width,), F32), dense_bias.astype(F32) + shrink_bias.astype(F32), me * rows, 0
    )
    notes = jnp.concatenate(
        [
            bias_parts.reshape(HEADS, note_rows, lanes),
            jnp.broadcast_to(own_out_bias.reshape(1, slice_rows, lanes), (HEADS, slice_rows, lanes)),
            jnp.zeros((HEADS, -(note_rows + slice_rows) % 8, lanes), F32),
        ],
        1,
    )

    def trig_of(positions):
        angles = angles_of(positions)
        cosine, sine = jnp.cos(angles), jnp.sin(angles)
        rest = ((0, 0), (0, lanes - ROT))
        return jnp.stack(
            [
                jnp.pad(jnp.concatenate([cosine, cosine], 1), rest, constant_values=1.0),
                jnp.pad(jnp.concatenate([sine, sine], 1), rest),
            ]
        )

    within = jnp.arange(STRIPE, dtype=jnp.int32)
    rows_run = group_rows // runs

    bases = base.reshape(2, ways, HEADS, 2, runs)
    own_base = lax.dynamic_index_in_dim(bases, x, 0, False)
    own_base = lax.dynamic_index_in_dim(own_base, w, 0, False)
    own_base = lax.dynamic_index_in_dim(own_base, c, 1, False)
    row_tokens = (own_base.T[:, :, None] + within).reshape(runs, rows_run)
    col_tokens = (bases.transpose(4, 1, 0, 3, 2)[..., None] + within).reshape(runs, run_size)

    fuse, opened = open_all(
        ways, rows, hidden, prompt_runs, prompt_total,
        normed_low.reshape(runs, STRIPE, width), grad_low.reshape(runs, STRIPE, width), weights, notes,
        trig_of(base_position), trig_of(within), row_tokens[:, :, None], col_tokens[:, None, :],
    )
    n_all, g_all, w_all, note, tables = opened[:5]
    w_all = w_all.reshape(width, w_all.shape[-1])
    bias_block = note[:note_rows].reshape(block_columns)
    out_bias = note[note_rows : note_rows + slice_rows].reshape(width)
    if fuse:
        left, right, half, part = opened[5:]
    else:
        n_all, g_all = n_all.reshape(group_rows, width), g_all.reshape(group_rows, width)
        flat = tables.reshape(3, group_rows, lanes)
        cosine, sine = flat[0, :, : ROT // 2], flat[2, :, ROT // 2 : ROT]
        w_in, w_out = w_all[:, :block_columns], w_all[:, block_columns:]
        mixed = jnp.dot(n_all, w_in[:, :head3], preferred_element_type=F32) + bias_block[:head3]
        queries = (rotate(mixed[:, :HEAD_DIM], cosine, sine) * (1.0 / math.sqrt(HEAD_DIM))).astype(BF)
        keys = rotate(mixed[:, HEAD_DIM : 2 * HEAD_DIM], cosine, sine).astype(BF)
        values = mixed[:, 2 * HEAD_DIM :].astype(BF)
        pairs = exchange(ways, jnp.concatenate([keys, values], 1).reshape(runs, rows_run, 2 * HEAD_DIM))
        pairs = pairs.reshape(runs, run_size, 2 * HEAD_DIM)
        d_attended = jnp.dot(g_all, w_out[:, :HEAD_DIM], preferred_element_type=F32).astype(BF)
        expanded = jnp.dot(n_all, w_in[:, head3:], preferred_element_type=F32) + bias_block[head3:]
        activated, gelu_back = jax.vjp(lambda v: jax.nn.gelu(v, approximate=False), expanded)
        activated = activated.astype(BF)
        d_activated = jnp.dot(g_all, w_out[:, HEAD_DIM:], preferred_element_type=F32)
        d_expanded = gelu_back(d_activated)[0].astype(BF)

        def meta(tokens):
            is_prompt = tokens < prompt_total
            cont = (tokens - prompt_total) // CONT
            matches = cont[..., None] == jnp.arange(cont_parent.shape[0], dtype=jnp.int32)
            prompt = jnp.where(is_prompt, tokens // PROMPT, jnp.sum(jnp.where(matches, cont_parent, 0), -1))
            segment = jnp.where(is_prompt, -1 - tokens // PROMPT, cont)
            return tokens, segment, prompt

        attended, d_queries, d_pairs = attention(
            prompt_runs, one_prompt,
            queries.reshape(runs, rows_run, HEAD_DIM), d_attended.reshape(runs, rows_run, HEAD_DIM),
            pairs, jnp.stack(meta(row_tokens), -1), jnp.stack(meta(col_tokens), 1), tables,
        )
        attended = attended.reshape(group_rows, HEAD_DIM)

        left = jnp.concatenate([attended, activated], 1)
        part = lax.dot_general(left, w_out, (((1,), (1,)), ((), ())), preferred_element_type=F32)
        part = part.reshape(runs, HEADS, STRIPE, width)
        others = [[w2 * 2 * HEADS + h2 * 2 + c2 for h2 in range(HEADS)] for w2 in range(ways) for c2 in range(2)]
        out_rows = lax.psum_scatter(part, "blk", scatter_dimension=1, axis_index_groups=others, tiled=True)[:, 0]
        half = part = None
        n_all, g_all = n_all.T, g_all.T
        d_pairs = d_pairs.astype(F32).reshape(runs, ways, 2, 2, rows_run, 2 * HEAD_DIM).transpose(1, 3, 2, 0, 4, 5)
        d_pairs = d_pairs.reshape(2 * ways, 2, runs, rows_run, 2 * HEAD_DIM)
        alike = [[w2 * 2 * HEADS + h2 * 2 + c2 for w2 in range(ways) for c2 in range(2)] for h2 in range(HEADS)]
        d_pairs = lax.psum_scatter(d_pairs, "blk", scatter_dimension=0, axis_index_groups=alike, tiled=True)[0]
        d_pairs = lax.psum_scatter(d_pairs, "head", scatter_dimension=0, tiled=True)
        d_pairs = d_pairs.reshape(group_rows, 2 * HEAD_DIM)
        d_keys = rotate(d_pairs[:, :HEAD_DIM].astype(BF).astype(F32), cosine, -sine).astype(BF)
        right = jnp.concatenate(
            [d_queries.reshape(group_rows, HEAD_DIM), d_keys, d_pairs[:, HEAD_DIM:].astype(BF), d_expanded], 1
        )

    own_sums = jnp.sum(grad_out, 0).reshape(width // lanes, lanes)
    sum_note = jnp.concatenate(
        [jnp.zeros((note_rows, lanes), F32), own_sums, jnp.zeros((-(note_rows + width // lanes) % 8, lanes), F32)]
    )
    out_sum, e_sum, owned_a, owned_b, owned_notes = finish(
        ways, rows, left, right, w_all, n_all, g_all, sum_note, half, part
    )
    if not fuse:
        out_sum = out_rows
    output = restored((states + out_sum.reshape(tok_dev, width) + out_bias).astype(BF))
    e_sum = e_sum.reshape(tok_dev, width)
    dx = inverse_spread * (
        e_sum - jnp.mean(e_sum, -1, keepdims=True) - normed * jnp.mean(e_sum * normed, -1, keepdims=True)
    )
    input_grad = restored((grad_out + dx).astype(BF))
    owned_a, owned_b = owned_a.astype(F32), owned_b.astype(F32)

    def join_qkv(values):
        return values.reshape(HEADS, -1, 3, HEAD_DIM).transpose(1, 2, 0, 3).reshape(-1, 3 * width)

    def join(values):
        return values.transpose(1, 0, 2).reshape(values.shape[1], -1)

    raw_qkv = join_qkv(owned_b)
    dense_grad = join(owned_a[..., :HEAD_DIM])
    shrink_grad = join(owned_a[..., HEAD_DIM : HEAD_DIM + hidden])
    raw_expand = join(owned_a[..., HEAD_DIM + hidden :])
    column_sums = owned_notes[:, :note_rows].reshape(HEADS, 1, block_columns)
    qkv_sum = join_qkv(column_sums[..., :head3])
    expand_sum = join(column_sums[..., head3:])
    all_sums = jnp.sum(owned_notes[:, note_rows : note_rows + width // lanes], 0).reshape(width)
    bias_grad = lax.dynamic_slice_in_dim(all_sums, me * rows, rows, 0)
    qkv_grad = gain_one[:, None] * raw_qkv + shift_one[:, None] * qkv_sum
    expand_grad = gain_two[:, None] * raw_expand + shift_two[:, None] * expand_sum

    def own(values, count):
        return lax.dynamic_slice_in_dim(values, me * count, count, 0)

    return (
        output,
        input_grad,
        jnp.sum(qkv_wide * raw_qkv, 1),
        jnp.sum(qkv_wide * qkv_sum, 1),
        jnp.sum(expand_wide * raw_expand, 1),
        jnp.sum(expand_wide * expand_sum, 1),
        qkv_grad,
        own(qkv_sum[0, : 2 * width], 2 * width // devices),
        own(qkv_sum[0, 2 * width :], width // devices),
        dense_grad,
        bias_grad,
        expand_grad,
        own(expand_sum[0], HEADS * hidden // devices),
        shrink_grad,
        bias_grad,
    )


def solution(mesh):
    matrix, vector = P(("head", "blk"), None), P(("head", "blk"))
    return jax.shard_map(
        per_device,
        mesh=mesh,
        in_specs=(
            matrix, vector, vector, vector, vector, matrix, vector, matrix, vector, matrix, vector, matrix, vector,
            P(), P(), vector, matrix,
        ),
        out_specs=(
            matrix, matrix, vector, vector, vector, vector, matrix, vector, vector, matrix, vector, matrix, vector,
            matrix, vector,
        ),
        check_vma=False,
    )
```

```python
import functools
import math

import jax
import jax.numpy as jnp
import numpy as np
from jax import lax
from jax.experimental import pallas as pl
from jax.experimental.pallas import tpu as pltpu
from jax.sharding import PartitionSpec as P

HEADS = 8
HEAD_DIM = 256
ROT = 64
PROMPT = 2048
CONT = 256
STRIPE = 16
MESH = pl.DeviceIdType.MESH
BF = jnp.bfloat16
F32 = jnp.float32
ANY = pl.BlockSpec(memory_space=pl.ANY)
VMEM = pl.BlockSpec(memory_space=pltpu.VMEM)
DMA = pltpu.SemaphoreType.DMA


class Place:
    def __init__(self, ways):
        self.ways = ways
        self.x = lax.axis_index("head")
        b = lax.axis_index("blk")
        self.c = b % 2
        self.h = (b // 2) % HEADS
        self.w = b // (2 * HEADS)
        self.hy = self.h % 2
        self.hz = self.h // 2

    def device(self, x=None, w=None, h=None, c=None):
        x = self.x if x is None else x
        w = self.w if w is None else w
        h = self.h if h is None else h
        c = self.c if c is None else c
        return (x, w * (2 * HEADS) + h * 2 + c)

    def peers_h(self):
        return [self.device(h=(self.h + k) % HEADS) for k in range(1, HEADS)]

    def peers_w(self):
        return [self.device(w=(self.w + k) % self.ways) for k in range(1, self.ways)]

    def peer_x(self):
        return self.device(x=1 - self.x)

    def peer_c(self):
        return self.device(c=1 - self.c)

    def peer_y(self):
        return self.device(h=self.h + 1 - 2 * self.hy)


def greet(devices):
    barrier = pltpu.get_barrier_semaphore()
    for one in devices:
        pl.semaphore_signal(barrier, inc=1, device_id=one, device_id_type=MESH)
    pl.semaphore_wait(barrier, len(devices))


def remote(src, dst, send, recv, device):
    return pltpu.make_async_remote_copy(
        src_ref=src, dst_ref=dst, send_sem=send, recv_sem=recv, device_id=device, device_id_type=MESH
    )


def call(body, out_shape, ins, scratch, ident, out_spec=ANY, in_spec=ANY):
    return pl.pallas_call(
        body,
        out_shape=out_shape,
        in_specs=[in_spec] * len(ins),
        out_specs=jax.tree.map(lambda _: out_spec, out_shape),
        scratch_shapes=scratch,
        compiler_params=pltpu.CompilerParams(
            collective_id=ident, has_side_effects=True, vmem_limit_bytes=60 * 2**20
        ),
    )(*ins)


LINE = HEADS // 2
A_ORDER = (0, 4, 1, 5, 2, 6, 3, 7)
EARLY = 2


def relay_rows(place, own, full, s, r):
    hz, hy = place.hz, place.hy
    d0, d1 = hz % 2, hz // 2

    def index(e1, e0, y):
        return (e1 * 2 + e0) * 2 + y

    far = place.device(h=index(1 - d1, d0, hy))
    near = place.device(h=index(d1, 1 - d0, hy))
    side = place.peer_y()
    made = []

    def push(src, idx, k, device):
        copy = remote(src, full.at[:, idx], s.at[k], r.at[idx], device)
        copy.start()
        made.append(copy)

    def arrived(idx):
        remote(full.at[:, idx], full.at[:, idx], s.at[0], r.at[idx], side).wait_recv()

    def first_z():
        push(own, place.h, 0, far)
        push(own, place.h, 1, near)

    def first_y():
        push(own, place.h, 2, side)

    def from_far():
        idx = index(1 - d1, d0, hy)
        arrived(idx)
        push(full.at[:, idx], idx, 3, near)
        push(full.at[:, idx], idx, 4, side)

    def from_near():
        idx = index(d1, 1 - d0, hy)
        arrived(idx)
        push(full.at[:, idx], idx, 5, side)

    def from_near_far():
        idx = index(1 - d1, 1 - d0, hy)
        arrived(idx)
        push(full.at[:, idx], idx, 6, side)

    def from_side():
        for z in range(LINE):
            arrived(z * 2 + 1 - hy)

    def sent():
        for copy in made:
            copy.wait_send()

    return first_z, first_y, from_far, from_near, from_near_far, from_side, sent


def open_kernel(ways, cuts, fuse, prompt_runs, prompt_total, *refs):
    names = ["x_in", "g_in", "tokens", "places", "gain_one", "shift_one", "gain_two", "shift_two", "qkv_bias", "expand_bias", "dense_bias", "shrink_bias", "freq_in", "step_in"]
    names += ["qkv_in", "expand_in", "dense_in", "shrink_in", "n_out", "g_out", "w_out", "note_out", "turn_out", "sums_out"]
    if fuse:
        names += ["left_out", "right_out", "half_out", "part_out"]
    names += ["v_n", "v_g", "v_w", "v_turn", "trig", "note", "note_c", "note_x", "note_w", "note_h", "own", "put"]
    names += ["v_qkv", "v_expand", "trig_own", "placed", "sums"]
    names += ["ns", "nr", "gs", "gr", "wa", "wr", "xs", "xr", "cs", "cr", "t_s", "t_r", "nc_s", "nc_r", "nx_s", "nx_r", "nw_s", "nw_r", "nh_s", "nh_r"]
    if fuse:
        names += ["v_q", "v_do", "v_kv", "v_slope", "v_left", "v_right", "v_out", "lse", "s_ref", "sum_ref", "kv_c", "kv_x", "o_p", "o_y", "flat", "flat_sem", "row_tok", "col_tok"]
        names += ["kx_s", "kx_r", "kc_s", "kc_r", "fc_s", "fc_r", "fx_s", "fx_r", "oy_s", "oy_r"]
    at = dict(zip(names, refs, strict=True))
    (step_in, n_out, g_out, w_out, turn_out, v_n, v_g, v_w, v_turn) = (
        at[k] for k in ["step_in", "n_out", "g_out", "w_out", "turn_out", "v_n", "v_g", "v_w", "v_turn"]
    )
    v_qkv, v_expand, trig_own, placed, sums = (at[k] for k in ["v_qkv", "v_expand", "trig_own", "placed", "sums"])
    trig, note, note_c, note_x, note_w, note_h, own, put = (
        at[k] for k in ["trig", "note", "note_c", "note_x", "note_w", "note_h", "own", "put"]
    )
    place = Place(ways)
    x, w, h, c = place.x, place.w, place.h, place.c
    runs = v_n.shape[0]
    width = v_n.shape[-1]
    per_run = HEADS * STRIPE
    stage_a = [(dw, dh) for dw in range(ways) for dh in range(HEADS) if (dw, dh) != (0, 0)]
    sends, puts = [], []

    def send(src, dst, s, r, device):
        copy = remote(src, dst, s, r, device)
        copy.start()
        sends.append(copy)
        return copy

    def save(src, dst):
        copy = pltpu.make_async_copy(src, dst, put.at[len(puts)])
        copy.start()
        puts.append(copy)

    devices, rows = at["tokens"].shape[0], v_qkv.shape[0]
    hidden = v_expand.shape[1] // HEADS
    run_size = devices * STRIPE
    me = x * (2 * HEADS * ways) + w * (2 * HEADS) + h * 2 + c
    raw = [
        pltpu.make_async_copy(at["qkv_in"], v_qkv, own.at[0]),
        pltpu.make_async_copy(at["expand_in"], v_expand, own.at[1]),
    ]
    for copy in raw:
        copy.start()
    mine = at["tokens"][pl.ds(me, 1), :]
    mine_run = mine // run_size
    tok_dev = mine.shape[1]
    pick = lax.broadcasted_iota(jnp.int32, (tok_dev, tok_dev), 0) == mine_run * STRIPE + mine % STRIPE
    pick = jnp.where(pick, 1.0, 0.0).astype(BF)

    def ordered(ref):
        return jnp.dot(pick, ref[...], preferred_element_type=F32)

    states = ordered(at["x_in"])
    centered = states - jnp.mean(states, -1, keepdims=True)
    normed = centered * lax.rsqrt(jnp.mean(centered * centered, -1, keepdims=True) + 1e-05)
    v_n[:, pl.ds(h, 1)] = normed.astype(BF).reshape(runs, 1, STRIPE, width)
    grads = ordered(at["g_in"])
    v_g[:, pl.ds(h, 1)] = grads.astype(BF).reshape(runs, 1, STRIPE, width)
    sums[...] = jnp.zeros_like(sums)
    g_sum = jnp.sum(grads, 0, keepdims=True)
    first_sum = (3 * HEAD_DIM + hidden) // 128
    for k in range(width // 128):
        sums[first_sum + k : first_sum + k + 1, :] = g_sum[:, k * 128 : (k + 1) * 128]
    far_off = jnp.int32(2**30)
    for k in range(runs):
        start = jnp.min(jnp.where(mine_run == k, at["places"][...], far_off), 1, keepdims=True)
        angle = start.astype(F32) * at["freq_in"][...]
        turned = lax.broadcasted_iota(jnp.int32, angle.shape, 1) < ROT
        trig_own[0, k : k + 1] = jnp.where(turned, jnp.cos(angle), 1.0)
        trig_own[1, k : k + 1] = jnp.where(turned, jnp.sin(angle), 0.0)

    def share_of(name):
        return at[name][...].astype(F32).reshape(1, at[name].shape[0])

    def place_share(value, first):
        count = value.shape[1]
        span = -(-count // 128) * 128 + 128
        value = jnp.concatenate([value, jnp.zeros((1, span - count), F32)], 1)
        value = pltpu.roll(value, (me * count) % 128, 1)
        for k in range(span // 128):
            placed[pl.ds(first + me * count // 128 + k, 1), :] = value[:, k * 128 : (k + 1) * 128]

    placed[...] = jnp.zeros_like(placed)
    q_rows, e_rows, o_rows = 3 * width // 128, HEADS * hidden // 128, width // 128
    place_share(share_of("qkv_bias"), 0)
    place_share(share_of("expand_bias"), q_rows + 1)
    place_share(share_of("dense_bias") + share_of("shrink_bias"), q_rows + e_rows + 2)
    square = lax.broadcasted_iota(jnp.int32, (rows, rows), 0) == lax.broadcasted_iota(jnp.int32, (rows, rows), 1)
    note[...] = jnp.zeros_like(note)

    def spread(weight, gain, shift, step, put_rows):
        diagonal = jnp.where(square, gain, 0.0).astype(BF)
        for at_col in range(0, weight.shape[1], step):
            value = weight[:, at_col : at_col + step]
            through = jnp.dot(jnp.broadcast_to(shift, (16, rows)).astype(BF), value, preferred_element_type=F32)
            weight[:, at_col : at_col + step] = jnp.dot(diagonal, value, preferred_element_type=F32).astype(BF)
            for k in range(step // 128):
                put_rows(at_col // 128 + k, through[:1, k * 128 : (k + 1) * 128])

    def qkv_row(k, value):
        third, rest = k // (q_rows // 3), k % (q_rows // 3)
        hh, kk = rest // (HEAD_DIM // 128), rest % (HEAD_DIM // 128)
        to = third * (HEAD_DIM // 128) + kk
        note[hh, to : to + 1] = value + placed[k : k + 1, :]

    def expand_row(k, value):
        hh, kk = k // (hidden // 128), k % (hidden // 128)
        to = 3 * HEAD_DIM // 128 + kk
        note[hh, to : to + 1] = value + placed[q_rows + 1 + k : q_rows + 2 + k, :]

    raw[0].wait()
    spread(v_qkv, share_of("gain_one"), share_of("shift_one"), 1024, qkv_row)
    raw[1].wait()
    spread(v_expand, share_of("gain_two"), share_of("shift_two"), 1024, expand_row)
    to = (3 * HEAD_DIM + hidden) // 128
    first = q_rows + e_rows + 2
    note[:, to : to + o_rows] = jnp.broadcast_to(placed[first : first + o_rows][None], (HEADS, o_rows, 128))
    greet(
        [place.device(w=(w + dw) % ways, h=(h + dh) % HEADS) for dw, dh in stage_a]
        + [place.peer_x(), place.peer_c()]
    )

    def share(g, hs):
        first, count = cuts[g]
        if g < 3:
            return v_qkv.at[:, pl.ds(pl.multiple_of(g * width + hs * HEAD_DIM, 256), count)]
        if g == 3:
            return v_expand.at[:, pl.ds(pl.multiple_of(hs * hidden, 256), count)]
        if g == 4:
            return at["dense_in"].at[:, pl.ds(pl.multiple_of(hs * HEAD_DIM, 256), count)]
        return at["shrink_in"].at[:, pl.ds(pl.multiple_of(hs * hidden + (g - 5) * count, 256), count)]

    kept = [
        pltpu.make_async_copy(share(g, h), v_w.at[x, w, h, c, :, pl.ds(*cuts[g])], own.at[2 + g]) for g in range(len(cuts))
    ]
    trig_kept = pltpu.make_async_copy(trig_own, trig.at[h], own.at[2 + len(cuts)])
    for copy in kept + [trig_kept]:
        copy.start()
    n_in, g_in = v_n.at[:, h], v_g.at[:, h]
    save(sums, at["sums_out"])
    n_first_z, n_first_y, n_far, n_near, n_last, n_side, n_sent = relay_rows(place, n_in, v_n, at["ns"], at["nr"])
    g_first_z, g_first_y, g_far, g_near, g_last, g_side, g_sent = relay_rows(place, g_in, v_g, at["gs"], at["gr"])
    wa, wr, xs, xr, cs, cr = (at[k] for k in ["wa", "wr", "xs", "xr", "cs", "cr"])

    def columns(g):
        return pl.ds(cuts[g][0], cuts[g][1])

    def w_first(g, odd):
        for k, (dw, dh) in enumerate(stage_a):
            if dh % 2 != odd:
                continue
            h2 = (h + dh) % HEADS
            send(share(g, h2), v_w.at[x, w, h, c, :, columns(g)], wa.at[g, k], wr.at[g, w, h],
                 place.device(w=(w + dw) % ways, h=h2))

    def w_across(g):
        for dw, dh in stage_a:
            ws, hs = (w - dw) % ways, (h - dh) % HEADS
            spot = v_w.at[x, ws, hs, c, :, columns(g)]
            remote(spot, spot, wa.at[g, 0], wr.at[g, ws, hs], place.peer_x()).wait_recv()
        kept[g].wait()
        block = v_w.at[x, :, :, c, :, columns(g)]
        send(block, block, xs.at[g], xr.at[g], place.peer_x())
        send(block, block, cs.at[g, 0], cr.at[g, 0], place.peer_c())

    def w_beside(g):
        block = v_w.at[1 - x, :, :, c, :, columns(g)]
        remote(block, block, xs.at[g], xr.at[g], place.peer_x()).wait_recv()
        send(block, block, cs.at[g, 1], cr.at[g, 1], place.peer_c())

    def w_ready(g):
        for k, xx in ((0, x), (1, 1 - x)):
            block = v_w.at[xx, :, :, 1 - c, :, columns(g)]
            remote(block, block, cs.at[g, k], cr.at[g, k], place.peer_c()).wait_recv()
        if cuts[g][0] < w_out.shape[-1]:
            save(v_w.at[..., columns(g)], w_out.at[..., columns(g)])

    plan = []

    def step(time, body, *given):
        plan.append((time, len(plan), body, given))

    state = {}

    def trig_send():
        for k in range(1, HEADS):
            send(trig_own, trig.at[h], at["t_s"].at[k], at["t_r"].at[h], place.device(h=(h + k) % HEADS))

    def note_first():
        state["note"] = send(note, note_c, at["nc_s"].at[0], at["nc_r"].at[0], place.peer_c())

    def note_cross():
        state["note"].wait_recv()
        note_c[...] = note_c[...] + note[...]
        state["note"] = send(note_c, note_x, at["nx_s"].at[0], at["nx_r"].at[0], place.peer_x())

    def note_out():
        state["note"].wait_recv()
        note_x[...] = note_x[...] + note_c[...]
        summed = note_x
        if ways > 1:
            crossed = [
                send(note_x, note_w.at[k], at["nw_s"].at[k], at["nw_r"].at[k], device)
                for k, device in enumerate(place.peers_w())
            ]
            for copy in crossed:
                copy.wait_recv()
            total = note_x[...]
            for k in range(ways - 1):
                total = total + note_w[k]
            state["note"].wait_send()
            sends[:] = [one for one in sends if one is not state["note"]]
            note_c[...] = total
            summed = note_c
        for k in range(1, HEADS):
            h2 = (h + k) % HEADS
            send(summed.at[h2], note_h.at[h], at["nh_s"].at[k], at["nh_r"].at[h], place.device(h=h2))
        state["summed"] = summed

    def note_sum():
        bias = state["summed"][h]
        for k in range(1, HEADS):
            hs = (h - k) % HEADS
            remote(note_h.at[hs], note_h.at[hs], at["nh_s"].at[k], at["nh_r"].at[hs], place.peer_x()).wait_recv()
            bias = bias + note_h[hs]
        note_h[h] = bias
        save(note_h.at[h], at["note_out"])

    def turn_tables():
        trig_kept.wait()
        for k in range(1, HEADS):
            hs = (h - k) % HEADS
            remote(trig.at[hs], trig.at[hs], at["t_s"].at[k], at["t_r"].at[hs], place.peer_x()).wait_recv()
        lane = lax.broadcasted_iota(jnp.int32, (STRIPE, 128), 1)
        for hh in range(HEADS):
            @pl.loop(0, runs)
            def _(run):
                cosine, sine = trig[hh, 0, pl.ds(run, 1)], trig[hh, 1, pl.ds(run, 1)]
                full = sine * step_in[0] + cosine * step_in[1]
                here = pl.ds(hh * STRIPE, STRIPE)
                v_turn[0, run, here] = cosine * step_in[0] - sine * step_in[1]
                v_turn[1, run, here] = jnp.where(lane < ROT // 2, -full, 0.0)
                v_turn[2, run, here] = jnp.where(lane < ROT // 2, 0.0, full)
        if not fuse:
            save(v_turn, turn_out)

    def rows_done(side, src, dst):
        side()
        if not fuse:
            save(src, dst)

    flipped = []

    def flip(src, dst, t):
        spot = at["flat"].at[len(flipped) % 2]
        if len(flipped) >= 2:
            flipped[-2].wait()
        spot[...] = src[..., t * 256 : (t + 1) * 256].reshape(runs * per_run, 256).T
        copy = pltpu.make_async_copy(spot, dst.at[t * 256 : (t + 1) * 256], at["flat_sem"].at[len(flipped) % 2])
        copy.start()
        flipped.append(copy)

    expand_at, dense_at = 3, 4
    shrink = list(range(5, len(cuts)))
    step(0, trig_send)
    step(0.01, n_first_z)
    step(0.01, n_first_y)
    for k in range(3):
        step(0.02, w_first, k, 1)
        step(0.02, w_first, k, 0)
    step(0.2, note_first)
    step(3, note_cross)
    step(6, note_out)
    for k in range(3):
        step(31 + 4 * k, w_across, k)
        step(43 + 5 * k, w_beside, k)
        step(66, w_ready, k)
    step(16, n_near)
    step(27, n_far)
    step(36.1, w_first, expand_at, 0)
    step(52, n_last)
    step(52.1, w_first, expand_at, 1)
    step(52.2, w_first, dense_at, 1)
    step(52.3, w_first, dense_at, 0)
    step(52.4, g_first_z)
    step(52.5, g_first_y)
    step(55, turn_tables)
    step(57, note_sum)
    step(65, rows_done, n_side, v_n, n_out)
    step(75.5, w_across, expand_at)
    step(86, w_across, dense_at)
    step(86.1, g_near)
    step(98, g_far)
    for g in shrink:
        step(98.1, w_first, g, 1)
        step(98.2, w_first, g, 0)
    step(112, w_beside, expand_at)
    step(113, w_ready, expand_at)
    step(117.7, g_last)
    step(121.5, w_beside, dense_at)
    step(134, rows_done, g_side, v_g, g_out)
    step(134.1, w_ready, dense_at)
    for k, g in enumerate(shrink):
        step((117.6, 117.72, 117.83, 117.95)[k], w_across, g)
        step((135.6, 142, 147, 152)[k], w_beside, g)
        step(156, w_ready, g)
    if fuse:
        v_q, v_do, v_kv, v_slope, v_left, v_right, v_out, lse, s_ref, sum_ref, kv_c, kv_x, o_p, o_y = (
            at[k] for k in ["v_q", "v_do", "v_kv", "v_slope", "v_left", "v_right", "v_out", "lse", "s_ref", "sum_ref", "kv_c", "kv_x", "o_p", "o_y"]
        )
        kx_s, kx_r, kc_s, kc_r = (at[k] for k in ["kx_s", "kx_r", "kc_s", "kc_r"])
        kv_sends = []
        tile = 256

        def weight(first):
            return v_w[..., first : first + tile].reshape(width, tile)

        def bias_of(t):
            return jnp.concatenate([note_h[h, 2 * t : 2 * t + 1], note_h[h, 2 * t + 1 : 2 * t + 2]], 1)

        parts = 4
        span = runs // parts
        slot = x * 2 + c

        def project(p):
            lo = p * span
            left = v_n[lo : lo + span].reshape(span * per_run, width)
            tables = [v_turn[t, lo : lo + span].reshape(span * per_run, 128) for t in range(3)]
            for t in range(3):
                value = jnp.dot(left, weight(t * HEAD_DIM), preferred_element_type=F32) + bias_of(t)
                if t < 2:
                    value = turn(value, tables, 1.0)
                if t == 0:
                    v_q[lo : lo + span] = (value * (1.0 / math.sqrt(HEAD_DIM))).astype(BF).reshape(span, per_run, HEAD_DIM)
                else:
                    here = pl.ds((t - 1) * HEAD_DIM, HEAD_DIM)
                    v_kv[lo : lo + span, slot, :, here] = value.astype(BF).reshape(span, per_run, HEAD_DIM)
            block = v_kv.at[lo : lo + span, slot]
            kv_sends.append(send(block, block, kx_s.at[p], kx_r.at[p], place.peer_x()))
            kv_sends.append(send(block, block, kc_s.at[0, p], kc_r.at[0, p], place.peer_c()))

        def kv_beside(p):
            block = v_kv.at[pl.ds(p * span, span), (1 - x) * 2 + c]
            remote(block, block, kx_s.at[p], kx_r.at[p], place.peer_x()).wait_recv()
            kv_sends.append(send(block, block, kc_s.at[1, p], kc_r.at[1, p], place.peer_c()))

        def kv_ready(p):
            for k, xx in ((0, x), (1, 1 - x)):
                block = v_kv.at[pl.ds(p * span, span), xx * 2 + 1 - c]
                remote(block, block, kc_s.at[k, p], kc_r.at[k, p], place.peer_c()).wait_recv()

        half = runs * per_run // 2

        def expand(m, t):
            left = v_n[m * runs // 2 : (m + 1) * runs // 2].reshape(half, width)
            value = jnp.dot(left, weight(cuts[expand_at][0] + t * tile), preferred_element_type=F32) + bias_of(3 + t)
            sigma = 0.5 * (1.0 + lax.erf(value * math.sqrt(0.5)))
            slope = sigma + value * jnp.exp(-0.5 * value * value) * (1.0 / math.sqrt(2 * math.pi))
            v_slope[m * half : (m + 1) * half, t * tile : (t + 1) * tile] = slope
            first = HEAD_DIM + t * tile
            v_left[m * half : (m + 1) * half, first : first + tile] = (value * sigma).astype(BF)

        def shrink_back(m, t):
            left = v_g[m * runs // 2 : (m + 1) * runs // 2].reshape(half, width)
            value = jnp.dot(left, weight(cuts[shrink[0]][0] + t * tile), preferred_element_type=F32)
            value = value * v_slope[m * half : (m + 1) * half, t * tile : (t + 1) * tile]
            first = 3 * HEAD_DIM + t * tile
            v_right[m * half : (m + 1) * half, first : first + tile] = value.astype(BF)

        row_tok, col_tok = at["row_tok"], at["col_tok"]

        def token_tables():
            tokens = at["tokens"][...]
            starts = [
                jnp.min(jnp.where(tokens // run_size == k, tokens, far_off), 1, keepdims=True) for k in range(runs)
            ]
            base = jnp.concatenate(starts, 1)
            parts_of = [(base // 64).astype(F32).astype(BF), (base % 64).astype(F32).astype(BF)]
            row = lax.broadcasted_iota(jnp.int32, (per_run, devices), 0)
            owner = x * (2 * HEADS) + row // STRIPE * 2 + c
            pick_row = owner == lax.broadcasted_iota(jnp.int32, (per_run, devices), 1)
            pick_row = jnp.where(pick_row, 1.0, 0.0).astype(BF)
            lane = lax.broadcasted_iota(jnp.int32, (devices, 4 * per_run), 1)
            group = lane // per_run
            owner = group // 2 * (2 * HEADS) + lane % per_run // STRIPE * 2 + group % 2
            pick_col = owner == lax.broadcasted_iota(jnp.int32, (devices, 4 * per_run), 0)
            pick_col = jnp.where(pick_col, 1.0, 0.0).astype(BF)
            high, low = (jnp.dot(pick_row, part, preferred_element_type=F32) for part in parts_of)
            within = lax.broadcasted_iota(jnp.int32, (per_run, runs), 0) % STRIPE
            row_tok[...] = (high * 64 + low).astype(jnp.int32) + within
            turn_over = (((0,), (0,)), ((), ()))
            high, low = (
                lax.dot_general(part, pick_col, turn_over, preferred_element_type=F32) for part in parts_of
            )
            within = lax.broadcasted_iota(jnp.int32, (runs, 4 * per_run), 1) % STRIPE
            col_tok[...] = (high * 64 + low).astype(jnp.int32) + within

        step(74, token_tables)

        def segment(tokens):
            return jnp.where(tokens < prompt_total, -1 - tokens // PROMPT, (tokens - prompt_total) // CONT)

        def mask(i, k):
            if i != k:
                return None
            rows, cols = row_tok[:, i : i + 1], col_tok[i : i + 1, :]
            return (segment(rows) == segment(cols)) & (cols <= rows)

        def attended_back():
            for m in range(2):
                left = v_g[m * runs // 2 : (m + 1) * runs // 2].reshape(half, width)
                value = jnp.dot(left, weight(cuts[dense_at][0]), preferred_element_type=F32)
                v_do[m * runs // 2 : (m + 1) * runs // 2] = value.astype(BF).reshape(runs // 2, per_run, HEAD_DIM)

        def key(k):
            return v_kv[k, :, :, :HEAD_DIM].reshape(4 * per_run, HEAD_DIM)

        def value_of(k):
            return v_kv[k, :, :, HEAD_DIM:].reshape(4 * per_run, HEAD_DIM)

        def attend(i):
            here = slice(i * per_run, (i + 1) * per_run)
            out, total = attention_forward(i, prompt_runs, mask, v_q, key, value_of, s_ref)
            v_out[here], lse[:, i : i + 1] = out, total
            v_left[here, :HEAD_DIM] = out.astype(BF)

        def attend_back(i):
            here = slice(i * per_run, (i + 1) * per_run)
            back = attention_backward(
                i, prompt_runs, mask, v_q, v_do, key, value_of, v_out[here], lse[:, i : i + 1], v_turn, sum_ref
            )
            v_right[here, :HEAD_DIM] = back.astype(BF)

        def fold_first():
            for copy in kv_sends:
                copy.wait_send()
            sends[:] = [one for one in sends if not any(one is other for other in kv_sends)]
            v_kv[...] = sum_ref[...].astype(BF).reshape(v_kv.shape)
            for k, xx in ((0, 1 - x), (1, x)):
                state["fold", k] = send(
                    v_kv.at[:, xx * 2 + 1 - c], kv_c.at[:, k], at["fc_s"].at[k], at["fc_r"].at[k], place.peer_c()
                )

        def fold_add(k, final):
            state["fold", k].wait_recv()
            mine_slot = (x if k else 1 - x) * 2 + c

            @pl.loop(0, runs)
            def _(run):
                value = v_kv[run, mine_slot].astype(F32) + kv_c[run, k].astype(F32)
                if final:
                    value = value + kv_x[run].astype(F32)
                    back = turn(value[:, :HEAD_DIM].astype(BF).astype(F32), [v_turn[t, run] for t in range(3)], -1.0)
                    here = pl.ds(pl.multiple_of(run * per_run, per_run), per_run)
                    v_right[here, HEAD_DIM : 2 * HEAD_DIM] = back.astype(BF)
                    v_right[here, 2 * HEAD_DIM : 3 * HEAD_DIM] = value[:, HEAD_DIM:].astype(BF)
                else:
                    kv_c[run, k] = value.astype(BF)

        def fold_cross():
            fold_add(0, False)
            state["fold_x"] = send(kv_c.at[:, 0], kv_x, at["fx_s"].at[0], at["fx_r"].at[0], place.peer_x())

        def fold_close():
            state["fold_x"].wait_recv()
            fold_add(1, True)
            save(v_right.at[:, pl.ds(0, 3 * HEAD_DIM)], at["right_out"].at[:, pl.ds(0, 3 * HEAD_DIM)])

        chunks, early, wide = o_p.shape[0], o_y.shape[0], o_p.shape[-1]

        def out_part(q):
            for k in range(wide // tile):
                n = q * (wide // tile) + k
                per_x = width // 2 // tile
                low = n % per_x * HEADS // per_x
                some = v_w[n // per_x, 0, low : low + HEADS // per_x, :, :, cuts[dense_at][0] :]
                value = lax.dot_general(
                    v_left[...], some.reshape(tile, v_left.shape[1]), (((1,), (1,)), ((), ())), preferred_element_type=F32
                )
                o_p[q, :, :, :, :, :, k * tile : (k + 1) * tile] = value.astype(BF).reshape(runs, 2, 2, 2, STRIPE, tile)
            if q < early:
                state["out", q] = send(
                    o_p.at[q, :, :, :, 1 - place.hy], o_y.at[q], at["oy_s"].at[q], at["oy_r"].at[q], place.peer_y()
                )
            else:
                save(o_p.at[q], at["part_out"].at[q - early])

        def out_side(q):
            state["out", q].wait_recv()

            @pl.loop(0, runs)
            def _(run):
                for t in range(LINE):
                    value = o_y[q, run, t // 2, t % 2].astype(F32) + o_p[q, run, t // 2, t % 2, place.hy].astype(F32)
                    o_y[q, run, t // 2, t % 2] = value.astype(BF)

            save(o_y.at[q], at["half_out"].at[q])

        for p in range(parts):
            step(67 + 2 * p, project, p)
            step(80.5 + 6 * p, kv_beside, p)
            step(101, kv_ready, p)
        for i in range(runs):
            step(105.5 + 1.2 * i, attend, i)
            step(135 + 2 * i, attend_back, i)
            step(75, flip, v_n, n_out, i)
            step(163, flip, v_g, g_out, i)
        count = v_slope.shape[1] // tile
        for t in range(count):
            for m in range(2):
                step(117.51 + 0.1 * t + 0.05 * m, expand, m, t)
                step(161 + 0.1 * t, shrink_back, m, t)
        step(134.5, attended_back)
        step(151.5, fold_first)
        step(155, fold_cross)
        for q in range(chunks):
            step(156.5 + 0.1 * q if q < early else 162, out_part, q)
        for q in range(early):
            step(172 + 12 * q, out_side, q)
        step(157, save, v_left, at["left_out"])
        step(161.9, save, v_right.at[:, pl.ds(3 * HEAD_DIM, v_slope.shape[1])], at["right_out"].at[:, pl.ds(3 * HEAD_DIM, v_slope.shape[1])])
        step(183, fold_close)
    for _, _, body, given in sorted(plan, key=lambda one: one[:2]):
        body(*given)
    for copy in puts + flipped[-2:]:
        copy.wait()
    for copy in sends:
        copy.wait_send()
    n_sent()
    g_sent()


def open_all(ways, prompt_runs, prompt_total, inputs, cotangent, tokens, positions, scales, biases, qkv, expand, dense, shrink):
    tok_dev, width = inputs.shape
    rows, hidden = qkv.shape[0], expand.shape[1] // HEADS
    runs = tok_dev // STRIPE
    columns = 3 * HEAD_DIM + hidden + HEAD_DIM + hidden
    note_rows = -(-((3 * HEAD_DIM + hidden) // 128 + width // 128) // 8) * 8
    notes = jax.ShapeDtypeStruct((HEADS, note_rows, 128), F32)
    trig = jax.ShapeDtypeStruct((2, runs, 128), F32)

    frequency = np.float32(10000.0) ** (-np.arange(0, ROT, 2, dtype=np.float32) / np.float32(ROT))
    lanes_of = np.pad(np.concatenate([frequency, frequency]), (0, 128 - ROT))[None].astype(np.float32)
    step_angles = np.arange(STRIPE, dtype=np.float32)[:, None] * lanes_of
    turned = np.arange(128)[None] < ROT
    steps = np.stack([np.where(turned, np.cos(step_angles), 1.0), np.where(turned, np.sin(step_angles), 0.0)])
    lanes_of, steps = jnp.asarray(lanes_of), jnp.asarray(steps.astype(np.float32))
    fuse = ways == 1 and prompt_total == PROMPT
    head3 = 3 * HEAD_DIM
    cuts = [(k * HEAD_DIM, HEAD_DIM) for k in range(3)] + [(head3, hidden), (head3 + hidden, HEAD_DIM)]
    cuts += [(head3 + hidden + HEAD_DIM + k * 256, 256) for k in range(hidden // 256)]
    blocks = (2, ways, HEADS, 2, rows, columns)
    group = runs * HEADS * STRIPE
    per_run = HEADS * STRIPE

    def shape(dims, kind=BF):
        return jax.ShapeDtypeStruct(dims, kind)

    gathered = (runs, HEADS, STRIPE, width)
    tables = (3, runs, per_run, 128)
    chunks, wide = 4, width // 4
    kept = head3 + hidden if fuse else columns
    outs = [
        shape((width, group) if fuse else gathered), shape((width, group) if fuse else gathered), shape(blocks[:-1] + (kept,)), shape(notes.shape[1:], F32),
        shape((1, 1, 8, 128) if fuse else tables, F32), shape(notes.shape[1:], F32),
    ]
    if fuse:
        outs += [
            shape((group, HEAD_DIM + hidden)), shape((group, head3 + hidden)),
            shape((EARLY, runs, 2, 2, STRIPE, wide)), shape((chunks - EARLY, runs, 2, 2, 2, STRIPE, wide)),
        ]
    extra = max(ways - 1, 1)
    count = len(cuts)
    scratch = [
        pltpu.VMEM(gathered, BF), pltpu.VMEM(gathered, BF), pltpu.VMEM(blocks, BF), pltpu.VMEM(tables, F32),
        pltpu.VMEM((HEADS,) + trig.shape, F32),
        pltpu.VMEM(notes.shape, F32), pltpu.VMEM(notes.shape, F32), pltpu.VMEM(notes.shape, F32),
        pltpu.VMEM((extra,) + notes.shape if ways > 1 else (1, 1, 8, 128), F32), pltpu.VMEM(notes.shape, F32),
        DMA((3 + count,)), DMA((count + 15,)),
        pltpu.VMEM(qkv.shape, BF), pltpu.VMEM(expand.shape, BF), pltpu.VMEM(trig.shape, F32),
        pltpu.VMEM(((3 * width + HEADS * hidden + width) // 128 + 8, 128), F32), pltpu.VMEM(notes.shape[1:], F32),
        DMA((7,)), DMA((HEADS,)), DMA((7,)), DMA((HEADS,)),
        DMA((count, ways * HEADS)), DMA((count, ways, HEADS)), DMA((count,)), DMA((count,)), DMA((count, 2)), DMA((count, 2)),
        DMA((HEADS,)), DMA((HEADS,)), DMA((1,)), DMA((1,)), DMA((1,)), DMA((1,)), DMA((extra,)), DMA((extra,)),
        DMA((HEADS,)), DMA((HEADS,)),
    ]
    if fuse:
        scratch += [
            pltpu.VMEM((runs, per_run, HEAD_DIM), BF), pltpu.VMEM((runs, per_run, HEAD_DIM), BF),
            pltpu.VMEM((runs, 4, per_run, 2 * HEAD_DIM), BF), pltpu.VMEM((group, hidden), F32),
            pltpu.VMEM((group, HEAD_DIM + hidden), BF), pltpu.VMEM((group, head3 + hidden), BF),
            pltpu.VMEM((group, HEAD_DIM), F32), pltpu.VMEM((per_run, runs), F32),
            pltpu.VMEM((per_run, (prompt_runs + 1) * 4 * per_run), F32),
            pltpu.VMEM((runs, 4 * per_run, 2 * HEAD_DIM), F32),
            pltpu.VMEM((runs, 2, per_run, 2 * HEAD_DIM), BF), pltpu.VMEM((runs, per_run, 2 * HEAD_DIM), BF),
            pltpu.VMEM((chunks, runs, 2, 2, 2, STRIPE, wide), BF), pltpu.VMEM((EARLY, runs, 2, 2, STRIPE, wide), BF),
            pltpu.VMEM((2, 256, group), BF), DMA((2,)),
            pltpu.VMEM((per_run, runs), jnp.int32), pltpu.VMEM((runs, 4 * per_run), jnp.int32),
            DMA((4,)), DMA((4,)), DMA((2, 4)), DMA((2, 4)),
            DMA((2,)), DMA((2,)), DMA((1,)), DMA((1,)), DMA((EARLY,)), DMA((EARLY,)),
        ]
    return fuse, pl.pallas_call(
        functools.partial(open_kernel, ways, tuple(cuts), fuse, prompt_runs, prompt_total),
        out_shape=tuple(outs),
        in_specs=[VMEM] * 14 + [ANY] * 4,
        out_specs=(ANY,) * len(outs),
        scratch_shapes=scratch,
        compiler_params=pltpu.CompilerParams(collective_id=0, has_side_effects=True, vmem_limit_bytes=62 * 2**20),
    )(
        inputs, cotangent, tokens, positions, *scales, *biases, lanes_of, steps, qkv, expand, dense, shrink
    )


def exchange_kernel(ways, own, full, local, to_w, to_x, to_c, recv):
    place = Place(ways)
    x, w, c = place.x, place.w, place.c
    runs = own.shape[0]
    parts = 4
    span = runs // parts
    greet(place.peers_w() + [place.peer_x(), place.peer_c()])

    def spot(ws, xs, cs, p):
        return full.at[pl.ds(p * span, span), ws * 4 + xs * 2 + cs]

    sends = []

    def send(src, ws, xs, cs, p, sem, device):
        copy = remote(src, spot(ws, xs, cs, p), sem, recv.at[ws, xs, cs, p], device)
        copy.start()
        sends.append(copy)

    def arrived(ws, xs, cs, p):
        remote(spot(ws, xs, cs, p), spot(ws, xs, cs, p), local.at[0], recv.at[ws, xs, cs, p], place.peer_x()).wait_recv()

    keep = pltpu.make_async_copy(own, full.at[:, w * 4 + x * 2 + c], local.at[0])
    for p in range(parts):
        src = own.at[pl.ds(p * span, span)]
        for k, device in enumerate(place.peers_w()):
            send(src, w, x, c, p, to_w.at[k, p], device)
        send(src, w, x, c, p, to_x.at[w, p], place.peer_x())
    for p in range(parts):
        send(own.at[pl.ds(p * span, span)], w, x, c, p, to_c.at[w, x, p], place.peer_c())
    keep.start()
    for k in range(1, ways):
        ws = (w - k) % ways
        for p in range(parts):
            arrived(ws, x, c, p)
            send(spot(ws, x, c, p), ws, x, c, p, to_x.at[ws, p], place.peer_x())
            send(spot(ws, x, c, p), ws, x, c, p, to_c.at[ws, x, p], place.peer_c())
    for k in range(ways):
        ws = (w - k) % ways
        for p in range(parts):
            arrived(ws, 1 - x, c, p)
            send(spot(ws, 1 - x, c, p), ws, 1 - x, c, p, to_c.at[ws, 1 - x, p], place.peer_c())
    for k in range(ways):
        ws = (w - k) % ways
        for p in range(parts):
            arrived(ws, x, 1 - c, p)
            arrived(ws, 1 - x, 1 - c, p)
    keep.wait()
    for copy in sends:
        copy.wait_send()


def exchange(ways, own):
    runs, rows, columns = own.shape
    return call(
        functools.partial(exchange_kernel, ways),
        jax.ShapeDtypeStruct((runs, 4 * ways, rows, columns), BF),
        (own,),
        [DMA((1,)), DMA((ways, 4)), DMA((ways, 4)), DMA((ways, 2, 4)), DMA((ways, 2, 2, 4))],
        1,
    )


def turn(u, tables, sign):
    cosine, lower, upper = tables
    front = u[:, :128]
    moved = pltpu.roll(front, 96, 1) * lower + pltpu.roll(front, 32, 1) * upper
    return jnp.concatenate([front * cosine + moved * sign, u[:, 128:]], 1)


def finish_kernel(ways, early, left, right, w_all, n_all, g_all, note, half_in, part_in,
                  out_sum, e_sum, own_a, own_b, note_all,
                  v_left, v_right, v_w, o_own, o_y, o_1, o_2, e_p, e_y, e_1, e_2,
                  raw, ring, a_c, a_x, a_w, b_c, b_x, b_w, n_mine, n_c, n_x, n_w,
                  load, load_raw, load_o,
                  oy_s, oy_r, o1_s, o1_r, o2_s, o2_r, ey_s, ey_r, e1_s, e1_r, e2_s, e2_r,
                  ac_s, ac_r, ax_s, ax_r, aw_s, aw_r, ah_s, ah_r,
                  bc_s, bc_r, bx_s, bx_r, bw_s, bw_r, bh_s, bh_r, keep, n_s, n_r):
    place = Place(ways)
    x, w, h, c, hy, hz = place.x, place.w, place.h, place.c, place.hy, place.hz
    d0, d1 = hz % 2, hz // 2
    runs = v_left.shape[0]
    chunks = e_p.shape[0]
    wide = e_p.shape[-1]
    rows = own_a.shape[1]
    hp = 256 // (2 * rows)
    tiles = HEADS // hp
    a_cols, b_cols = own_a.shape[2], own_b.shape[2]
    inner = v_left.shape[-1]
    head3 = 3 * HEAD_DIM
    group = runs * HEADS * STRIPE
    sends = []

    def send(src, dst, s, r, device):
        copy = remote(src, dst, s, r, device)
        copy.start()
        sends.append(copy)
        return copy

    greet(place.peers_h() + place.peers_w() + [place.peer_x(), place.peer_c()])

    def fetch(src, dst, sem):
        copy = pltpu.make_async_copy(src, dst, sem)
        copy.start()
        return copy


    def partial(src, q, buf, depth):
        @pl.loop(0, wide // 256)
        def _(k):
            at = pl.multiple_of(k * 256, 256)
            value = lax.dot_general(
                src[...].reshape(group, depth),
                v_w[pl.ds(pl.multiple_of(q * wide + at, 256), 256), :depth],
                (((1,), (1,)), ((), ())),
                preferred_element_type=F32,
            )
            buf[q, :, :, :, :, :, pl.ds(at, 256)] = value.astype(BF).reshape(runs, 2, 2, 2, STRIPE, 256)

    def sums(mine, y, one, two, s_1, r_1, s_2, r_2, total):
        def near(q):
            target = place.device(h=(hz + 1 - 2 * d0) * 2 + hy)
            return send(y.at[q, :, :, 1 - d0], one.at[q], s_1.at[q], r_1.at[q], target)

        def after_y(q, copy):
            copy.wait_recv()

            @pl.loop(0, runs)
            def _(run):
                for t in range(LINE):
                    value = y[q, run, t // 2, t % 2].astype(F32) + mine(q, run, t).astype(F32)
                    y[q, run, t // 2, t % 2] = value.astype(BF)

            return near(q)

        def after_1(q, copy):
            copy.wait_recv()

            @pl.loop(0, runs)
            def _(run):
                for t in range(2):
                    value = one[q, run, t].astype(F32) + y[q, run, t, d0].astype(F32)
                    one[q, run, t] = value.astype(BF)

            target = place.device(h=((1 - d1) * 2 + d0) * 2 + hy)
            return send(one.at[q, :, 1 - d1], two.at[q], s_2.at[q], r_2.at[q], target)

        def after_2(q, copy):
            copy.wait_recv()

            @pl.loop(0, runs)
            def _(run):
                total[run, :, q * wide : (q + 1) * wide] = two[q, run].astype(F32) + one[q, run, d1].astype(F32)

        return near, after_y, after_1, after_2

    o_near, o_after_y, o_after_1, o_after_2 = sums(
        lambda q, run, t: o_own[q - (early or 0), run, t // 2, t % 2], o_y, o_1, o_2, o1_s, o1_r, o2_s, o2_r, out_sum
    )
    _, e_after_y, e_after_1, e_after_2 = sums(
        lambda q, run, t: e_p[q, run, t // 2, t % 2, hy], e_y, e_1, e_2, e1_s, e1_r, e2_s, e2_r, e_sum
    )

    order_t = [(k, dw, dt) for k in range(2) for dw in list(range(1, ways)) + [0] for dt in list(range(1, tiles)) + [0]]
    own_t = h // hp

    def where(k, dw, dt):
        return (1 - x if k == 0 else x), (w + dw) % ways, (own_t + dt) % tiles

    def product(m, buf, src, first, count, at):
        @pl.loop(0, count // 256)
        def _(k):
            col = pl.multiple_of(k * 256, 256)
            value = jnp.dot(
                raw[m % 2, buf], src[..., pl.ds(first + col, 256)].reshape(group, 256), preferred_element_type=F32
            )
            ring[m % 3, :, :, :, pl.ds(at + col, 256)] = value.astype(BF).reshape(hp, 2, rows, 256)

    made, order_m = [], []

    def raw_copies(m):
        n, need = order_m[m]
        xs, ws, t = where(*order_t[n])
        at = pl.multiple_of(((xs * ways + ws) * tiles + t) * 256, 256)
        return [
            pltpu.make_async_copy(src.at[pl.ds(at, 256)], raw.at[m % 2, buf], load_raw.at[m % 2, buf])
            for buf, src in need
        ]

    def begin(m):
        if m < len(order_m):
            for copy in raw_copies(m):
                copy.start()

    def grads(cols, from_c, from_x, from_w, c_s, c_r, x_s, x_r, w_s, w_r, h_s, h_r, out, fill, flag):
        first, second, third, spot = {}, {}, {}, {}

        def make(n):
            m = len(made)
            if m >= 3:
                made[m - 3].wait_send()
            for copy in raw_copies(m):
                copy.wait()
            fill(m)
            begin(m + 1)
            k, dw, dt = order_t[n]
            first[n] = remote(
                ring.at[m % 3, :, 1 - c, :, pl.ds(0, cols)], from_c.at[k, dw, dt], c_s.at[n], c_r.at[n], place.peer_c()
            )
            first[n].start()
            spot[n] = m % 3
            made.append(first[n])

        def mine(n):
            k, dw, dt = order_t[n]
            first[n].wait_recv()

            @pl.loop(0, hp)
            def _(q):
                value = from_c[k, dw, dt, q].astype(F32) + ring[spot[n], q, c, :, :cols].astype(F32)
                from_c[k, dw, dt, q] = value.astype(BF)

        def cross(n):
            k, dw, dt = order_t[n]
            second[dw, dt] = send(from_c.at[0, dw, dt], from_x.at[dw, dt], x_s.at[dw, dt], x_r.at[dw, dt], place.peer_x())

        def close(n):
            k, dw, dt = order_t[n]
            _, ws, t = where(k, dw, dt)
            second[dw, dt].wait_recv()
            more = [from_x.at[dw, dt]]
            if dw == 0:
                for dv in range(1, ways):
                    third[dv, dt].wait_recv()
                    more.append(from_w.at[dv - 1, dt])

            @pl.loop(0, hp)
            def _(q):
                value = from_c[1, dw, dt, q].astype(F32)
                for ref in more:
                    value = value + ref[q].astype(F32)
                from_c[1, dw, dt, q] = value.astype(BF)

            if dw != 0:
                third[dw, dt] = send(from_c.at[1, dw, dt], from_w.at[dw - 1, dt], w_s.at[dw - 1, dt], w_r.at[dw - 1, dt], place.device(w=ws))
                return
            for q in range(hp):
                hs = t * hp + q
                at = dt * hp + q

                @pl.when(hs != h)
                def _():
                    remote(from_c.at[1, 0, dt, q], out.at[h], h_s.at[at], h_r.at[h], place.device(h=hs)).start()

                @pl.when(hs == h)
                def _():
                    pltpu.make_async_copy(from_c.at[1, 0, dt, q], out.at[h], keep.at[flag]).start()

        def end():
            for n in range(len(order_t)):
                k, dw, dt = order_t[n]
                if k == 1 and dw == 0:
                    _, _, t = where(k, dw, dt)
                    for q in range(hp):
                        hs = t * hp + q

                        @pl.when(hs != h)
                        def _():
                            remote(from_c.at[1, 0, dt, q], out.at[h], h_s.at[dt * hp + q], h_r.at[h], place.device(h=hs)).wait_send()
            for dh in range(1, HEADS):
                hs = (h + dh) % HEADS
                remote(out.at[hs], out.at[hs], h_s.at[0], h_r.at[hs], place.peer_x()).wait_recv()
            pltpu.make_async_copy(from_c.at[1, 0, 0, 0], out.at[h], keep.at[flag]).wait()

        return make, mine, cross, close, end

    def fill_a(m):
        product(m, 1, v_left, 0, inner, 0)
        product(m, 0, v_right, head3, a_cols - inner, inner)

    def fill_b(m):
        product(m, 0, v_right, 0, head3, 0)

    a_make, a_mine, a_cross, a_close, a_end = grads(
        a_cols, a_c, a_x, a_w, ac_s, ac_r, ax_s, ax_r, aw_s, aw_r, ah_s, ah_r, own_a, fill_a, 0
    )
    b_make, b_mine, b_cross, b_close, b_end = grads(
        b_cols, b_c, b_x, b_w, bc_s, bc_r, bx_s, bx_r, bw_s, bw_r, bh_s, bh_r, own_b, fill_b, 1
    )
    count = len(order_t)
    half = count // 2
    order_m += [(n, ((0, n_all), (1, g_all))) for n in A_ORDER] + [(n, ((0, n_all),)) for n in A_ORDER]

    plan = []

    def step(time, body, *given):
        plan.append((time, len(plan), body, given))

    state = {}

    def wait_all(copies):
        for copy in copies:
            copy.wait()

    def e_part(q):
        partial(v_right, q, e_p, v_right.shape[-1])
        state["e", q] = send(e_p.at[q, :, :, :, 1 - hy], e_y.at[q], ey_s.at[q], ey_r.at[q], place.peer_y())

    def o_start():
        for q in range(early, chunks):
            state["o", q] = send(part_in.at[q - early, :, :, :, 1 - hy], o_y.at[q], oy_s.at[q], oy_r.at[q], place.peer_y())
        for q in range(chunks):
            if q < early:
                state["o_load", q] = fetch(half_in.at[q], o_y.at[q], load_o.at[q])
            else:
                state["o_load", q] = fetch(part_in.at[q - early, :, :, :, hy], o_own.at[q - early], load_o.at[q])

    def o_first(q):
        state["o_load", q].wait()
        if q < early:
            state["o", q] = o_near(q)
        else:
            state["o", q] = o_after_y(q, state["o", q])

    def advance(key, body, q):
        state[key, q] = body(q, state[key, q])

    note_w = []
    base = 1 + ways

    def note_sums():
        state["note_load"].wait()

        @pl.loop(0, v_right.shape[-1] // 128)
        def _(k):
            at = pl.multiple_of(k * 128, 128)
            value = v_right[..., pl.ds(at, 128)].reshape(group, 128).astype(F32)
            n_mine[pl.ds(k, 1), :] = jnp.sum(value, 0, keepdims=True)

        state["note"] = send(n_mine, n_c, n_s.at[0], n_r.at[0], place.peer_c())

    def note_cross():
        state["note"].wait_recv()
        n_c[...] = n_c[...] + n_mine[...]
        state["note"] = send(n_c, n_x, n_s.at[1], n_r.at[1], place.peer_x())

    def note_ways():
        state["note"].wait_recv()
        n_x[...] = n_x[...] + n_c[...]
        for k, device in enumerate(place.peers_w()):
            note_w.append(send(n_x, n_w.at[k], n_s.at[2 + k], n_r.at[2 + k], device))

    def note_out():
        if ways > 1:
            wait_all(note_w)
            total = n_x[...]
            for k in range(ways - 1):
                total = total + n_w[k]
            n_x[...] = total
        for dh in range(1, HEADS):
            send(n_x, note_all.at[h], n_s.at[base + dh], n_r.at[base + h], place.device(h=(h + dh) % HEADS))
        state["note_keep"] = pltpu.make_async_copy(n_x, note_all.at[h], keep.at[3])
        state["note_keep"].start()

    if early is not None:
        o_start()
    state["note_load"] = fetch(note, n_mine, keep.at[2])
    loads = [fetch(right, v_right, load.at[0]), fetch(left, v_left, load.at[1])]
    begin(0)
    w_load = fetch(w_all.at[:, pl.ds(0, v_right.shape[-1])], v_w, load.at[2])
    if early is not None:
        for q, times in enumerate(((0.5, 9, 19.5), (0.6, 14.5, 25), (14.2, 37, 49), (26, 48.2, 62))):
            step(times[0], o_first, q)
            step(times[1], advance, "o", o_after_1, q)
            step(times[2], advance, "o", o_after_2, q)
    step(1, wait_all, loads)
    for i, (n, time) in enumerate(zip(A_ORDER, (2, 4.5, 10, 15, 19.6, 26.2, 31, 36), strict=True)):
        step(time, a_make, n)
        if i > 0:
            step(time, a_mine, A_ORDER[i - 1])
            if A_ORDER[i - 1] < half:
                step(time, a_cross, A_ORDER[i - 1])
    step(38, a_mine, A_ORDER[-1])
    step(7.2, w_load.wait)
    for q in range(chunks):
        step((7.3, 13, 17.5, 22.5)[q], e_part, q)
    step(25.5, note_sums)
    step(36.5, note_cross)
    step(60, note_ways)
    step(60, note_out)
    for i, (n, time) in enumerate(zip(A_ORDER, (39, 40, 41, 42, 44, 45, 46, 47), strict=True)):
        step(time, b_make, n)
        if i > 0:
            step(time, b_mine, A_ORDER[i - 1])
            if A_ORDER[i - 1] < half:
                step(time, b_cross, A_ORDER[i - 1])
    step(47.5, b_mine, A_ORDER[-1])
    for n, times in zip(range(half, count), ((22, 74), (35.5, 79), (49.5, 84), (63, 88)), strict=True):
        step(times[0], a_close, n)
        step(times[1], b_close, n)
    for q, times in enumerate(((48, 66, 80), (59, 77, 92), (71, 89, 104), (83, 101, 114))):
        step(times[0], advance, "e", e_after_y, q)
        step(times[1], advance, "e", e_after_1, q)
        step(times[2], advance, "e", e_after_2, q)
    for _, _, body, given in sorted(plan, key=lambda one: one[:2]):
        body(*given)
    for copy in made[-3:]:
        copy.wait_send()
    a_end()
    b_end()
    state["note_keep"].wait()
    for dh in range(1, HEADS):
        hs = (h + dh) % HEADS
        remote(note_all.at[hs], note_all.at[hs], n_s.at[0], n_r.at[base + hs], place.peer_x()).wait_recv()
    for copy in sends:
        if not any(copy is other for other in note_w):
            copy.wait_send()


def finish(ways, rows, left, right, w_all, n_all, g_all, note, half, part):
    width = w_all.shape[0]
    inner, right_cols = left.shape[1], right.shape[1]
    head3 = 3 * HEAD_DIM
    a_cols, b_cols = inner + right_cols - head3, head3
    group = n_all.shape[1]
    runs = group // (HEADS * STRIPE)
    lines = (runs, LINE, 2, STRIPE)
    hp = 256 // (2 * rows)
    tiles = HEADS // hp
    chunks, wide = 4, width // 4
    extra = max(ways - 1, 1)
    count = 2 * ways * tiles
    assert count == len(A_ORDER)
    early = None if half is None else half.shape[0]

    def vm(shape, kind=BF):
        return pltpu.VMEM(shape, kind)

    def row_buffers(first, used):
        return [
            vm(first),
            vm((chunks, runs, 2, 2, STRIPE, wide) if used else (1, 1, 1, 1, 16, 128)),
            vm((chunks, runs, 2, STRIPE, wide) if used else (1, 1, 1, 16, 128)),
            vm((chunks, runs, STRIPE, wide) if used else (1, 1, 16, 128)),
        ]

    def spare(shape):
        return shape if ways > 1 else (1,) * (len(shape) - 2) + (16, 128)

    def gradient_buffers(cols):
        return [
            vm((2, ways, tiles, hp, rows, cols)),
            vm((ways, tiles, hp, rows, cols)),
            vm(spare((extra, tiles, hp, rows, cols))),
        ]

    def gradient_sems():
        return [
            DMA((count,)), DMA((count,)), DMA((ways, tiles)), DMA((ways, tiles)), DMA((extra, tiles)), DMA((extra, tiles)),
            DMA((HEADS,)), DMA((HEADS,)),
        ]

    scratch = (
        [
            vm(lines + (inner,)), vm(lines + (right_cols,)), vm((width, right_cols)),
        ]
        + row_buffers((max(chunks - (early or 0), 1), runs, 2, 2, STRIPE, wide) if early is not None else (1, 1, 1, 1, 16, 128), early is not None)
        + row_buffers((chunks, runs, 2, 2, 2, STRIPE, wide), True)
        + [vm((2, 2, 256, group)), vm((3, hp, 2, rows, a_cols))]
        + gradient_buffers(a_cols) + gradient_buffers(b_cols)
        + [vm(note.shape, F32)] * 3 + [vm((extra,) + note.shape, F32)]
        + [DMA((3,)), DMA((2, 2)), DMA((chunks,))]
        + [DMA((chunks,))] * 12
        + gradient_sems() + gradient_sems()
        + [DMA((4,)), DMA((1 + ways + HEADS,)), DMA((1 + ways + HEADS,))]
    )
    shapes = (
        jax.ShapeDtypeStruct((runs, STRIPE, width), F32),
        jax.ShapeDtypeStruct((runs, STRIPE, width), F32),
        jax.ShapeDtypeStruct((HEADS, rows, a_cols), BF),
        jax.ShapeDtypeStruct((HEADS, rows, b_cols), BF),
        jax.ShapeDtypeStruct((HEADS,) + note.shape, F32),
    )
    empty = jnp.zeros((1, 1, 1, 1, 16, 128), BF)
    ins = (
        left.reshape(lines + (inner,)), right.reshape(lines + (right_cols,)), w_all, n_all, g_all, note,
        empty if half is None else half, empty if part is None else part,
    )
    return pl.pallas_call(
        functools.partial(finish_kernel, ways, early),
        out_shape=shapes,
        in_specs=[ANY] * len(ins),
        out_specs=(VMEM, VMEM, ANY, ANY, ANY),
        scratch_shapes=scratch,
        compiler_params=pltpu.CompilerParams(collective_id=2, has_side_effects=True, vmem_limit_bytes=62 * 2**20),
    )(*ins)


def close_kernel(tokens, note, notes, gain_one, shift_one, gain_two, shift_two, *refs):
    sources, rest = refs[:8], refs[8:]
    (output, input_grad, gain_one_grad, shift_one_grad, gain_two_grad, shift_two_grad, qkv_out, qk_bias, v_bias, dense_out,
     dense_bias, expand_out, expand_bias, shrink_out, shrink_bias) = rest[:15]
    x_in, g_in, out_sum, e_sum, qkv_in, expand_in, own_a, own_b = kept = rest[15:23]
    qkv_grad, dense_grad, expand_grad, shrink_grad, load, put = rest[23:]
    loads = [pltpu.make_async_copy(src, dst, load.at[k]) for k, (src, dst) in enumerate(zip(sources, kept, strict=True))]
    for k in (6, 7, 4, 5, 0, 2, 1, 3):
        loads[k].start()
    saves = []

    def save(src, dst):
        copy = pltpu.make_async_copy(src, dst, put.at[len(saves)])
        copy.start()
        saves.append(copy)

    x, b = lax.axis_index("head"), lax.axis_index("blk")
    devices, rows = tokens.shape[0], qkv_in.shape[0]
    me = x * (devices // 2) + b
    width = x_in.shape[1]
    hidden = expand_in.shape[1] // HEADS
    head_rows, block_rows = HEAD_DIM // 128, (3 * HEAD_DIM + hidden) // 128

    square = lax.broadcasted_iota(jnp.int32, (rows, rows), 0) == lax.broadcasted_iota(jnp.int32, (rows, rows), 1)

    def down(ref):
        return jnp.sum(jnp.where(square, ref[...].astype(F32).reshape(1, rows), 0.0), 1, keepdims=True)

    def across(column):
        return jnp.sum(jnp.where(square, column, 0.0), 0, keepdims=True)

    def sums_of(h, first, count):
        return jnp.concatenate([notes[h, first + k : first + k + 1] for k in range(count)], 1)

    def one_norm(gain, shift, weight, grad, pieces):
        by_gain, by_shift = 0.0, 0.0
        for first, value, column_sums in pieces:
            count = value.shape[1]
            here = slice(first, first + count)
            kept = weight[:, here].astype(F32)
            grad[:, here] = gain * value + shift * column_sums
            by_gain = by_gain + jnp.sum(kept * value, 1, keepdims=True)
            by_shift = by_shift + jnp.sum(kept * column_sums, 1, keepdims=True)
        return across(by_gain), across(by_shift)

    qkv_pieces = (
        (t * width + h * HEAD_DIM, own_b[h, :, t * HEAD_DIM : (t + 1) * HEAD_DIM].astype(F32),
         sums_of(h, t * head_rows, head_rows))
        for h in range(HEADS) for t in range(3)
    )
    expand_pieces = (
        (h * hidden, own_a[h, :, HEAD_DIM + hidden :].astype(F32), sums_of(h, 3 * head_rows, hidden // 128))
        for h in range(HEADS)
    )
    loads[6].wait()
    for h in range(HEADS):
        shrink_grad[:, h * hidden : (h + 1) * hidden] = own_a[h, :, HEAD_DIM : HEAD_DIM + hidden].astype(F32)
    save(shrink_grad, shrink_out)
    for h in range(HEADS):
        dense_grad[:, h * HEAD_DIM : (h + 1) * HEAD_DIM] = own_a[h, :, :HEAD_DIM].astype(F32)
    save(dense_grad, dense_out)
    loads[5].wait()
    gain_two_grad[...], shift_two_grad[...] = one_norm(
        down(gain_two), down(shift_two), expand_in, expand_grad, expand_pieces
    )
    save(expand_grad, expand_out)
    loads[7].wait()
    loads[4].wait()
    gain_one_grad[...], shift_one_grad[...] = one_norm(down(gain_one), down(shift_one), qkv_in, qkv_grad, qkv_pieces)
    save(qkv_grad, qkv_out)
    for k in range(4):
        loads[k].wait()

    def share(row, count):
        return jnp.where(me % (128 // count) == 0, row[:, :count], row[:, 128 - count :])

    in_head = HEADS * head_rows
    third, rest = me // in_head, me % in_head
    qk_bias[...] = notes[pl.ds(rest // head_rows, 1), pl.ds(third * head_rows + rest % head_rows, 1)][0]
    half = me // 2
    v_bias[...] = share(notes[pl.ds(half // head_rows, 1), pl.ds(2 * head_rows + half % head_rows, 1)][0], rows)
    per_head = hidden // 128
    for k in range(2):
        row = me * 2 + k
        expand_bias[:, k * 128 : (k + 1) * 128] = notes[
            pl.ds(row // per_head, 1), pl.ds(3 * head_rows + row % per_head, 1)
        ][0]
    total = 0.0
    for h in range(HEADS):
        total = total + notes[pl.ds(h, 1), pl.ds(block_rows + half, 1)][0]
    dense_bias[...] = share(total, rows)
    shrink_bias[...] = share(total, rows)

    mine = tokens[pl.ds(me, 1), :]
    tok_dev = mine.shape[1]
    pick = lax.broadcasted_iota(jnp.int32, (tok_dev, tok_dev), 0) == mine // (devices * STRIPE) * STRIPE + mine % STRIPE
    pick = jnp.where(pick, 1.0, 0.0).astype(BF)

    def restored(value):
        value = value.astype(BF)
        return lax.dot_general(pick, value, (((0,), (0,)), ((), ())), preferred_element_type=F32).astype(BF)

    states = jnp.dot(pick, x_in[...], preferred_element_type=F32)
    bias = jnp.concatenate([note[block_rows + k : block_rows + k + 1] for k in range(width // 128)], 1)
    output[...] = restored(states + out_sum[...].reshape(tok_dev, width) + bias)
    centered = states - jnp.mean(states, -1, keepdims=True)
    inverse_spread = lax.rsqrt(jnp.mean(centered * centered, -1, keepdims=True) + 1e-05)
    normed = centered * inverse_spread
    e = e_sum[...].reshape(tok_dev, width)
    dx = inverse_spread * (e - jnp.mean(e, -1, keepdims=True) - normed * jnp.mean(e * normed, -1, keepdims=True))
    input_grad[...] = restored(jnp.dot(pick, g_in[...], preferred_element_type=F32) + dx)
    for copy in saves:
        copy.wait()


def close(tokens, inputs, cotangent, out_sum, e_sum, note, notes, scales, qkv, expand, own_a, own_b):
    rows, hidden_all = expand.shape
    width = inputs.shape[1]
    devices = tokens.shape[0]

    def shape(*dims):
        return jax.ShapeDtypeStruct(dims, F32)

    low = jax.ShapeDtypeStruct(inputs.shape, BF)
    sources = (inputs, cotangent, out_sum, e_sum, qkv, expand, own_a, own_b)
    outs = (
        low, low, shape(1, rows), shape(1, rows), shape(1, rows), shape(1, rows), shape(rows, 3 * width),
        shape(1, 2 * width // devices), shape(1, rows), shape(rows, width), shape(1, rows), shape(rows, hidden_all),
        shape(1, hidden_all // devices), shape(rows, hidden_all), shape(1, rows),
    )
    large = (6, 9, 11, 13)
    results = pl.pallas_call(
        close_kernel,
        out_shape=outs,
        in_specs=[VMEM] * 7 + [ANY] * len(sources),
        out_specs=tuple(ANY if k in large else VMEM for k in range(len(outs))),
        scratch_shapes=[pltpu.VMEM(one.shape, one.dtype) for one in sources]
        + [pltpu.VMEM(outs[k].shape, F32) for k in large]
        + [DMA((len(sources),)), DMA((4,))],
        compiler_params=pltpu.CompilerParams(vmem_limit_bytes=62 * 2**20),
    )(tokens, note, notes, *scales, *sources)
    return tuple(one[0] if one.shape[0] == 1 else one for one in results)


def pieces_of(i, prompt_runs):
    return list(range(min(i + 1, prompt_runs))) + ([i] if i >= prompt_runs else [])


def attention_forward(i, prompt_runs, mask, q_ref, key, value_of, s_ref):
    q = q_ref[i]
    peak, scores = None, []
    for at, k in enumerate(pieces_of(i, prompt_runs)):
        keys = key(k)
        s = lax.dot_general(q, keys, (((1,), (1,)), ((), ())), preferred_element_type=F32)
        keep = mask(i, k)
        if keep is not None:
            s = jnp.where(keep, s, -1e30)
        here = slice(at * keys.shape[0], (at + 1) * keys.shape[0])
        s_ref[:, here] = s
        top = jnp.max(s, -1, keepdims=True)
        peak = top if peak is None else jnp.maximum(peak, top)
        scores.append((k, here))
    total, out = 0.0, 0.0
    for k, here in scores:
        p = jnp.exp(s_ref[:, here] - peak)
        keep = mask(i, k)
        if keep is not None:
            p = jnp.where(keep, p, 0.0)
        total = total + jnp.sum(p, -1, keepdims=True)
        out = out + jnp.dot(p.astype(BF), value_of(k), preferred_element_type=F32)
    return out / total, peak + jnp.log(total)


def attention_backward(i, prompt_runs, mask, q_ref, do_ref, key, value_of, out, lse, turn_ref, sum_ref):
    by_rows = (((1,), (1,)), ((), ()))
    by_tokens = (((0,), (0,)), ((), ()))

    def dot(a, b, dims=(((1,), (0,)), ((), ()))):
        return lax.dot_general(a, b, dims, preferred_element_type=F32)

    q, do = q_ref[i], do_ref[i]
    delta = jnp.sum(out * do.astype(F32), -1, keepdims=True)
    dq = 0.0
    for k in pieces_of(i, prompt_runs):
        keys = key(k)
        p = jnp.exp(dot(q, keys, by_rows) - lse)
        keep = mask(i, k)
        if keep is not None:
            p = jnp.where(keep, p, 0.0)
        ds = (p * (dot(do, value_of(k), by_rows) - delta)).astype(BF)
        dq = dq + dot(ds, keys)
        dk = dot(ds, q, by_tokens)
        dv = dot(p.astype(BF), do, by_tokens)
        if i == k:
            sum_ref[k, :, :HEAD_DIM] = dk
            sum_ref[k, :, HEAD_DIM:] = dv
        else:
            sum_ref[k, :, :HEAD_DIM] = sum_ref[k, :, :HEAD_DIM] + dk
            sum_ref[k, :, HEAD_DIM:] = sum_ref[k, :, HEAD_DIM:] + dv
    dq = (dq * (1.0 / math.sqrt(HEAD_DIM))).astype(BF).astype(F32)
    return turn(dq, [turn_ref[t, i] for t in range(3)], -1.0)


def attention_kernel(prompt_runs, one_prompt, q_ref, do_ref, kv_ref, row_ref, col_ref, turn_ref,
                     o_ref, dq_ref, dkv_ref, s_ref, sum_ref):
    def mask(i, k):
        rows, cols = row_ref[i], col_ref[k]
        if i == k:
            return (rows[:, 1:2] == cols[1:2, :]) & (cols[0:1, :] <= rows[:, 0:1])
        if one_prompt:
            return None
        return rows[:, 2:3] == cols[2:3, :]

    def key(k):
        return kv_ref[k, :, :HEAD_DIM]

    def value_of(k):
        return kv_ref[k, :, HEAD_DIM:]

    for i in range(q_ref.shape[0]):
        out, lse = attention_forward(i, prompt_runs, mask, q_ref, key, value_of, s_ref)
        o_ref[i] = out.astype(BF)
        back = attention_backward(
            i, prompt_runs, mask, q_ref, do_ref, key, value_of, out, lse, turn_ref, sum_ref
        )
        dq_ref[i] = back.astype(BF)
    dkv_ref[...] = sum_ref[...].astype(BF)


def attention(prompt_runs, one_prompt, queries, d_out, pairs, row_meta, col_meta, tables):
    m = queries.shape[1]
    count = pairs.shape[1]
    return pl.pallas_call(
        functools.partial(attention_kernel, prompt_runs, one_prompt),
        out_shape=(
            jax.ShapeDtypeStruct(queries.shape, BF),
            jax.ShapeDtypeStruct(queries.shape, BF),
            jax.ShapeDtypeStruct(pairs.shape, BF),
        ),
        in_specs=[VMEM] * 6,
        out_specs=(VMEM,) * 3,
        scratch_shapes=[pltpu.VMEM((m, (prompt_runs + 1) * count), F32), pltpu.VMEM(pairs.shape, F32)],
        compiler_params=pltpu.CompilerParams(vmem_limit_bytes=60 * 2**20),
    )(queries, d_out, pairs, row_meta, col_meta, tables)


def rotate(values, cosine, sine):
    half = ROT // 2
    leading, behind = values[:, :half], values[:, half:ROT]
    return jnp.concatenate(
        [leading * cosine - behind * sine, behind * cosine + leading * sine, values[:, ROT:]], -1
    )


def per_device(
    inputs, attn_norm_gain, attn_norm_bias, mlp_norm_gain, mlp_norm_bias, qkv_weight, qkv_bias, dense_weight,
    dense_bias, expand_weight, expand_bias, shrink_weight, shrink_bias, token_of_row, cont_parent, position_ids,
    cotangent,
):
    heads, blocks = lax.axis_size("head"), lax.axis_size("blk")
    devices = heads * blocks
    ways = blocks // (2 * HEADS)
    assert heads == 2 and blocks == ways * 2 * HEADS
    x = lax.axis_index("head")
    b = lax.axis_index("blk")
    me = x * blocks + b
    c, h, w = b % 2, (b // 2) % HEADS, b // (2 * HEADS)
    tok_dev, width = inputs.shape
    rows = qkv_weight.shape[0]
    hidden = expand_weight.shape[1] // HEADS
    runs = tok_dev // STRIPE
    run_size = devices * STRIPE
    prompt_total = token_of_row.shape[0] - cont_parent.shape[0] * CONT
    prompt_runs = prompt_total // run_size
    one_prompt = prompt_total == PROMPT
    assert prompt_runs * run_size == prompt_total
    group_rows = runs * HEADS * STRIPE
    head3 = 3 * HEAD_DIM
    block_columns = head3 + hidden

    by_device = token_of_row.reshape(devices, tok_dev)
    mine = lax.dynamic_index_in_dim(by_device, me, 0, False)
    sorted_at = mine // run_size * STRIPE + mine % STRIPE
    pick = (sorted_at[None, :] == jnp.arange(tok_dev, dtype=jnp.int32)[:, None]).astype(BF)

    def ordered(rows_in):
        return jnp.dot(pick, rows_in, preferred_element_type=F32).astype(BF)

    def restored(rows_in):
        return lax.dot_general(pick, rows_in, (((0,), (0,)), ((), ())), preferred_element_type=F32).astype(BF)

    scales = (attn_norm_gain, attn_norm_bias, mlp_norm_gain, mlp_norm_bias)
    fuse, opened = open_all(
        ways, prompt_runs, prompt_total, inputs, cotangent, by_device, position_ids[None],
        scales, (qkv_bias, expand_bias, dense_bias, shrink_bias),
        qkv_weight, expand_weight, dense_weight, shrink_weight,
    )
    lanes = 128
    note_rows = block_columns // lanes
    slice_rows = width // lanes
    rows_run = group_rows // runs
    n_all, g_all, w_all, note, tables, sum_note = opened[:6]
    w_all = w_all.reshape(width, w_all.shape[-1])
    out_bias = note[note_rows : note_rows + slice_rows].reshape(width)
    gain_one, shift_one = attn_norm_gain.astype(F32), attn_norm_bias.astype(F32)
    gain_two, shift_two = mlp_norm_gain.astype(F32), mlp_norm_bias.astype(F32)
    qkv_wide, expand_wide = qkv_weight.astype(F32), expand_weight.astype(F32)
    states = ordered(inputs).astype(F32)
    grad_out = ordered(cotangent).astype(F32)
    average = jnp.mean(states, -1, keepdims=True)
    centered = states - average
    inverse_spread = lax.rsqrt(jnp.mean(centered * centered, -1, keepdims=True) + 1e-05)
    normed = centered * inverse_spread
    if fuse:
        left, right, half, part = opened[6:]
    else:
        n_all, g_all = n_all.reshape(group_rows, width), g_all.reshape(group_rows, width)
        bias_block = note[:note_rows].reshape(block_columns)
        run_of = by_device // run_size
        each_run = jnp.arange(runs, dtype=jnp.int32)
        base = jnp.min(jnp.where(run_of[:, :, None] == each_run, by_device[:, :, None], 2**30), 1)
        within = jnp.arange(STRIPE, dtype=jnp.int32)
        bases = base.reshape(2, ways, HEADS, 2, runs)
        own_base = lax.dynamic_index_in_dim(bases, x, 0, False)
        own_base = lax.dynamic_index_in_dim(own_base, w, 0, False)
        own_base = lax.dynamic_index_in_dim(own_base, c, 1, False)
        row_tokens = (own_base.T[:, :, None] + within).reshape(runs, rows_run)
        col_tokens = (bases.transpose(4, 1, 0, 3, 2)[..., None] + within).reshape(runs, run_size)
        flat = tables.reshape(3, group_rows, lanes)
        cosine, sine = flat[0, :, : ROT // 2], flat[2, :, ROT // 2 : ROT]
        w_in, w_out = w_all[:, :block_columns], w_all[:, block_columns:]
        mixed = jnp.dot(n_all, w_in[:, :head3], preferred_element_type=F32) + bias_block[:head3]
        queries = (rotate(mixed[:, :HEAD_DIM], cosine, sine) * (1.0 / math.sqrt(HEAD_DIM))).astype(BF)
        keys = rotate(mixed[:, HEAD_DIM : 2 * HEAD_DIM], cosine, sine).astype(BF)
        values = mixed[:, 2 * HEAD_DIM :].astype(BF)
        pairs = exchange(ways, jnp.concatenate([keys, values], 1).reshape(runs, rows_run, 2 * HEAD_DIM))
        pairs = pairs.reshape(runs, run_size, 2 * HEAD_DIM)
        d_attended = jnp.dot(g_all, w_out[:, :HEAD_DIM], preferred_element_type=F32).astype(BF)
        expanded = jnp.dot(n_all, w_in[:, head3:], preferred_element_type=F32) + bias_block[head3:]
        activated, gelu_back = jax.vjp(lambda v: jax.nn.gelu(v, approximate=False), expanded)
        activated = activated.astype(BF)
        d_activated = jnp.dot(g_all, w_out[:, HEAD_DIM:], preferred_element_type=F32)
        d_expanded = gelu_back(d_activated)[0].astype(BF)

        def meta(tokens):
            is_prompt = tokens < prompt_total
            cont = (tokens - prompt_total) // CONT
            matches = cont[..., None] == jnp.arange(cont_parent.shape[0], dtype=jnp.int32)
            prompt = jnp.where(is_prompt, tokens // PROMPT, jnp.sum(jnp.where(matches, cont_parent, 0), -1))
            segment = jnp.where(is_prompt, -1 - tokens // PROMPT, cont)
            return tokens, segment, prompt

        attended, d_queries, d_pairs = attention(
            prompt_runs, one_prompt,
            queries.reshape(runs, rows_run, HEAD_DIM), d_attended.reshape(runs, rows_run, HEAD_DIM),
            pairs, jnp.stack(meta(row_tokens), -1), jnp.stack(meta(col_tokens), 1), tables,
        )
        attended = attended.reshape(group_rows, HEAD_DIM)

        left = jnp.concatenate([attended, activated], 1)
        part = lax.dot_general(left, w_out, (((1,), (1,)), ((), ())), preferred_element_type=F32)
        part = part.reshape(runs, HEADS, STRIPE, width)
        others = [[w2 * 2 * HEADS + h2 * 2 + c2 for h2 in range(HEADS)] for w2 in range(ways) for c2 in range(2)]
        out_rows = lax.psum_scatter(part, "blk", scatter_dimension=1, axis_index_groups=others, tiled=True)[:, 0]
        half = part = None
        n_all, g_all = n_all.T, g_all.T
        d_pairs = d_pairs.astype(F32).reshape(runs, ways, 2, 2, rows_run, 2 * HEAD_DIM).transpose(1, 3, 2, 0, 4, 5)
        d_pairs = d_pairs.reshape(2 * ways, 2, runs, rows_run, 2 * HEAD_DIM)
        alike = [[w2 * 2 * HEADS + h2 * 2 + c2 for w2 in range(ways) for c2 in range(2)] for h2 in range(HEADS)]
        d_pairs = lax.psum_scatter(d_pairs, "blk", scatter_dimension=0, axis_index_groups=alike, tiled=True)[0]
        d_pairs = lax.psum_scatter(d_pairs, "head", scatter_dimension=0, tiled=True)
        d_pairs = d_pairs.reshape(group_rows, 2 * HEAD_DIM)
        d_keys = rotate(d_pairs[:, :HEAD_DIM].astype(BF).astype(F32), cosine, -sine).astype(BF)
        right = jnp.concatenate(
            [d_queries.reshape(group_rows, HEAD_DIM), d_keys, d_pairs[:, HEAD_DIM:].astype(BF), d_expanded], 1
        )

    out_sum, e_sum, owned_a, owned_b, owned_notes = finish(
        ways, rows, left, right, w_all, n_all, g_all, sum_note, half, part
    )
    if fuse:
        return close(
            by_device, inputs, cotangent, out_sum, e_sum, note, owned_notes, scales, qkv_weight, expand_weight, owned_a,
            owned_b,
        )
    out_sum = out_rows
    output = restored((states + out_sum.reshape(tok_dev, width) + out_bias).astype(BF))
    e_sum = e_sum.reshape(tok_dev, width)
    dx = inverse_spread * (
        e_sum - jnp.mean(e_sum, -1, keepdims=True) - normed * jnp.mean(e_sum * normed, -1, keepdims=True)
    )
    input_grad = restored((grad_out + dx).astype(BF))
    owned_a, owned_b = owned_a.astype(F32), owned_b.astype(F32)

    def join_qkv(values):
        return values.reshape(HEADS, -1, 3, HEAD_DIM).transpose(1, 2, 0, 3).reshape(-1, 3 * width)

    def join(values):
        return values.transpose(1, 0, 2).reshape(values.shape[1], -1)

    raw_qkv = join_qkv(owned_b)
    dense_grad = join(owned_a[..., :HEAD_DIM])
    shrink_grad = join(owned_a[..., HEAD_DIM : HEAD_DIM + hidden])
    raw_expand = join(owned_a[..., HEAD_DIM + hidden :])
    column_sums = owned_notes[:, :note_rows].reshape(HEADS, 1, block_columns)
    qkv_sum = join_qkv(column_sums[..., :head3])
    expand_sum = join(column_sums[..., head3:])
    all_sums = jnp.sum(owned_notes[:, note_rows : note_rows + width // lanes], 0).reshape(width)
    bias_grad = lax.dynamic_slice_in_dim(all_sums, me * rows, rows, 0)
    qkv_grad = gain_one[:, None] * raw_qkv + shift_one[:, None] * qkv_sum
    expand_grad = gain_two[:, None] * raw_expand + shift_two[:, None] * expand_sum

    def own(values, count):
        return lax.dynamic_slice_in_dim(values, me * count, count, 0)

    return (
        output,
        input_grad,
        jnp.sum(qkv_wide * raw_qkv, 1),
        jnp.sum(qkv_wide * qkv_sum, 1),
        jnp.sum(expand_wide * raw_expand, 1),
        jnp.sum(expand_wide * expand_sum, 1),
        qkv_grad,
        own(qkv_sum[0, : 2 * width], 2 * width // devices),
        own(qkv_sum[0, 2 * width :], width // devices),
        dense_grad,
        bias_grad,
        expand_grad,
        own(expand_sum[0], HEADS * hidden // devices),
        shrink_grad,
        bias_grad,
    )


def solution(mesh):
    matrix, vector = P(("head", "blk"), None), P(("head", "blk"))
    return jax.shard_map(
        per_device,
        mesh=mesh,
        in_specs=(
            matrix, vector, vector, vector, vector, matrix, vector, matrix, vector, matrix, vector, matrix, vector,
            P(), P(), vector, matrix,
        ),
        out_specs=(
            matrix, matrix, vector, vector, vector, vector, matrix, vector, vector, matrix, vector, matrix, vector,
            matrix, vector,
        ),
        check_vma=False,
    )
```

```python
import functools
import math

import jax
import jax.numpy as jnp
import numpy as np
from jax import lax
from jax.experimental import pallas as pl
from jax.experimental.pallas import tpu as pltpu
from jax.sharding import PartitionSpec as P

HEADS = 8
HEAD_DIM = 256
ROT = 64
PROMPT = 2048
CONT = 256
STRIPE = 16
MESH = pl.DeviceIdType.MESH
BF = jnp.bfloat16
F32 = jnp.float32
ANY = pl.BlockSpec(memory_space=pl.ANY)
VMEM = pl.BlockSpec(memory_space=pltpu.VMEM)
DMA = pltpu.SemaphoreType.DMA


class Place:
    def __init__(self, ways):
        self.ways = ways
        self.x = lax.axis_index("head")
        b = lax.axis_index("blk")
        self.c = b % 2
        self.h = (b // 2) % HEADS
        self.w = b // (2 * HEADS)
        self.hy = self.h % 2
        self.hz = self.h // 2

    def device(self, x=None, w=None, h=None, c=None):
        x = self.x if x is None else x
        w = self.w if w is None else w
        h = self.h if h is None else h
        c = self.c if c is None else c
        return (x, w * (2 * HEADS) + h * 2 + c)

    def peers_h(self):
        return [self.device(h=(self.h + k) % HEADS) for k in range(1, HEADS)]

    def peers_w(self):
        return [self.device(w=(self.w + k) % self.ways) for k in range(1, self.ways)]

    def peer_x(self):
        return self.device(x=1 - self.x)

    def peer_c(self):
        return self.device(c=1 - self.c)

    def peer_y(self):
        return self.device(h=self.h + 1 - 2 * self.hy)


def greet(devices):
    barrier = pltpu.get_barrier_semaphore()
    for one in devices:
        pl.semaphore_signal(barrier, inc=1, device_id=one, device_id_type=MESH)
    pl.semaphore_wait(barrier, len(devices))


def remote(src, dst, send, recv, device):
    return pltpu.make_async_remote_copy(
        src_ref=src, dst_ref=dst, send_sem=send, recv_sem=recv, device_id=device, device_id_type=MESH
    )


def call(body, out_shape, ins, scratch, ident, out_spec=ANY, in_spec=ANY):
    return pl.pallas_call(
        body,
        out_shape=out_shape,
        in_specs=[in_spec] * len(ins),
        out_specs=jax.tree.map(lambda _: out_spec, out_shape),
        scratch_shapes=scratch,
        compiler_params=pltpu.CompilerParams(
            collective_id=ident, has_side_effects=True, vmem_limit_bytes=60 * 2**20
        ),
    )(*ins)


LINE = HEADS // 2
A_ORDER = (0, 4, 1, 5, 2, 6, 3, 7)
EARLY = 2


def relay_rows(place, own, full, s, r):
    hz, hy = place.hz, place.hy
    d0, d1 = hz % 2, hz // 2

    def index(e1, e0, y):
        return (e1 * 2 + e0) * 2 + y

    far = place.device(h=index(1 - d1, d0, hy))
    near = place.device(h=index(d1, 1 - d0, hy))
    side = place.peer_y()
    made = []

    def push(src, idx, k, device):
        copy = remote(src, full.at[:, idx], s.at[k], r.at[idx], device)
        copy.start()
        made.append(copy)

    def arrived(idx):
        remote(full.at[:, idx], full.at[:, idx], s.at[0], r.at[idx], side).wait_recv()

    def first_z():
        push(own, place.h, 0, far)
        push(own, place.h, 1, near)

    def first_y():
        push(own, place.h, 2, side)

    def from_far():
        idx = index(1 - d1, d0, hy)
        arrived(idx)
        push(full.at[:, idx], idx, 3, near)
        push(full.at[:, idx], idx, 4, side)

    def from_near():
        idx = index(d1, 1 - d0, hy)
        arrived(idx)
        push(full.at[:, idx], idx, 5, side)

    def from_near_far():
        idx = index(1 - d1, 1 - d0, hy)
        arrived(idx)
        push(full.at[:, idx], idx, 6, side)

    def from_side():
        for z in range(LINE):
            arrived(z * 2 + 1 - hy)

    def sent():
        for copy in made:
            copy.wait_send()

    return first_z, first_y, from_far, from_near, from_near_far, from_side, sent


def open_kernel(ways, cuts, fuse, prompt_runs, prompt_total, *refs):
    refs = list(refs)

    def take(count):
        taken = refs[:count]
        del refs[:count]
        return taken

    (x_in, grad_in, token_ref, places, gain_one, shift_one, gain_two, shift_two, qkv_bias, expand_bias, dense_bias,
     shrink_bias, freq_in, step_in, qkv_in, expand_in, dense_in, shrink_in) = take(18)
    n_out, g_out, w_out, note_ref, turn_out, sums_out = take(6)
    left_out, right_out, half_out, part_out = take(4) if fuse else [None] * 4
    v_n, v_g, v_w, v_turn, trig, note, note_c, note_x, note_w, note_h, own, put = take(12)
    v_qkv, v_expand, trig_own, placed, sums = take(5)
    ns, nr, gs, gr, wa, wr, xs, xr, cs, cr = take(10)
    t_s, t_r, nc_s, nc_r, nx_s, nx_r, nw_s, nw_r, nh_s, nh_r = take(10)
    if fuse:
        (v_q, v_do, v_kv, v_slope, v_left, v_right, v_out, lse, s_ref, sum_ref, kv_c, kv_x, o_p, o_y, flat, flat_sem,
         row_tok, col_tok) = take(18)
        kx_s, kx_r, kc_s, kc_r, fc_s, fc_r, fx_s, fx_r, oy_s, oy_r = take(10)
    assert not refs
    place = Place(ways)
    x, w, h, c = place.x, place.w, place.h, place.c
    runs = v_n.shape[0]
    width = v_n.shape[-1]
    per_run = HEADS * STRIPE
    stage_a = [(dw, dh) for dw in range(ways) for dh in range(HEADS) if (dw, dh) != (0, 0)]
    sends, puts = [], []

    def send(src, dst, s, r, device):
        copy = remote(src, dst, s, r, device)
        copy.start()
        sends.append(copy)
        return copy

    def save(src, dst):
        copy = pltpu.make_async_copy(src, dst, put.at[len(puts)])
        copy.start()
        puts.append(copy)

    devices, rows = token_ref.shape[0], v_qkv.shape[0]
    hidden = v_expand.shape[1] // HEADS
    run_size = devices * STRIPE
    me = x * (2 * HEADS * ways) + w * (2 * HEADS) + h * 2 + c
    raw = [
        pltpu.make_async_copy(qkv_in, v_qkv, own.at[0]),
        pltpu.make_async_copy(expand_in, v_expand, own.at[1]),
    ]
    for copy in raw:
        copy.start()
    mine = token_ref[pl.ds(me, 1), :]
    mine_run = mine // run_size
    tok_dev = mine.shape[1]
    pick = lax.broadcasted_iota(jnp.int32, (tok_dev, tok_dev), 0) == mine_run * STRIPE + mine % STRIPE
    pick = jnp.where(pick, 1.0, 0.0).astype(BF)

    def ordered(ref):
        return jnp.dot(pick, ref[...], preferred_element_type=F32)

    states = ordered(x_in)
    centered = states - jnp.mean(states, -1, keepdims=True)
    normed = centered * lax.rsqrt(jnp.mean(centered * centered, -1, keepdims=True) + 1e-05)
    v_n[:, pl.ds(h, 1)] = normed.astype(BF).reshape(runs, 1, STRIPE, width)
    grads = ordered(grad_in)
    v_g[:, pl.ds(h, 1)] = grads.astype(BF).reshape(runs, 1, STRIPE, width)
    sums[...] = jnp.zeros_like(sums)
    g_sum = jnp.sum(grads, 0, keepdims=True)
    first_sum = (3 * HEAD_DIM + hidden) // 128
    for k in range(width // 128):
        sums[first_sum + k : first_sum + k + 1, :] = g_sum[:, k * 128 : (k + 1) * 128]
    far_off = jnp.int32(2**30)
    for k in range(runs):
        start = jnp.min(jnp.where(mine_run == k, places[...], far_off), 1, keepdims=True)
        angle = start.astype(F32) * freq_in[...]
        turned = lax.broadcasted_iota(jnp.int32, angle.shape, 1) < ROT
        trig_own[0, k : k + 1] = jnp.where(turned, jnp.cos(angle), 1.0)
        trig_own[1, k : k + 1] = jnp.where(turned, jnp.sin(angle), 0.0)

    def share_of(ref):
        return ref[...].astype(F32).reshape(1, ref.shape[0])

    def place_share(value, first):
        count = value.shape[1]
        span = -(-count // 128) * 128 + 128
        value = jnp.concatenate([value, jnp.zeros((1, span - count), F32)], 1)
        value = pltpu.roll(value, (me * count) % 128, 1)
        for k in range(span // 128):
            placed[pl.ds(first + me * count // 128 + k, 1), :] = value[:, k * 128 : (k + 1) * 128]

    placed[...] = jnp.zeros_like(placed)
    q_rows, e_rows, o_rows = 3 * width // 128, HEADS * hidden // 128, width // 128
    place_share(share_of(qkv_bias), 0)
    place_share(share_of(expand_bias), q_rows + 1)
    place_share(share_of(dense_bias) + share_of(shrink_bias), q_rows + e_rows + 2)
    square = lax.broadcasted_iota(jnp.int32, (rows, rows), 0) == lax.broadcasted_iota(jnp.int32, (rows, rows), 1)
    note[...] = jnp.zeros_like(note)

    def spread(weight, gain, shift, step, put_rows):
        diagonal = jnp.where(square, gain, 0.0).astype(BF)
        for at_col in range(0, weight.shape[1], step):
            value = weight[:, at_col : at_col + step]
            through = jnp.dot(jnp.broadcast_to(shift, (16, rows)).astype(BF), value, preferred_element_type=F32)
            weight[:, at_col : at_col + step] = jnp.dot(diagonal, value, preferred_element_type=F32).astype(BF)
            for k in range(step // 128):
                put_rows(at_col // 128 + k, through[:1, k * 128 : (k + 1) * 128])

    def qkv_row(k, value):
        third, rest = k // (q_rows // 3), k % (q_rows // 3)
        hh, kk = rest // (HEAD_DIM // 128), rest % (HEAD_DIM // 128)
        to = third * (HEAD_DIM // 128) + kk
        note[hh, to : to + 1] = value + placed[k : k + 1, :]

    def expand_row(k, value):
        hh, kk = k // (hidden // 128), k % (hidden // 128)
        to = 3 * HEAD_DIM // 128 + kk
        note[hh, to : to + 1] = value + placed[q_rows + 1 + k : q_rows + 2 + k, :]

    raw[0].wait()
    spread(v_qkv, share_of(gain_one), share_of(shift_one), 1024, qkv_row)
    raw[1].wait()
    spread(v_expand, share_of(gain_two), share_of(shift_two), 1024, expand_row)
    to = (3 * HEAD_DIM + hidden) // 128
    first = q_rows + e_rows + 2
    note[:, to : to + o_rows] = jnp.broadcast_to(placed[first : first + o_rows][None], (HEADS, o_rows, 128))
    greet(
        [place.device(w=(w + dw) % ways, h=(h + dh) % HEADS) for dw, dh in stage_a]
        + [place.peer_x(), place.peer_c()]
    )

    def share(g, hs):
        first, count = cuts[g]
        if g < 3:
            return v_qkv.at[:, pl.ds(pl.multiple_of(g * width + hs * HEAD_DIM, 256), count)]
        if g == 3:
            return v_expand.at[:, pl.ds(pl.multiple_of(hs * hidden, 256), count)]
        if g == 4:
            return dense_in.at[:, pl.ds(pl.multiple_of(hs * HEAD_DIM, 256), count)]
        return shrink_in.at[:, pl.ds(pl.multiple_of(hs * hidden + (g - 5) * count, 256), count)]

    kept = [
        pltpu.make_async_copy(share(g, h), v_w.at[x, w, h, c, :, pl.ds(*cuts[g])], own.at[2 + g]) for g in range(len(cuts))
    ]
    trig_kept = pltpu.make_async_copy(trig_own, trig.at[h], own.at[2 + len(cuts)])
    for copy in kept + [trig_kept]:
        copy.start()
    n_in, g_in = v_n.at[:, h], v_g.at[:, h]
    save(sums, sums_out)
    n_first_z, n_first_y, n_far, n_near, n_last, n_side, n_sent = relay_rows(place, n_in, v_n, ns, nr)
    g_first_z, g_first_y, g_far, g_near, g_last, g_side, g_sent = relay_rows(place, g_in, v_g, gs, gr)

    def columns(g):
        return pl.ds(cuts[g][0], cuts[g][1])

    def w_first(g, odd):
        for k, (dw, dh) in enumerate(stage_a):
            if dh % 2 != odd:
                continue
            h2 = (h + dh) % HEADS
            send(share(g, h2), v_w.at[x, w, h, c, :, columns(g)], wa.at[g, k], wr.at[g, w, h],
                 place.device(w=(w + dw) % ways, h=h2))

    def w_across(g):
        for dw, dh in stage_a:
            ws, hs = (w - dw) % ways, (h - dh) % HEADS
            spot = v_w.at[x, ws, hs, c, :, columns(g)]
            remote(spot, spot, wa.at[g, 0], wr.at[g, ws, hs], place.peer_x()).wait_recv()
        kept[g].wait()
        block = v_w.at[x, :, :, c, :, columns(g)]
        send(block, block, xs.at[g], xr.at[g], place.peer_x())
        send(block, block, cs.at[g, 0], cr.at[g, 0], place.peer_c())

    def w_beside(g):
        block = v_w.at[1 - x, :, :, c, :, columns(g)]
        remote(block, block, xs.at[g], xr.at[g], place.peer_x()).wait_recv()
        send(block, block, cs.at[g, 1], cr.at[g, 1], place.peer_c())

    def w_ready(g):
        for k, xx in ((0, x), (1, 1 - x)):
            block = v_w.at[xx, :, :, 1 - c, :, columns(g)]
            remote(block, block, cs.at[g, k], cr.at[g, k], place.peer_c()).wait_recv()
        if cuts[g][0] < w_out.shape[-1]:
            save(v_w.at[..., columns(g)], w_out.at[..., columns(g)])

    plan = []

    def step(time, body, *given):
        plan.append((time, len(plan), body, given))

    state = {}

    def trig_send():
        for k in range(1, HEADS):
            send(trig_own, trig.at[h], t_s.at[k], t_r.at[h], place.device(h=(h + k) % HEADS))

    def note_first():
        state["note"] = send(note, note_c, nc_s.at[0], nc_r.at[0], place.peer_c())

    def note_cross():
        state["note"].wait_recv()
        note_c[...] = note_c[...] + note[...]
        state["note"] = send(note_c, note_x, nx_s.at[0], nx_r.at[0], place.peer_x())

    def note_out():
        state["note"].wait_recv()
        note_x[...] = note_x[...] + note_c[...]
        summed = note_x
        if ways > 1:
            crossed = [
                send(note_x, note_w.at[k], nw_s.at[k], nw_r.at[k], device)
                for k, device in enumerate(place.peers_w())
            ]
            for copy in crossed:
                copy.wait_recv()
            total = note_x[...]
            for k in range(ways - 1):
                total = total + note_w[k]
            state["note"].wait_send()
            sends[:] = [one for one in sends if one is not state["note"]]
            note_c[...] = total
            summed = note_c
        for k in range(1, HEADS):
            h2 = (h + k) % HEADS
            send(summed.at[h2], note_h.at[h], nh_s.at[k], nh_r.at[h], place.device(h=h2))
        state["summed"] = summed

    def note_sum():
        bias = state["summed"][h]
        for k in range(1, HEADS):
            hs = (h - k) % HEADS
            remote(note_h.at[hs], note_h.at[hs], nh_s.at[k], nh_r.at[hs], place.peer_x()).wait_recv()
            bias = bias + note_h[hs]
        note_h[h] = bias
        save(note_h.at[h], note_ref)

    def turn_tables():
        trig_kept.wait()
        for k in range(1, HEADS):
            hs = (h - k) % HEADS
            remote(trig.at[hs], trig.at[hs], t_s.at[k], t_r.at[hs], place.peer_x()).wait_recv()
        lane = lax.broadcasted_iota(jnp.int32, (STRIPE, 128), 1)
        for hh in range(HEADS):
            @pl.loop(0, runs)
            def _(run):
                cosine, sine = trig[hh, 0, pl.ds(run, 1)], trig[hh, 1, pl.ds(run, 1)]
                full = sine * step_in[0] + cosine * step_in[1]
                here = pl.ds(hh * STRIPE, STRIPE)
                v_turn[0, run, here] = cosine * step_in[0] - sine * step_in[1]
                v_turn[1, run, here] = jnp.where(lane < ROT // 2, -full, 0.0)
                v_turn[2, run, here] = jnp.where(lane < ROT // 2, 0.0, full)
        if not fuse:
            save(v_turn, turn_out)

    def rows_done(side, src, dst):
        side()
        if not fuse:
            save(src, dst)

    flipped = []

    def flip(src, dst, t):
        spot = flat.at[len(flipped) % 2]
        if len(flipped) >= 2:
            flipped[-2].wait()
        spot[...] = src[..., t * 256 : (t + 1) * 256].reshape(runs * per_run, 256).T
        copy = pltpu.make_async_copy(spot, dst.at[t * 256 : (t + 1) * 256], flat_sem.at[len(flipped) % 2])
        copy.start()
        flipped.append(copy)

    expand_at, dense_at = 3, 4
    shrink = list(range(5, len(cuts)))
    step(0, trig_send)
    step(0.01, n_first_z)
    step(0.01, n_first_y)
    for k in range(3):
        step(0.02, w_first, k, 1)
        step(0.02, w_first, k, 0)
    step(0.2, note_first)
    step(3, note_cross)
    step(6, note_out)
    for k in range(3):
        step(31 + 4 * k, w_across, k)
        step(43 + 5 * k, w_beside, k)
        step(66, w_ready, k)
    step(16, n_near)
    step(27, n_far)
    step(36.1, w_first, expand_at, 0)
    step(52, n_last)
    step(41, w_first, expand_at, 1)
    step(52.2, w_first, dense_at, 1)
    step(52.3, w_first, dense_at, 0)
    step(52.4, g_first_z)
    step(52.5, g_first_y)
    step(55, turn_tables)
    step(57, note_sum)
    step(65, rows_done, n_side, v_n, n_out)
    step(64.9, w_across, expand_at)
    step(86, w_across, dense_at)
    step(86.1, g_near)
    step(95, g_far)
    for g in shrink:
        step(95.1, w_first, g, 1)
        step(95.2, w_first, g, 0)
    step(96, w_beside, expand_at)
    step(97, w_ready, expand_at)
    step(118.5, g_last)
    step(127.5, w_beside, dense_at)
    step(134, rows_done, g_side, v_g, g_out)
    step(134.1, w_ready, dense_at)
    for k, g in enumerate(shrink):
        step((128, 130, 132, 138.5)[k], w_across, g)
        step((141, 145, 149, 152)[k], w_beside, g)
        step(156, w_ready, g)
    if fuse:
        kv_sends = []
        tile = 256

        def weight(first):
            return v_w[..., first : first + tile].reshape(width, tile)

        def bias_of(t):
            return jnp.concatenate([note_h[h, 2 * t : 2 * t + 1], note_h[h, 2 * t + 1 : 2 * t + 2]], 1)

        parts = 4
        span = runs // parts
        slot = x * 2 + c

        def project(p):
            lo = p * span
            left = v_n[lo : lo + span].reshape(span * per_run, width)
            tables = [v_turn[t, lo : lo + span].reshape(span * per_run, 128) for t in range(3)]
            for t in range(3):
                value = jnp.dot(left, weight(t * HEAD_DIM), preferred_element_type=F32) + bias_of(t)
                if t < 2:
                    value = turn(value, tables, 1.0)
                if t == 0:
                    v_q[lo : lo + span] = (value * (1.0 / math.sqrt(HEAD_DIM))).astype(BF).reshape(span, per_run, HEAD_DIM)
                else:
                    here = pl.ds((t - 1) * HEAD_DIM, HEAD_DIM)
                    v_kv[lo : lo + span, slot, :, here] = value.astype(BF).reshape(span, per_run, HEAD_DIM)
            block = v_kv.at[lo : lo + span, slot]
            kv_sends.append(send(block, block, kx_s.at[p], kx_r.at[p], place.peer_x()))
            kv_sends.append(send(block, block, kc_s.at[0, p], kc_r.at[0, p], place.peer_c()))

        def kv_beside(p):
            block = v_kv.at[pl.ds(p * span, span), (1 - x) * 2 + c]
            remote(block, block, kx_s.at[p], kx_r.at[p], place.peer_x()).wait_recv()
            kv_sends.append(send(block, block, kc_s.at[1, p], kc_r.at[1, p], place.peer_c()))

        def kv_ready(p):
            for k, xx in ((0, x), (1, 1 - x)):
                block = v_kv.at[pl.ds(p * span, span), xx * 2 + 1 - c]
                remote(block, block, kc_s.at[k, p], kc_r.at[k, p], place.peer_c()).wait_recv()

        half = runs * per_run // 2

        def expand(m, t):
            left = v_n[m * runs // 2 : (m + 1) * runs // 2].reshape(half, width)
            value = jnp.dot(left, weight(cuts[expand_at][0] + t * tile), preferred_element_type=F32) + bias_of(3 + t)
            sigma = 0.5 * (1.0 + lax.erf(value * math.sqrt(0.5)))
            slope = sigma + value * jnp.exp(-0.5 * value * value) * (1.0 / math.sqrt(2 * math.pi))
            v_slope[m * half : (m + 1) * half, t * tile : (t + 1) * tile] = slope
            first = HEAD_DIM + t * tile
            v_left[m * half : (m + 1) * half, first : first + tile] = (value * sigma).astype(BF)

        def shrink_back(m, t):
            left = v_g[m * runs // 2 : (m + 1) * runs // 2].reshape(half, width)
            value = jnp.dot(left, weight(cuts[shrink[0]][0] + t * tile), preferred_element_type=F32)
            value = value * v_slope[m * half : (m + 1) * half, t * tile : (t + 1) * tile]
            first = 3 * HEAD_DIM + t * tile
            v_right[m * half : (m + 1) * half, first : first + tile] = value.astype(BF)


        def token_tables():
            tokens = token_ref[...]
            starts = [
                jnp.min(jnp.where(tokens // run_size == k, tokens, far_off), 1, keepdims=True) for k in range(runs)
            ]
            base = jnp.concatenate(starts, 1)
            parts_of = [(base // 64).astype(F32).astype(BF), (base % 64).astype(F32).astype(BF)]
            row = lax.broadcasted_iota(jnp.int32, (per_run, devices), 0)
            owner = x * (2 * HEADS) + row // STRIPE * 2 + c
            pick_row = owner == lax.broadcasted_iota(jnp.int32, (per_run, devices), 1)
            pick_row = jnp.where(pick_row, 1.0, 0.0).astype(BF)
            lane = lax.broadcasted_iota(jnp.int32, (devices, 4 * per_run), 1)
            group = lane // per_run
            owner = group // 2 * (2 * HEADS) + lane % per_run // STRIPE * 2 + group % 2
            pick_col = owner == lax.broadcasted_iota(jnp.int32, (devices, 4 * per_run), 0)
            pick_col = jnp.where(pick_col, 1.0, 0.0).astype(BF)
            high, low = (jnp.dot(pick_row, part, preferred_element_type=F32) for part in parts_of)
            within = lax.broadcasted_iota(jnp.int32, (per_run, runs), 0) % STRIPE
            row_tok[...] = (high * 64 + low).astype(jnp.int32) + within
            turn_over = (((0,), (0,)), ((), ()))
            high, low = (
                lax.dot_general(part, pick_col, turn_over, preferred_element_type=F32) for part in parts_of
            )
            within = lax.broadcasted_iota(jnp.int32, (runs, 4 * per_run), 1) % STRIPE
            col_tok[...] = (high * 64 + low).astype(jnp.int32) + within

        step(74, token_tables)

        def segment(tokens):
            return jnp.where(tokens < prompt_total, -1 - tokens // PROMPT, (tokens - prompt_total) // CONT)

        def mask(i, k):
            if i != k:
                return None
            rows, cols = row_tok[:, i : i + 1], col_tok[i : i + 1, :]
            return (segment(rows) == segment(cols)) & (cols <= rows)

        def attended_back():
            for m in range(2):
                left = v_g[m * runs // 2 : (m + 1) * runs // 2].reshape(half, width)
                value = jnp.dot(left, weight(cuts[dense_at][0]), preferred_element_type=F32)
                v_do[m * runs // 2 : (m + 1) * runs // 2] = value.astype(BF).reshape(runs // 2, per_run, HEAD_DIM)

        def key(k):
            return v_kv[k, :, :, :HEAD_DIM].reshape(4 * per_run, HEAD_DIM)

        def value_of(k):
            return v_kv[k, :, :, HEAD_DIM:].reshape(4 * per_run, HEAD_DIM)

        def attend(i):
            here = slice(i * per_run, (i + 1) * per_run)
            out, total = attention_forward(i, prompt_runs, mask, v_q, key, value_of, s_ref)
            v_out[here], lse[:, i : i + 1] = out, total
            v_left[here, :HEAD_DIM] = out.astype(BF)

        def attend_back(i):
            here = slice(i * per_run, (i + 1) * per_run)
            back = attention_backward(
                i, prompt_runs, mask, v_q, v_do, key, value_of, v_out[here], lse[:, i : i + 1], v_turn, sum_ref
            )
            v_right[here, :HEAD_DIM] = back.astype(BF)

        def fold_first():
            for copy in kv_sends:
                copy.wait_send()
            sends[:] = [one for one in sends if not any(one is other for other in kv_sends)]
            v_kv[...] = sum_ref[...].astype(BF).reshape(v_kv.shape)
            for k, xx in ((0, 1 - x), (1, x)):
                state["fold", k] = send(
                    v_kv.at[:, xx * 2 + 1 - c], kv_c.at[:, k], fc_s.at[k], fc_r.at[k], place.peer_c()
                )

        def fold_add(k, final):
            state["fold", k].wait_recv()
            mine_slot = (x if k else 1 - x) * 2 + c

            @pl.loop(0, runs)
            def _(run):
                value = v_kv[run, mine_slot].astype(F32) + kv_c[run, k].astype(F32)
                if final:
                    value = value + kv_x[run].astype(F32)
                    back = turn(value[:, :HEAD_DIM].astype(BF).astype(F32), [v_turn[t, run] for t in range(3)], -1.0)
                    here = pl.ds(pl.multiple_of(run * per_run, per_run), per_run)
                    v_right[here, HEAD_DIM : 2 * HEAD_DIM] = back.astype(BF)
                    v_right[here, 2 * HEAD_DIM : 3 * HEAD_DIM] = value[:, HEAD_DIM:].astype(BF)
                else:
                    kv_c[run, k] = value.astype(BF)

        def fold_cross():
            fold_add(0, False)
            state["fold_x"] = send(kv_c.at[:, 0], kv_x, fx_s.at[0], fx_r.at[0], place.peer_x())

        def fold_close():
            state["fold_x"].wait_recv()
            fold_add(1, True)
            save(v_right.at[:, pl.ds(0, 3 * HEAD_DIM)], right_out.at[:, pl.ds(0, 3 * HEAD_DIM)])

        chunks, early, wide = o_p.shape[0], o_y.shape[0], o_p.shape[-1]

        def out_part(q):
            for k in range(wide // tile):
                n = q * (wide // tile) + k
                per_x = width // 2 // tile
                low = n % per_x * HEADS // per_x
                some = v_w[n // per_x, 0, low : low + HEADS // per_x, :, :, cuts[dense_at][0] :]
                value = lax.dot_general(
                    v_left[...], some.reshape(tile, v_left.shape[1]), (((1,), (1,)), ((), ())), preferred_element_type=F32
                )
                o_p[q, :, :, :, :, :, k * tile : (k + 1) * tile] = value.astype(BF).reshape(runs, 2, 2, 2, STRIPE, tile)
            if q < early:
                state["out", q] = send(
                    o_p.at[q, :, :, :, 1 - place.hy], o_y.at[q], oy_s.at[q], oy_r.at[q], place.peer_y()
                )
            else:
                save(o_p.at[q], part_out.at[q - early])

        def out_side(q):
            state["out", q].wait_recv()

            @pl.loop(0, runs)
            def _(run):
                for t in range(LINE):
                    value = o_y[q, run, t // 2, t % 2].astype(F32) + o_p[q, run, t // 2, t % 2, place.hy].astype(F32)
                    o_y[q, run, t // 2, t % 2] = value.astype(BF)

            save(o_y.at[q], half_out.at[q])

        for p in range(parts):
            step(67 + 2 * p, project, p)
            step(108.5 + 2 * p, kv_beside, p)
            step(118, kv_ready, p)
        for i in range(runs):
            step(119 + i, attend, i)
            step(135 + 2 * i, attend_back, i)
            step(75, flip, v_n, n_out, i)
            step(163, flip, v_g, g_out, i)
        count = v_slope.shape[1] // tile
        for t in range(count):
            for m in range(2):
                step(97.51 + 0.1 * t + 0.05 * m, expand, m, t)
                step(161 + 0.1 * t, shrink_back, m, t)
        step(134.5, attended_back)
        step(151.5, fold_first)
        step(155, fold_cross)
        for q in range(chunks):
            step(156.5 + 0.1 * q if q < early else 162, out_part, q)
        for q in range(early):
            step(172 + 12 * q, out_side, q)
        step(157, save, v_left, left_out)
        step(161.9, save, v_right.at[:, pl.ds(3 * HEAD_DIM, v_slope.shape[1])], right_out.at[:, pl.ds(3 * HEAD_DIM, v_slope.shape[1])])
        step(183, fold_close)
    for _, _, body, given in sorted(plan, key=lambda one: one[:2]):
        body(*given)
    for copy in puts + flipped[-2:]:
        copy.wait()
    for copy in sends:
        copy.wait_send()
    n_sent()
    g_sent()


def open_all(ways, prompt_runs, prompt_total, inputs, cotangent, tokens, positions, scales, biases, qkv, expand, dense, shrink):
    tok_dev, width = inputs.shape
    rows, hidden = qkv.shape[0], expand.shape[1] // HEADS
    runs = tok_dev // STRIPE
    columns = 3 * HEAD_DIM + hidden + HEAD_DIM + hidden
    note_rows = -(-((3 * HEAD_DIM + hidden) // 128 + width // 128) // 8) * 8
    notes = jax.ShapeDtypeStruct((HEADS, note_rows, 128), F32)
    trig = jax.ShapeDtypeStruct((2, runs, 128), F32)

    frequency = np.float32(10000.0) ** (-np.arange(0, ROT, 2, dtype=np.float32) / np.float32(ROT))
    lanes_of = np.pad(np.concatenate([frequency, frequency]), (0, 128 - ROT))[None].astype(np.float32)
    step_angles = np.arange(STRIPE, dtype=np.float32)[:, None] * lanes_of
    turned = np.arange(128)[None] < ROT
    steps = np.stack([np.where(turned, np.cos(step_angles), 1.0), np.where(turned, np.sin(step_angles), 0.0)])
    lanes_of, steps = jnp.asarray(lanes_of), jnp.asarray(steps.astype(np.float32))
    fuse = ways == 1 and prompt_total == PROMPT
    head3 = 3 * HEAD_DIM
    cuts = [(k * HEAD_DIM, HEAD_DIM) for k in range(3)] + [(head3, hidden), (head3 + hidden, HEAD_DIM)]
    cuts += [(head3 + hidden + HEAD_DIM + k * 256, 256) for k in range(hidden // 256)]
    blocks = (2, ways, HEADS, 2, rows, columns)
    group = runs * HEADS * STRIPE
    per_run = HEADS * STRIPE

    def shape(dims, kind=BF):
        return jax.ShapeDtypeStruct(dims, kind)

    gathered = (runs, HEADS, STRIPE, width)
    tables = (3, runs, per_run, 128)
    chunks, wide = 4, width // 4
    kept = head3 + hidden if fuse else columns
    outs = [
        shape((width, group) if fuse else gathered), shape((width, group) if fuse else gathered), shape(blocks[:-1] + (kept,)), shape(notes.shape[1:], F32),
        shape((1, 1, 8, 128) if fuse else tables, F32), shape(notes.shape[1:], F32),
    ]
    if fuse:
        outs += [
            shape((group, HEAD_DIM + hidden)), shape((group, head3 + hidden)),
            shape((EARLY, runs, 2, 2, STRIPE, wide)), shape((chunks - EARLY, runs, 2, 2, 2, STRIPE, wide)),
        ]
    extra = max(ways - 1, 1)
    count = len(cuts)
    scratch = [
        pltpu.VMEM(gathered, BF), pltpu.VMEM(gathered, BF), pltpu.VMEM(blocks, BF), pltpu.VMEM(tables, F32),
        pltpu.VMEM((HEADS,) + trig.shape, F32),
        pltpu.VMEM(notes.shape, F32), pltpu.VMEM(notes.shape, F32), pltpu.VMEM(notes.shape, F32),
        pltpu.VMEM((extra,) + notes.shape if ways > 1 else (1, 1, 8, 128), F32), pltpu.VMEM(notes.shape, F32),
        DMA((3 + count,)), DMA((count + 15,)),
        pltpu.VMEM(qkv.shape, BF), pltpu.VMEM(expand.shape, BF), pltpu.VMEM(trig.shape, F32),
        pltpu.VMEM(((3 * width + HEADS * hidden + width) // 128 + 8, 128), F32), pltpu.VMEM(notes.shape[1:], F32),
        DMA((7,)), DMA((HEADS,)), DMA((7,)), DMA((HEADS,)),
        DMA((count, ways * HEADS)), DMA((count, ways, HEADS)), DMA((count,)), DMA((count,)), DMA((count, 2)), DMA((count, 2)),
        DMA((HEADS,)), DMA((HEADS,)), DMA((1,)), DMA((1,)), DMA((1,)), DMA((1,)), DMA((extra,)), DMA((extra,)),
        DMA((HEADS,)), DMA((HEADS,)),
    ]
    if fuse:
        scratch += [
            pltpu.VMEM((runs, per_run, HEAD_DIM), BF), pltpu.VMEM((runs, per_run, HEAD_DIM), BF),
            pltpu.VMEM((runs, 4, per_run, 2 * HEAD_DIM), BF), pltpu.VMEM((group, hidden), F32),
            pltpu.VMEM((group, HEAD_DIM + hidden), BF), pltpu.VMEM((group, head3 + hidden), BF),
            pltpu.VMEM((group, HEAD_DIM), F32), pltpu.VMEM((per_run, runs), F32),
            pltpu.VMEM((per_run, (prompt_runs + 1) * 4 * per_run), F32),
            pltpu.VMEM((runs, 4 * per_run, 2 * HEAD_DIM), F32),
            pltpu.VMEM((runs, 2, per_run, 2 * HEAD_DIM), BF), pltpu.VMEM((runs, per_run, 2 * HEAD_DIM), BF),
            pltpu.VMEM((chunks, runs, 2, 2, 2, STRIPE, wide), BF), pltpu.VMEM((EARLY, runs, 2, 2, STRIPE, wide), BF),
            pltpu.VMEM((2, 256, group), BF), DMA((2,)),
            pltpu.VMEM((per_run, runs), jnp.int32), pltpu.VMEM((runs, 4 * per_run), jnp.int32),
            DMA((4,)), DMA((4,)), DMA((2, 4)), DMA((2, 4)),
            DMA((2,)), DMA((2,)), DMA((1,)), DMA((1,)), DMA((EARLY,)), DMA((EARLY,)),
        ]
    return fuse, pl.pallas_call(
        functools.partial(open_kernel, ways, tuple(cuts), fuse, prompt_runs, prompt_total),
        out_shape=tuple(outs),
        in_specs=[VMEM] * 14 + [ANY] * 4,
        out_specs=(ANY,) * len(outs),
        scratch_shapes=scratch,
        compiler_params=pltpu.CompilerParams(collective_id=0, has_side_effects=True, vmem_limit_bytes=62 * 2**20),
    )(
        inputs, cotangent, tokens, positions, *scales, *biases, lanes_of, steps, qkv, expand, dense, shrink
    )


def exchange_kernel(ways, own, full, local, to_w, to_x, to_c, recv):
    place = Place(ways)
    x, w, c = place.x, place.w, place.c
    runs = own.shape[0]
    parts = 4
    span = runs // parts
    greet(place.peers_w() + [place.peer_x(), place.peer_c()])

    def spot(ws, xs, cs, p):
        return full.at[pl.ds(p * span, span), ws * 4 + xs * 2 + cs]

    sends = []

    def send(src, ws, xs, cs, p, sem, device):
        copy = remote(src, spot(ws, xs, cs, p), sem, recv.at[ws, xs, cs, p], device)
        copy.start()
        sends.append(copy)

    def arrived(ws, xs, cs, p):
        remote(spot(ws, xs, cs, p), spot(ws, xs, cs, p), local.at[0], recv.at[ws, xs, cs, p], place.peer_x()).wait_recv()

    keep = pltpu.make_async_copy(own, full.at[:, w * 4 + x * 2 + c], local.at[0])
    for p in range(parts):
        src = own.at[pl.ds(p * span, span)]
        for k, device in enumerate(place.peers_w()):
            send(src, w, x, c, p, to_w.at[k, p], device)
        send(src, w, x, c, p, to_x.at[w, p], place.peer_x())
    for p in range(parts):
        send(own.at[pl.ds(p * span, span)], w, x, c, p, to_c.at[w, x, p], place.peer_c())
    keep.start()
    for k in range(1, ways):
        ws = (w - k) % ways
        for p in range(parts):
            arrived(ws, x, c, p)
            send(spot(ws, x, c, p), ws, x, c, p, to_x.at[ws, p], place.peer_x())
            send(spot(ws, x, c, p), ws, x, c, p, to_c.at[ws, x, p], place.peer_c())
    for k in range(ways):
        ws = (w - k) % ways
        for p in range(parts):
            arrived(ws, 1 - x, c, p)
            send(spot(ws, 1 - x, c, p), ws, 1 - x, c, p, to_c.at[ws, 1 - x, p], place.peer_c())
    for k in range(ways):
        ws = (w - k) % ways
        for p in range(parts):
            arrived(ws, x, 1 - c, p)
            arrived(ws, 1 - x, 1 - c, p)
    keep.wait()
    for copy in sends:
        copy.wait_send()


def exchange(ways, own):
    runs, rows, columns = own.shape
    return call(
        functools.partial(exchange_kernel, ways),
        jax.ShapeDtypeStruct((runs, 4 * ways, rows, columns), BF),
        (own,),
        [DMA((1,)), DMA((ways, 4)), DMA((ways, 4)), DMA((ways, 2, 4)), DMA((ways, 2, 2, 4))],
        1,
    )


def turn(u, tables, sign):
    cosine, lower, upper = tables
    front = u[:, :128]
    moved = pltpu.roll(front, 96, 1) * lower + pltpu.roll(front, 32, 1) * upper
    return jnp.concatenate([front * cosine + moved * sign, u[:, 128:]], 1)


def finish_kernel(ways, early, left, right, w_all, n_all, g_all, note, half_in, part_in,
                  out_sum, e_sum, own_a, own_b, note_all,
                  v_left, v_right, v_w, o_own, o_y, o_1, o_2, e_p, e_y, e_1, e_2,
                  raw, ring, a_c, a_x, a_w, b_c, b_x, b_w, n_mine, n_c, n_x, n_w,
                  load, load_raw, load_o,
                  oy_s, oy_r, o1_s, o1_r, o2_s, o2_r, ey_s, ey_r, e1_s, e1_r, e2_s, e2_r,
                  ac_s, ac_r, ax_s, ax_r, aw_s, aw_r, ah_s, ah_r,
                  bc_s, bc_r, bx_s, bx_r, bw_s, bw_r, bh_s, bh_r, keep, n_s, n_r):
    place = Place(ways)
    x, w, h, c, hy, hz = place.x, place.w, place.h, place.c, place.hy, place.hz
    d0, d1 = hz % 2, hz // 2
    runs = v_left.shape[0]
    chunks = e_p.shape[0]
    wide = e_p.shape[-1]
    rows = own_a.shape[1]
    hp = 256 // (2 * rows)
    tiles = HEADS // hp
    a_cols, b_cols = own_a.shape[2], own_b.shape[2]
    inner = v_left.shape[-1]
    head3 = 3 * HEAD_DIM
    group = runs * HEADS * STRIPE
    sends = []

    def send(src, dst, s, r, device):
        copy = remote(src, dst, s, r, device)
        copy.start()
        sends.append(copy)
        return copy

    greet(place.peers_h() + place.peers_w() + [place.peer_x(), place.peer_c()])

    def fetch(src, dst, sem):
        copy = pltpu.make_async_copy(src, dst, sem)
        copy.start()
        return copy


    def partial(src, q, buf, depth):
        @pl.loop(0, wide // 256)
        def _(k):
            at = pl.multiple_of(k * 256, 256)
            value = lax.dot_general(
                src[...].reshape(group, depth),
                v_w[pl.ds(pl.multiple_of(q * wide + at, 256), 256), :depth],
                (((1,), (1,)), ((), ())),
                preferred_element_type=F32,
            )
            buf[q, :, :, :, :, :, pl.ds(at, 256)] = value.astype(BF).reshape(runs, 2, 2, 2, STRIPE, 256)

    def sums(mine, y, one, two, s_1, r_1, s_2, r_2, total):
        def near(q):
            target = place.device(h=(hz + 1 - 2 * d0) * 2 + hy)
            return send(y.at[q, :, :, 1 - d0], one.at[q], s_1.at[q], r_1.at[q], target)

        def after_y(q, copy):
            copy.wait_recv()

            @pl.loop(0, runs)
            def _(run):
                for t in range(LINE):
                    value = y[q, run, t // 2, t % 2].astype(F32) + mine(q, run, t).astype(F32)
                    y[q, run, t // 2, t % 2] = value.astype(BF)

            return near(q)

        def after_1(q, copy):
            copy.wait_recv()

            @pl.loop(0, runs)
            def _(run):
                for t in range(2):
                    value = one[q, run, t].astype(F32) + y[q, run, t, d0].astype(F32)
                    one[q, run, t] = value.astype(BF)

            target = place.device(h=((1 - d1) * 2 + d0) * 2 + hy)
            return send(one.at[q, :, 1 - d1], two.at[q], s_2.at[q], r_2.at[q], target)

        def after_2(q, copy):
            copy.wait_recv()

            @pl.loop(0, runs)
            def _(run):
                total[run, :, q * wide : (q + 1) * wide] = two[q, run].astype(F32) + one[q, run, d1].astype(F32)

        return near, after_y, after_1, after_2

    o_near, o_after_y, o_after_1, o_after_2 = sums(
        lambda q, run, t: o_own[q - (early or 0), run, t // 2, t % 2], o_y, o_1, o_2, o1_s, o1_r, o2_s, o2_r, out_sum
    )
    _, e_after_y, e_after_1, e_after_2 = sums(
        lambda q, run, t: e_p[q, run, t // 2, t % 2, hy], e_y, e_1, e_2, e1_s, e1_r, e2_s, e2_r, e_sum
    )

    order_t = [(k, dw, dt) for k in range(2) for dw in list(range(1, ways)) + [0] for dt in list(range(1, tiles)) + [0]]
    own_t = h // hp

    def where(k, dw, dt):
        return (1 - x if k == 0 else x), (w + dw) % ways, (own_t + dt) % tiles

    def product(m, buf, src, first, count, at):
        @pl.loop(0, count // 256)
        def _(k):
            col = pl.multiple_of(k * 256, 256)
            value = jnp.dot(
                raw[m % 2, buf], src[..., pl.ds(first + col, 256)].reshape(group, 256), preferred_element_type=F32
            )
            ring[m % 3, :, :, :, pl.ds(at + col, 256)] = value.astype(BF).reshape(hp, 2, rows, 256)

    made, order_m = [], []

    def raw_copies(m):
        n, need = order_m[m]
        xs, ws, t = where(*order_t[n])
        at = pl.multiple_of(((xs * ways + ws) * tiles + t) * 256, 256)
        return [
            pltpu.make_async_copy(src.at[pl.ds(at, 256)], raw.at[m % 2, buf], load_raw.at[m % 2, buf])
            for buf, src in need
        ]

    def begin(m):
        if m < len(order_m):
            for copy in raw_copies(m):
                copy.start()

    def grads(cols, from_c, from_x, from_w, c_s, c_r, x_s, x_r, w_s, w_r, h_s, h_r, out, fill, flag):
        first, second, third, spot = {}, {}, {}, {}

        def make(n):
            m = len(made)
            if m >= 3:
                made[m - 3].wait_send()
            for copy in raw_copies(m):
                copy.wait()
            fill(m)
            begin(m + 1)
            k, dw, dt = order_t[n]
            first[n] = remote(
                ring.at[m % 3, :, 1 - c, :, pl.ds(0, cols)], from_c.at[k, dw, dt], c_s.at[n], c_r.at[n], place.peer_c()
            )
            first[n].start()
            spot[n] = m % 3
            made.append(first[n])

        def mine(n):
            k, dw, dt = order_t[n]
            first[n].wait_recv()

            @pl.loop(0, hp)
            def _(q):
                value = from_c[k, dw, dt, q].astype(F32) + ring[spot[n], q, c, :, :cols].astype(F32)
                from_c[k, dw, dt, q] = value.astype(BF)

        def cross(n):
            k, dw, dt = order_t[n]
            second[dw, dt] = send(from_c.at[0, dw, dt], from_x.at[dw, dt], x_s.at[dw, dt], x_r.at[dw, dt], place.peer_x())

        def close(n):
            k, dw, dt = order_t[n]
            _, ws, t = where(k, dw, dt)
            second[dw, dt].wait_recv()
            more = [from_x.at[dw, dt]]
            if dw == 0:
                for dv in range(1, ways):
                    third[dv, dt].wait_recv()
                    more.append(from_w.at[dv - 1, dt])

            @pl.loop(0, hp)
            def _(q):
                value = from_c[1, dw, dt, q].astype(F32)
                for ref in more:
                    value = value + ref[q].astype(F32)
                from_c[1, dw, dt, q] = value.astype(BF)

            if dw != 0:
                third[dw, dt] = send(from_c.at[1, dw, dt], from_w.at[dw - 1, dt], w_s.at[dw - 1, dt], w_r.at[dw - 1, dt], place.device(w=ws))
                return
            for q in range(hp):
                hs = t * hp + q
                at = dt * hp + q

                @pl.when(hs != h)
                def _():
                    remote(from_c.at[1, 0, dt, q], out.at[h], h_s.at[at], h_r.at[h], place.device(h=hs)).start()

                @pl.when(hs == h)
                def _():
                    pltpu.make_async_copy(from_c.at[1, 0, dt, q], out.at[h], keep.at[flag]).start()

        def end():
            for n in range(len(order_t)):
                k, dw, dt = order_t[n]
                if k == 1 and dw == 0:
                    _, _, t = where(k, dw, dt)
                    for q in range(hp):
                        hs = t * hp + q

                        @pl.when(hs != h)
                        def _():
                            remote(from_c.at[1, 0, dt, q], out.at[h], h_s.at[dt * hp + q], h_r.at[h], place.device(h=hs)).wait_send()
            for dh in range(1, HEADS):
                hs = (h + dh) % HEADS
                remote(out.at[hs], out.at[hs], h_s.at[0], h_r.at[hs], place.peer_x()).wait_recv()
            pltpu.make_async_copy(from_c.at[1, 0, 0, 0], out.at[h], keep.at[flag]).wait()

        return make, mine, cross, close, end

    def fill_a(m):
        product(m, 1, v_left, 0, inner, 0)
        product(m, 0, v_right, head3, a_cols - inner, inner)

    def fill_b(m):
        product(m, 0, v_right, 0, head3, 0)

    a_make, a_mine, a_cross, a_close, a_end = grads(
        a_cols, a_c, a_x, a_w, ac_s, ac_r, ax_s, ax_r, aw_s, aw_r, ah_s, ah_r, own_a, fill_a, 0
    )
    b_make, b_mine, b_cross, b_close, b_end = grads(
        b_cols, b_c, b_x, b_w, bc_s, bc_r, bx_s, bx_r, bw_s, bw_r, bh_s, bh_r, own_b, fill_b, 1
    )
    count = len(order_t)
    half = count // 2
    order_m += [(n, ((0, n_all), (1, g_all))) for n in A_ORDER] + [(n, ((0, n_all),)) for n in A_ORDER]

    plan = []

    def step(time, body, *given):
        plan.append((time, len(plan), body, given))

    state = {}

    def wait_all(copies):
        for copy in copies:
            copy.wait()

    def e_part(q):
        partial(v_right, q, e_p, v_right.shape[-1])
        state["e", q] = send(e_p.at[q, :, :, :, 1 - hy], e_y.at[q], ey_s.at[q], ey_r.at[q], place.peer_y())

    def o_start():
        for q in range(early, chunks):
            state["o", q] = send(part_in.at[q - early, :, :, :, 1 - hy], o_y.at[q], oy_s.at[q], oy_r.at[q], place.peer_y())
        for q in range(chunks):
            if q < early:
                state["o_load", q] = fetch(half_in.at[q], o_y.at[q], load_o.at[q])
            else:
                state["o_load", q] = fetch(part_in.at[q - early, :, :, :, hy], o_own.at[q - early], load_o.at[q])

    def o_first(q):
        state["o_load", q].wait()
        if q < early:
            state["o", q] = o_near(q)
        else:
            state["o", q] = o_after_y(q, state["o", q])

    def advance(key, body, q):
        state[key, q] = body(q, state[key, q])

    note_w = []
    base = 1 + ways

    def note_sums():
        state["note_load"].wait()

        @pl.loop(0, v_right.shape[-1] // 128)
        def _(k):
            at = pl.multiple_of(k * 128, 128)
            value = v_right[..., pl.ds(at, 128)].reshape(group, 128).astype(F32)
            n_mine[pl.ds(k, 1), :] = jnp.sum(value, 0, keepdims=True)

        state["note"] = send(n_mine, n_c, n_s.at[0], n_r.at[0], place.peer_c())

    def note_cross():
        state["note"].wait_recv()
        n_c[...] = n_c[...] + n_mine[...]
        state["note"] = send(n_c, n_x, n_s.at[1], n_r.at[1], place.peer_x())

    def note_ways():
        state["note"].wait_recv()
        n_x[...] = n_x[...] + n_c[...]
        for k, device in enumerate(place.peers_w()):
            note_w.append(send(n_x, n_w.at[k], n_s.at[2 + k], n_r.at[2 + k], device))

    def note_out():
        if ways > 1:
            wait_all(note_w)
            total = n_x[...]
            for k in range(ways - 1):
                total = total + n_w[k]
            n_x[...] = total
        for dh in range(1, HEADS):
            send(n_x, note_all.at[h], n_s.at[base + dh], n_r.at[base + h], place.device(h=(h + dh) % HEADS))
        state["note_keep"] = pltpu.make_async_copy(n_x, note_all.at[h], keep.at[3])
        state["note_keep"].start()

    if early is not None:
        o_start()
    state["note_load"] = fetch(note, n_mine, keep.at[2])
    loads = [fetch(right, v_right, load.at[0]), fetch(left, v_left, load.at[1])]
    begin(0)
    w_load = fetch(w_all.at[:, pl.ds(0, v_right.shape[-1])], v_w, load.at[2])
    if early is not None:
        for q, times in enumerate(((0.5, 9, 19.5), (0.6, 14.5, 25), (14.2, 37, 49), (26, 48.2, 62))):
            step(times[0], o_first, q)
            step(times[1], advance, "o", o_after_1, q)
            step(times[2], advance, "o", o_after_2, q)
    step(1, wait_all, loads)
    for i, (n, time) in enumerate(zip(A_ORDER, (2, 4.5, 10, 15, 19.6, 26.2, 31, 36), strict=True)):
        step(time, a_make, n)
        if i > 0:
            step(time, a_mine, A_ORDER[i - 1])
            if A_ORDER[i - 1] < half:
                step(time, a_cross, A_ORDER[i - 1])
    step(38, a_mine, A_ORDER[-1])
    step(7.2, w_load.wait)
    for q in range(chunks):
        step((7.3, 13, 17.5, 22.5)[q], e_part, q)
    step(25.5, note_sums)
    step(36.5, note_cross)
    step(60, note_ways)
    step(60, note_out)
    for i, (n, time) in enumerate(zip(A_ORDER, (39, 40, 41, 42, 44, 45, 46, 47), strict=True)):
        step(time, b_make, n)
        if i > 0:
            step(time, b_mine, A_ORDER[i - 1])
            if A_ORDER[i - 1] < half:
                step(time, b_cross, A_ORDER[i - 1])
    step(47.5, b_mine, A_ORDER[-1])
    for n, times in zip(range(half, count), ((22, 77.5), (35.5, 79), (60, 84), (67, 88)), strict=True):
        step(times[0], a_close, n)
        step(times[1], b_close, n)
    for q, times in enumerate(((48, 66, 80), (49.2, 78, 92), (62, 89, 104), (76, 101, 114))):
        step(times[0], advance, "e", e_after_y, q)
        step(times[1], advance, "e", e_after_1, q)
        step(times[2], advance, "e", e_after_2, q)
    for _, _, body, given in sorted(plan, key=lambda one: one[:2]):
        body(*given)
    for copy in made[-3:]:
        copy.wait_send()
    a_end()
    b_end()
    state["note_keep"].wait()
    for dh in range(1, HEADS):
        hs = (h + dh) % HEADS
        remote(note_all.at[hs], note_all.at[hs], n_s.at[0], n_r.at[base + hs], place.peer_x()).wait_recv()
    for copy in sends:
        if not any(copy is other for other in note_w):
            copy.wait_send()


def finish(ways, rows, left, right, w_all, n_all, g_all, note, half, part):
    width = w_all.shape[0]
    inner, right_cols = left.shape[1], right.shape[1]
    head3 = 3 * HEAD_DIM
    a_cols, b_cols = inner + right_cols - head3, head3
    group = n_all.shape[1]
    runs = group // (HEADS * STRIPE)
    lines = (runs, LINE, 2, STRIPE)
    hp = 256 // (2 * rows)
    tiles = HEADS // hp
    chunks, wide = 4, width // 4
    extra = max(ways - 1, 1)
    count = 2 * ways * tiles
    assert count == len(A_ORDER)
    early = None if half is None else half.shape[0]

    def vm(shape, kind=BF):
        return pltpu.VMEM(shape, kind)

    def row_buffers(first, used):
        return [
            vm(first),
            vm((chunks, runs, 2, 2, STRIPE, wide) if used else (1, 1, 1, 1, 16, 128)),
            vm((chunks, runs, 2, STRIPE, wide) if used else (1, 1, 1, 16, 128)),
            vm((chunks, runs, STRIPE, wide) if used else (1, 1, 16, 128)),
        ]

    def spare(shape):
        return shape if ways > 1 else (1,) * (len(shape) - 2) + (16, 128)

    def gradient_buffers(cols):
        return [
            vm((2, ways, tiles, hp, rows, cols)),
            vm((ways, tiles, hp, rows, cols)),
            vm(spare((extra, tiles, hp, rows, cols))),
        ]

    def gradient_sems():
        return [
            DMA((count,)), DMA((count,)), DMA((ways, tiles)), DMA((ways, tiles)), DMA((extra, tiles)), DMA((extra, tiles)),
            DMA((HEADS,)), DMA((HEADS,)),
        ]

    scratch = (
        [
            vm(lines + (inner,)), vm(lines + (right_cols,)), vm((width, right_cols)),
        ]
        + row_buffers((max(chunks - (early or 0), 1), runs, 2, 2, STRIPE, wide) if early is not None else (1, 1, 1, 1, 16, 128), early is not None)
        + row_buffers((chunks, runs, 2, 2, 2, STRIPE, wide), True)
        + [vm((2, 2, 256, group)), vm((3, hp, 2, rows, a_cols))]
        + gradient_buffers(a_cols) + gradient_buffers(b_cols)
        + [vm(note.shape, F32)] * 3 + [vm((extra,) + note.shape, F32)]
        + [DMA((3,)), DMA((2, 2)), DMA((chunks,))]
        + [DMA((chunks,))] * 12
        + gradient_sems() + gradient_sems()
        + [DMA((4,)), DMA((1 + ways + HEADS,)), DMA((1 + ways + HEADS,))]
    )
    shapes = (
        jax.ShapeDtypeStruct((runs, STRIPE, width), F32),
        jax.ShapeDtypeStruct((runs, STRIPE, width), F32),
        jax.ShapeDtypeStruct((HEADS, rows, a_cols), BF),
        jax.ShapeDtypeStruct((HEADS, rows, b_cols), BF),
        jax.ShapeDtypeStruct((HEADS,) + note.shape, F32),
    )
    empty = jnp.zeros((1, 1, 1, 1, 16, 128), BF)
    ins = (
        left.reshape(lines + (inner,)), right.reshape(lines + (right_cols,)), w_all, n_all, g_all, note,
        empty if half is None else half, empty if part is None else part,
    )
    return pl.pallas_call(
        functools.partial(finish_kernel, ways, early),
        out_shape=shapes,
        in_specs=[ANY] * len(ins),
        out_specs=(VMEM, VMEM, ANY, ANY, ANY),
        scratch_shapes=scratch,
        compiler_params=pltpu.CompilerParams(collective_id=2, has_side_effects=True, vmem_limit_bytes=62 * 2**20),
    )(*ins)


def close_kernel(tokens, note, notes, gain_one, shift_one, gain_two, shift_two, *refs):
    sources, rest = refs[:8], refs[8:]
    (output, input_grad, gain_one_grad, shift_one_grad, gain_two_grad, shift_two_grad, qkv_out, qk_bias, v_bias, dense_out,
     dense_bias, expand_out, expand_bias, shrink_out, shrink_bias) = rest[:15]
    x_in, g_in, out_sum, e_sum, qkv_in, expand_in, own_a, own_b = kept = rest[15:23]
    qkv_grad, dense_grad, expand_grad, shrink_grad, load, put = rest[23:]
    loads = [pltpu.make_async_copy(src, dst, load.at[k]) for k, (src, dst) in enumerate(zip(sources, kept, strict=True))]
    for k in (6, 7, 4, 5, 0, 2, 1, 3):
        loads[k].start()
    saves = []

    def save(src, dst):
        copy = pltpu.make_async_copy(src, dst, put.at[len(saves)])
        copy.start()
        saves.append(copy)

    x, b = lax.axis_index("head"), lax.axis_index("blk")
    devices, rows = tokens.shape[0], qkv_in.shape[0]
    me = x * (devices // 2) + b
    width = x_in.shape[1]
    hidden = expand_in.shape[1] // HEADS
    head_rows, block_rows = HEAD_DIM // 128, (3 * HEAD_DIM + hidden) // 128

    square = lax.broadcasted_iota(jnp.int32, (rows, rows), 0) == lax.broadcasted_iota(jnp.int32, (rows, rows), 1)

    def down(ref):
        return jnp.sum(jnp.where(square, ref[...].astype(F32).reshape(1, rows), 0.0), 1, keepdims=True)

    def across(column):
        return jnp.sum(jnp.where(square, column, 0.0), 0, keepdims=True)

    def sums_of(h, first, count):
        return jnp.concatenate([notes[h, first + k : first + k + 1] for k in range(count)], 1)

    def one_norm(gain, shift, weight, grad, pieces):
        by_gain, by_shift = 0.0, 0.0
        for first, value, column_sums in pieces:
            count = value.shape[1]
            here = slice(first, first + count)
            kept = weight[:, here].astype(F32)
            grad[:, here] = gain * value + shift * column_sums
            by_gain = by_gain + jnp.sum(kept * value, 1, keepdims=True)
            by_shift = by_shift + jnp.sum(kept * column_sums, 1, keepdims=True)
        return across(by_gain), across(by_shift)

    qkv_pieces = (
        (t * width + h * HEAD_DIM, own_b[h, :, t * HEAD_DIM : (t + 1) * HEAD_DIM].astype(F32),
         sums_of(h, t * head_rows, head_rows))
        for h in range(HEADS) for t in range(3)
    )
    expand_pieces = (
        (h * hidden, own_a[h, :, HEAD_DIM + hidden :].astype(F32), sums_of(h, 3 * head_rows, hidden // 128))
        for h in range(HEADS)
    )
    loads[6].wait()
    for h in range(HEADS):
        shrink_grad[:, h * hidden : (h + 1) * hidden] = own_a[h, :, HEAD_DIM : HEAD_DIM + hidden].astype(F32)
    save(shrink_grad, shrink_out)
    for h in range(HEADS):
        dense_grad[:, h * HEAD_DIM : (h + 1) * HEAD_DIM] = own_a[h, :, :HEAD_DIM].astype(F32)
    save(dense_grad, dense_out)
    loads[5].wait()
    gain_two_grad[...], shift_two_grad[...] = one_norm(
        down(gain_two), down(shift_two), expand_in, expand_grad, expand_pieces
    )
    save(expand_grad, expand_out)
    loads[7].wait()
    loads[4].wait()
    gain_one_grad[...], shift_one_grad[...] = one_norm(down(gain_one), down(shift_one), qkv_in, qkv_grad, qkv_pieces)
    save(qkv_grad, qkv_out)
    for k in range(4):
        loads[k].wait()

    def share(row, count):
        return jnp.where(me % (128 // count) == 0, row[:, :count], row[:, 128 - count :])

    in_head = HEADS * head_rows
    third, rest = me // in_head, me % in_head
    qk_bias[...] = notes[pl.ds(rest // head_rows, 1), pl.ds(third * head_rows + rest % head_rows, 1)][0]
    half = me // 2
    v_bias[...] = share(notes[pl.ds(half // head_rows, 1), pl.ds(2 * head_rows + half % head_rows, 1)][0], rows)
    per_head = hidden // 128
    for k in range(2):
        row = me * 2 + k
        expand_bias[:, k * 128 : (k + 1) * 128] = notes[
            pl.ds(row // per_head, 1), pl.ds(3 * head_rows + row % per_head, 1)
        ][0]
    total = 0.0
    for h in range(HEADS):
        total = total + notes[pl.ds(h, 1), pl.ds(block_rows + half, 1)][0]
    dense_bias[...] = share(total, rows)
    shrink_bias[...] = share(total, rows)

    mine = tokens[pl.ds(me, 1), :]
    tok_dev = mine.shape[1]
    pick = lax.broadcasted_iota(jnp.int32, (tok_dev, tok_dev), 0) == mine // (devices * STRIPE) * STRIPE + mine % STRIPE
    pick = jnp.where(pick, 1.0, 0.0).astype(BF)

    def restored(value):
        value = value.astype(BF)
        return lax.dot_general(pick, value, (((0,), (0,)), ((), ())), preferred_element_type=F32).astype(BF)

    states = jnp.dot(pick, x_in[...], preferred_element_type=F32)
    bias = jnp.concatenate([note[block_rows + k : block_rows + k + 1] for k in range(width // 128)], 1)
    output[...] = restored(states + out_sum[...].reshape(tok_dev, width) + bias)
    centered = states - jnp.mean(states, -1, keepdims=True)
    inverse_spread = lax.rsqrt(jnp.mean(centered * centered, -1, keepdims=True) + 1e-05)
    normed = centered * inverse_spread
    e = e_sum[...].reshape(tok_dev, width)
    dx = inverse_spread * (e - jnp.mean(e, -1, keepdims=True) - normed * jnp.mean(e * normed, -1, keepdims=True))
    input_grad[...] = restored(jnp.dot(pick, g_in[...], preferred_element_type=F32) + dx)
    for copy in saves:
        copy.wait()


def close(tokens, inputs, cotangent, out_sum, e_sum, note, notes, scales, qkv, expand, own_a, own_b):
    rows, hidden_all = expand.shape
    width = inputs.shape[1]
    devices = tokens.shape[0]

    def shape(*dims):
        return jax.ShapeDtypeStruct(dims, F32)

    low = jax.ShapeDtypeStruct(inputs.shape, BF)
    sources = (inputs, cotangent, out_sum, e_sum, qkv, expand, own_a, own_b)
    outs = (
        low, low, shape(1, rows), shape(1, rows), shape(1, rows), shape(1, rows), shape(rows, 3 * width),
        shape(1, 2 * width // devices), shape(1, rows), shape(rows, width), shape(1, rows), shape(rows, hidden_all),
        shape(1, hidden_all // devices), shape(rows, hidden_all), shape(1, rows),
    )
    large = (6, 9, 11, 13)
    results = pl.pallas_call(
        close_kernel,
        out_shape=outs,
        in_specs=[VMEM] * 7 + [ANY] * len(sources),
        out_specs=tuple(ANY if k in large else VMEM for k in range(len(outs))),
        scratch_shapes=[pltpu.VMEM(one.shape, one.dtype) for one in sources]
        + [pltpu.VMEM(outs[k].shape, F32) for k in large]
        + [DMA((len(sources),)), DMA((4,))],
        compiler_params=pltpu.CompilerParams(vmem_limit_bytes=62 * 2**20),
    )(tokens, note, notes, *scales, *sources)
    return tuple(one[0] if one.shape[0] == 1 else one for one in results)


def pieces_of(i, prompt_runs):
    return list(range(min(i + 1, prompt_runs))) + ([i] if i >= prompt_runs else [])


def attention_forward(i, prompt_runs, mask, q_ref, key, value_of, s_ref):
    q = q_ref[i]
    peak, scores = None, []
    for at, k in enumerate(pieces_of(i, prompt_runs)):
        keys = key(k)
        s = lax.dot_general(q, keys, (((1,), (1,)), ((), ())), preferred_element_type=F32)
        keep = mask(i, k)
        if keep is not None:
            s = jnp.where(keep, s, -1e30)
        here = slice(at * keys.shape[0], (at + 1) * keys.shape[0])
        s_ref[:, here] = s
        top = jnp.max(s, -1, keepdims=True)
        peak = top if peak is None else jnp.maximum(peak, top)
        scores.append((k, here))
    total, out = 0.0, 0.0
    for k, here in scores:
        p = jnp.exp(s_ref[:, here] - peak)
        keep = mask(i, k)
        if keep is not None:
            p = jnp.where(keep, p, 0.0)
        total = total + jnp.sum(p, -1, keepdims=True)
        out = out + jnp.dot(p.astype(BF), value_of(k), preferred_element_type=F32)
    return out / total, peak + jnp.log(total)


def attention_backward(i, prompt_runs, mask, q_ref, do_ref, key, value_of, out, lse, turn_ref, sum_ref):
    by_rows = (((1,), (1,)), ((), ()))
    by_tokens = (((0,), (0,)), ((), ()))

    def dot(a, b, dims=(((1,), (0,)), ((), ()))):
        return lax.dot_general(a, b, dims, preferred_element_type=F32)

    q, do = q_ref[i], do_ref[i]
    delta = jnp.sum(out * do.astype(F32), -1, keepdims=True)
    dq = 0.0
    for k in pieces_of(i, prompt_runs):
        keys = key(k)
        p = jnp.exp(dot(q, keys, by_rows) - lse)
        keep = mask(i, k)
        if keep is not None:
            p = jnp.where(keep, p, 0.0)
        ds = (p * (dot(do, value_of(k), by_rows) - delta)).astype(BF)
        dq = dq + dot(ds, keys)
        dk = dot(ds, q, by_tokens)
        dv = dot(p.astype(BF), do, by_tokens)
        if i == k:
            sum_ref[k, :, :HEAD_DIM] = dk
            sum_ref[k, :, HEAD_DIM:] = dv
        else:
            sum_ref[k, :, :HEAD_DIM] = sum_ref[k, :, :HEAD_DIM] + dk
            sum_ref[k, :, HEAD_DIM:] = sum_ref[k, :, HEAD_DIM:] + dv
    dq = (dq * (1.0 / math.sqrt(HEAD_DIM))).astype(BF).astype(F32)
    return turn(dq, [turn_ref[t, i] for t in range(3)], -1.0)


def attention_kernel(prompt_runs, one_prompt, q_ref, do_ref, kv_ref, row_ref, col_ref, turn_ref,
                     o_ref, dq_ref, dkv_ref, s_ref, sum_ref):
    def mask(i, k):
        rows, cols = row_ref[i], col_ref[k]
        if i == k:
            return (rows[:, 1:2] == cols[1:2, :]) & (cols[0:1, :] <= rows[:, 0:1])
        if one_prompt:
            return None
        return rows[:, 2:3] == cols[2:3, :]

    def key(k):
        return kv_ref[k, :, :HEAD_DIM]

    def value_of(k):
        return kv_ref[k, :, HEAD_DIM:]

    for i in range(q_ref.shape[0]):
        out, lse = attention_forward(i, prompt_runs, mask, q_ref, key, value_of, s_ref)
        o_ref[i] = out.astype(BF)
        back = attention_backward(
            i, prompt_runs, mask, q_ref, do_ref, key, value_of, out, lse, turn_ref, sum_ref
        )
        dq_ref[i] = back.astype(BF)
    dkv_ref[...] = sum_ref[...].astype(BF)


def attention(prompt_runs, one_prompt, queries, d_out, pairs, row_meta, col_meta, tables):
    m = queries.shape[1]
    count = pairs.shape[1]
    return pl.pallas_call(
        functools.partial(attention_kernel, prompt_runs, one_prompt),
        out_shape=(
            jax.ShapeDtypeStruct(queries.shape, BF),
            jax.ShapeDtypeStruct(queries.shape, BF),
            jax.ShapeDtypeStruct(pairs.shape, BF),
        ),
        in_specs=[VMEM] * 6,
        out_specs=(VMEM,) * 3,
        scratch_shapes=[pltpu.VMEM((m, (prompt_runs + 1) * count), F32), pltpu.VMEM(pairs.shape, F32)],
        compiler_params=pltpu.CompilerParams(vmem_limit_bytes=60 * 2**20),
    )(queries, d_out, pairs, row_meta, col_meta, tables)


def rotate(values, cosine, sine):
    half = ROT // 2
    leading, behind = values[:, :half], values[:, half:ROT]
    return jnp.concatenate(
        [leading * cosine - behind * sine, behind * cosine + leading * sine, values[:, ROT:]], -1
    )


def per_device(
    inputs, attn_norm_gain, attn_norm_bias, mlp_norm_gain, mlp_norm_bias, qkv_weight, qkv_bias, dense_weight,
    dense_bias, expand_weight, expand_bias, shrink_weight, shrink_bias, token_of_row, cont_parent, position_ids,
    cotangent,
):
    heads, blocks = lax.axis_size("head"), lax.axis_size("blk")
    devices = heads * blocks
    ways = blocks // (2 * HEADS)
    assert heads == 2 and blocks == ways * 2 * HEADS
    x = lax.axis_index("head")
    b = lax.axis_index("blk")
    me = x * blocks + b
    c, h, w = b % 2, (b // 2) % HEADS, b // (2 * HEADS)
    tok_dev, width = inputs.shape
    rows = qkv_weight.shape[0]
    hidden = expand_weight.shape[1] // HEADS
    runs = tok_dev // STRIPE
    run_size = devices * STRIPE
    prompt_total = token_of_row.shape[0] - cont_parent.shape[0] * CONT
    prompt_runs = prompt_total // run_size
    one_prompt = prompt_total == PROMPT
    assert prompt_runs * run_size == prompt_total
    group_rows = runs * HEADS * STRIPE
    head3 = 3 * HEAD_DIM
    block_columns = head3 + hidden

    by_device = token_of_row.reshape(devices, tok_dev)
    mine = lax.dynamic_index_in_dim(by_device, me, 0, False)
    sorted_at = mine // run_size * STRIPE + mine % STRIPE
    pick = (sorted_at[None, :] == jnp.arange(tok_dev, dtype=jnp.int32)[:, None]).astype(BF)

    def ordered(rows_in):
        return jnp.dot(pick, rows_in, preferred_element_type=F32).astype(BF)

    def restored(rows_in):
        return lax.dot_general(pick, rows_in, (((0,), (0,)), ((), ())), preferred_element_type=F32).astype(BF)

    scales = (attn_norm_gain, attn_norm_bias, mlp_norm_gain, mlp_norm_bias)
    fuse, opened = open_all(
        ways, prompt_runs, prompt_total, inputs, cotangent, by_device, position_ids[None],
        scales, (qkv_bias, expand_bias, dense_bias, shrink_bias),
        qkv_weight, expand_weight, dense_weight, shrink_weight,
    )
    lanes = 128
    note_rows = block_columns // lanes
    slice_rows = width // lanes
    rows_run = group_rows // runs
    n_all, g_all, w_all, note, tables, sum_note = opened[:6]
    w_all = w_all.reshape(width, w_all.shape[-1])
    out_bias = note[note_rows : note_rows + slice_rows].reshape(width)
    gain_one, shift_one = attn_norm_gain.astype(F32), attn_norm_bias.astype(F32)
    gain_two, shift_two = mlp_norm_gain.astype(F32), mlp_norm_bias.astype(F32)
    qkv_wide, expand_wide = qkv_weight.astype(F32), expand_weight.astype(F32)
    states = ordered(inputs).astype(F32)
    grad_out = ordered(cotangent).astype(F32)
    average = jnp.mean(states, -1, keepdims=True)
    centered = states - average
    inverse_spread = lax.rsqrt(jnp.mean(centered * centered, -1, keepdims=True) + 1e-05)
    normed = centered * inverse_spread
    if fuse:
        left, right, half, part = opened[6:]
    else:
        n_all, g_all = n_all.reshape(group_rows, width), g_all.reshape(group_rows, width)
        bias_block = note[:note_rows].reshape(block_columns)
        run_of = by_device // run_size
        each_run = jnp.arange(runs, dtype=jnp.int32)
        base = jnp.min(jnp.where(run_of[:, :, None] == each_run, by_device[:, :, None], 2**30), 1)
        within = jnp.arange(STRIPE, dtype=jnp.int32)
        bases = base.reshape(2, ways, HEADS, 2, runs)
        own_base = lax.dynamic_index_in_dim(bases, x, 0, False)
        own_base = lax.dynamic_index_in_dim(own_base, w, 0, False)
        own_base = lax.dynamic_index_in_dim(own_base, c, 1, False)
        row_tokens = (own_base.T[:, :, None] + within).reshape(runs, rows_run)
        col_tokens = (bases.transpose(4, 1, 0, 3, 2)[..., None] + within).reshape(runs, run_size)
        flat = tables.reshape(3, group_rows, lanes)
        cosine, sine = flat[0, :, : ROT // 2], flat[2, :, ROT // 2 : ROT]
        w_in, w_out = w_all[:, :block_columns], w_all[:, block_columns:]
        mixed = jnp.dot(n_all, w_in[:, :head3], preferred_element_type=F32) + bias_block[:head3]
        queries = (rotate(mixed[:, :HEAD_DIM], cosine, sine) * (1.0 / math.sqrt(HEAD_DIM))).astype(BF)
        keys = rotate(mixed[:, HEAD_DIM : 2 * HEAD_DIM], cosine, sine).astype(BF)
        values = mixed[:, 2 * HEAD_DIM :].astype(BF)
        pairs = exchange(ways, jnp.concatenate([keys, values], 1).reshape(runs, rows_run, 2 * HEAD_DIM))
        pairs = pairs.reshape(runs, run_size, 2 * HEAD_DIM)
        d_attended = jnp.dot(g_all, w_out[:, :HEAD_DIM], preferred_element_type=F32).astype(BF)
        expanded = jnp.dot(n_all, w_in[:, head3:], preferred_element_type=F32) + bias_block[head3:]
        activated, gelu_back = jax.vjp(lambda v: jax.nn.gelu(v, approximate=False), expanded)
        activated = activated.astype(BF)
        d_activated = jnp.dot(g_all, w_out[:, HEAD_DIM:], preferred_element_type=F32)
        d_expanded = gelu_back(d_activated)[0].astype(BF)

        def meta(tokens):
            is_prompt = tokens < prompt_total
            cont = (tokens - prompt_total) // CONT
            matches = cont[..., None] == jnp.arange(cont_parent.shape[0], dtype=jnp.int32)
            prompt = jnp.where(is_prompt, tokens // PROMPT, jnp.sum(jnp.where(matches, cont_parent, 0), -1))
            segment = jnp.where(is_prompt, -1 - tokens // PROMPT, cont)
            return tokens, segment, prompt

        attended, d_queries, d_pairs = attention(
            prompt_runs, one_prompt,
            queries.reshape(runs, rows_run, HEAD_DIM), d_attended.reshape(runs, rows_run, HEAD_DIM),
            pairs, jnp.stack(meta(row_tokens), -1), jnp.stack(meta(col_tokens), 1), tables,
        )
        attended = attended.reshape(group_rows, HEAD_DIM)

        left = jnp.concatenate([attended, activated], 1)
        part = lax.dot_general(left, w_out, (((1,), (1,)), ((), ())), preferred_element_type=F32)
        part = part.reshape(runs, HEADS, STRIPE, width)
        others = [[w2 * 2 * HEADS + h2 * 2 + c2 for h2 in range(HEADS)] for w2 in range(ways) for c2 in range(2)]
        out_rows = lax.psum_scatter(part, "blk", scatter_dimension=1, axis_index_groups=others, tiled=True)[:, 0]
        half = part = None
        n_all, g_all = n_all.T, g_all.T
        d_pairs = d_pairs.astype(F32).reshape(runs, ways, 2, 2, rows_run, 2 * HEAD_DIM).transpose(1, 3, 2, 0, 4, 5)
        d_pairs = d_pairs.reshape(2 * ways, 2, runs, rows_run, 2 * HEAD_DIM)
        alike = [[w2 * 2 * HEADS + h2 * 2 + c2 for w2 in range(ways) for c2 in range(2)] for h2 in range(HEADS)]
        d_pairs = lax.psum_scatter(d_pairs, "blk", scatter_dimension=0, axis_index_groups=alike, tiled=True)[0]
        d_pairs = lax.psum_scatter(d_pairs, "head", scatter_dimension=0, tiled=True)
        d_pairs = d_pairs.reshape(group_rows, 2 * HEAD_DIM)
        d_keys = rotate(d_pairs[:, :HEAD_DIM].astype(BF).astype(F32), cosine, -sine).astype(BF)
        right = jnp.concatenate(
            [d_queries.reshape(group_rows, HEAD_DIM), d_keys, d_pairs[:, HEAD_DIM:].astype(BF), d_expanded], 1
        )

    out_sum, e_sum, owned_a, owned_b, owned_notes = finish(
        ways, rows, left, right, w_all, n_all, g_all, sum_note, half, part
    )
    if fuse:
        return close(
            by_device, inputs, cotangent, out_sum, e_sum, note, owned_notes, scales, qkv_weight, expand_weight, owned_a,
            owned_b,
        )
    out_sum = out_rows
    output = restored((states + out_sum.reshape(tok_dev, width) + out_bias).astype(BF))
    e_sum = e_sum.reshape(tok_dev, width)
    dx = inverse_spread * (
        e_sum - jnp.mean(e_sum, -1, keepdims=True) - normed * jnp.mean(e_sum * normed, -1, keepdims=True)
    )
    input_grad = restored((grad_out + dx).astype(BF))
    owned_a, owned_b = owned_a.astype(F32), owned_b.astype(F32)

    def join_qkv(values):
        return values.reshape(HEADS, -1, 3, HEAD_DIM).transpose(1, 2, 0, 3).reshape(-1, 3 * width)

    def join(values):
        return values.transpose(1, 0, 2).reshape(values.shape[1], -1)

    raw_qkv = join_qkv(owned_b)
    dense_grad = join(owned_a[..., :HEAD_DIM])
    shrink_grad = join(owned_a[..., HEAD_DIM : HEAD_DIM + hidden])
    raw_expand = join(owned_a[..., HEAD_DIM + hidden :])
    column_sums = owned_notes[:, :note_rows].reshape(HEADS, 1, block_columns)
    qkv_sum = join_qkv(column_sums[..., :head3])
    expand_sum = join(column_sums[..., head3:])
    all_sums = jnp.sum(owned_notes[:, note_rows : note_rows + width // lanes], 0).reshape(width)
    bias_grad = lax.dynamic_slice_in_dim(all_sums, me * rows, rows, 0)
    qkv_grad = gain_one[:, None] * raw_qkv + shift_one[:, None] * qkv_sum
    expand_grad = gain_two[:, None] * raw_expand + shift_two[:, None] * expand_sum

    def own(values, count):
        return lax.dynamic_slice_in_dim(values, me * count, count, 0)

    return (
        output,
        input_grad,
        jnp.sum(qkv_wide * raw_qkv, 1),
        jnp.sum(qkv_wide * qkv_sum, 1),
        jnp.sum(expand_wide * raw_expand, 1),
        jnp.sum(expand_wide * expand_sum, 1),
        qkv_grad,
        own(qkv_sum[0, : 2 * width], 2 * width // devices),
        own(qkv_sum[0, 2 * width :], width // devices),
        dense_grad,
        bias_grad,
        expand_grad,
        own(expand_sum[0], HEADS * hidden // devices),
        shrink_grad,
        bias_grad,
    )


def solution(mesh):
    matrix, vector = P(("head", "blk"), None), P(("head", "blk"))
    return jax.shard_map(
        per_device,
        mesh=mesh,
        in_specs=(
            matrix, vector, vector, vector, vector, matrix, vector, matrix, vector, matrix, vector, matrix, vector,
            P(), P(), vector, matrix,
        ),
        out_specs=(
            matrix, matrix, vector, vector, vector, vector, matrix, vector, vector, matrix, vector, matrix, vector,
            matrix, vector,
        ),
        check_vma=False,
    )
```
